32 devices in a mesh: fsdp: 4 (over x, core), ctx: 8 (over z, y).
Axes of the slice: x: 2, y: 2, z: 4, core: 2. Of those that a mesh axis runs over, the one named last changes fastest.
Arguments:
- tokens: bfloat16 [4, 1024, 1600], P('fsdp', 'ctx'), may hold values from -6 to 6
- cotangent: bfloat16 [4, 1024, 1600], P('fsdp', 'ctx'), may hold values from -6 to 6
- segments: int32 [4, 1024], P('fsdp'), may hold values from 0 to 3, never falling along the last dimension, each value on 1 to 512 neighbouring positions
- w_qkv: bfloat16 [1600, 2240], P('fsdp'), may hold values from -0.15625 to 0.15625
- m_qkv: float32 [2, 1600, 2240], P(None, 'ctx', 'fsdp'), may hold values from -12.8 to 40.96, as said below
- w_attn_out: bfloat16 [1600, 1600], P('fsdp'), may hold values from -0.15625 to 0.15625
- m_attn_out: float32 [2, 1600, 1600], P(None, 'ctx', 'fsdp'), may hold values from -12.8 to 40.96, as said below
- w_mamba_in: bfloat16 [1600, 6400], P('fsdp'), may hold values from -0.15625 to 0.15625
- m_mamba_in: float32 [2, 1600, 6400], P(None, 'ctx', 'fsdp'), may hold values from -12.8 to 40.96, as said below
- w_ssm_proj: bfloat16 [3200, 232], P('fsdp'), may hold values from -0.6 to 0.6
- m_ssm_proj: float32 [2, 3200, 232], P(None, 'ctx', 'fsdp'), may hold values from -12.8 to 40.96, as said below
- w_mamba_out: bfloat16 [3200, 1600], P('fsdp'), may hold values from -0.109375 to 0.109375
- m_mamba_out: float32 [2, 3200, 1600], P(None, 'ctx', 'fsdp'), may hold values from -12.8 to 40.96, as said below
- w_gate_up: bfloat16 [1600, 11008], P('fsdp'), may hold values from -0.15625 to 0.15625
- m_gate_up: float32 [2, 1600, 11008], P(None, 'ctx', 'fsdp'), may hold values from -12.8 to 40.96, as said below
- w_ffn_down: bfloat16 [5504, 1600], P('fsdp'), may hold values from -0.078125 to 0.078125
- m_ffn_down: float32 [2, 5504, 1600], P(None, 'ctx', 'fsdp'), may hold values from -12.8 to 40.96, as said below
- ssm_vec: float32 [22, 3200], replicated, may hold values from -10 to 3
- m_ssm_vec: float32 [2, 22, 3200], replicated, may hold values from -12.8 to 40.96, as said below
- embed_small: float32 [132, 1600], replicated, may hold values from -6 to 6
- m_embed_small: float32 [2, 132, 1600], replicated, may hold values from -12.8 to 40.96, as said below
Outputs:
- output: bfloat16 [4, 1024, 1600], P('fsdp', 'ctx')
- tokens_grad: float32 [4, 1024, 1600], P('fsdp', 'ctx')
- grad_qkv: float32 [1600, 2240], P('ctx', 'fsdp')
- moments_qkv: float32 [1600, 2240], P('ctx', 'fsdp')
- update_qkv: float32 [1600, 2240], P('ctx', 'fsdp')
- grad_attn_out: float32 [1600, 1600], P('ctx', 'fsdp')
- moments_attn_out: float32 [1600, 1600], P('ctx', 'fsdp')
- update_attn_out: float32 [1600, 1600], P('ctx', 'fsdp')
- grad_mamba_in: float32 [1600, 6400], P('ctx', 'fsdp')
- moments_mamba_in: float32 [1600, 6400], P('ctx', 'fsdp')
- update_mamba_in: float32 [1600, 6400], P('ctx', 'fsdp')
- grad_ssm_proj: float32 [3200, 232], P('ctx', 'fsdp')
- moments_ssm_proj: float32 [3200, 232], P('ctx', 'fsdp')
- update_ssm_proj: float32 [3200, 232], P('ctx', 'fsdp')
- grad_mamba_out: float32 [3200, 1600], P('ctx', 'fsdp')
- moments_mamba_out: float32 [3200, 1600], P('ctx', 'fsdp')
- update_mamba_out: float32 [3200, 1600], P('ctx', 'fsdp')
- grad_gate_up: float32 [1600, 11008], P('ctx', 'fsdp')
- moments_gate_up: float32 [1600, 11008], P('ctx', 'fsdp')
- update_gate_up: float32 [1600, 11008], P('ctx', 'fsdp')
- grad_ffn_down: float32 [5504, 1600], P('ctx', 'fsdp')
- moments_ffn_down: float32 [5504, 1600], P('ctx', 'fsdp')
- update_ffn_down: float32 [5504, 1600], P('ctx', 'fsdp')
- grad_ssm_vec: float32 [22, 3200], replicated
- moments_ssm_vec: float32 [22, 3200], replicated
- update_ssm_vec: float32 [22, 3200], replicated
- grad_embed_small: float32 [132, 1600], replicated
- moments_embed_small: float32 [132, 1600], replicated
- update_embed_small: float32 [132, 1600], replicated
The draws below stay inside these ranges and needn't reach their ends.
Inputs may be any that keep to these rules, and one draw needn't show every extreme that they name: `m_qkv`: row 0 holds first moments, row 1 positive second moments. `segments`: along a row the segment numbers never fall, and the longest segment has exactly 512 tokens. `m_attn_out`: row 0 holds first moments, row 1 positive second moments. `m_mamba_in`: row 0 holds first moments, row 1 positive second moments. `m_ssm_proj`: row 0 holds first moments, row 1 positive second moments. `m_mamba_out`: row 0 holds first moments, row 1 positive second moments. `m_gate_up`: row 0 holds first moments, row 1 positive second moments. `m_ffn_down`: row 0 holds first moments, row 1 positive second moments. `m_ssm_vec`: row 0 holds first moments, row 1 positive second moments. `m_embed_small`: row 0 holds first moments, row 1 positive second moments.
All inputs are finite; a program needn't handle non-finite values.
Results may differ from the reference program's by a relative error of at most 0.025.
Values may be sent and summed in bfloat16 or wider, within the bound.
A program may use at most 512 MiB of HBM per device.

```python
import math
import jax
import jax.numpy as jnp
import numpy as np
from jax import lax

D = 1600
NH = 25
KVH = 5
HD = 64
DI = 3200
DS = 16
DTR = 100
FF = 5504
META = 128
CONV = 4
WINDOW = 1024
QKV = 2240
PROJ = 232
SV = 22
ROW = 1024
BATCH = 4
TOKENS = 4096


def moment_pair(key, salt, rows_count, cols_count):
    own_key = jax.random.fold_in(key, salt)
    scale_base = 0.3 * math.sqrt(TOKENS)
    first_moment = jnp.clip(jax.random.normal(jax.random.fold_in(own_key, 11), (rows_count, cols_count), jnp.float32), -6.0, 6.0) * (0.11 * scale_base)
    second_moment = jnp.exp(jax.random.uniform(jax.random.fold_in(own_key, 12), (rows_count, cols_count), jnp.float32, -0.7, 0.7)) * (0.05 * scale_base * scale_base)
    return jnp.stack([first_moment, second_moment])


def draw_m_qkv(key, part):
    return moment_pair(key, 101, D, QKV)


def draw_m_attn_out(key, part):
    return moment_pair(key, 102, D, D)


def draw_m_mamba_in(key, part):
    return moment_pair(key, 103, D, 2 * DI)


def draw_m_ssm_proj(key, part):
    return moment_pair(key, 104, DI, PROJ)


def draw_m_mamba_out(key, part):
    return moment_pair(key, 105, DI, D)


def draw_m_gate_up(key, part):
    return moment_pair(key, 106, D, 2 * FF)


def draw_m_ffn_down(key, part):
    return moment_pair(key, 107, FF, D)


def draw_m_ssm_vec(key, part):
    return moment_pair(key, 108, SV, DI)


def draw_m_embed_small(key, part):
    return moment_pair(key, 109, META + 4, D)


def draw_w_ssm_proj(key, part):
    values = jnp.clip(jax.random.normal(jax.random.fold_in(key, 21), (DI, PROJ), jnp.float32), -6.0, 6.0)
    column = jnp.arange(PROJ)
    scales = jnp.where(column < DTR + 2 * DS, DI ** (-0.5), DTR ** (-0.5))
    return (values * scales[None, :]).astype(jnp.bfloat16)


def draw_ssm_vec(key, part):
    conv_taps = jnp.clip(jax.random.normal(jax.random.fold_in(key, 31), (CONV, DI), jnp.float32), -3.0, 3.0) * 0.5
    step_bias = jax.random.uniform(jax.random.fold_in(key, 32), (1, DI), jnp.float32, -10.0, -3.0)
    skip_gain = jax.random.uniform(jax.random.fold_in(key, 33), (1, DI), jnp.float32, 0.5, 1.5)
    log_rates = jax.random.uniform(jax.random.fold_in(key, 34), (DS, DI), jnp.float32, 0.0, math.log(16.0))
    return jnp.concatenate([conv_taps, step_bias, skip_gain, log_rates], axis=0)


def draw_embed_small(key, part):
    meta_rows = jnp.clip(jax.random.normal(jax.random.fold_in(key, 41), (META, D), jnp.float32), -6.0, 6.0)
    gain_rows = 1.0 + 0.1 * jnp.clip(jax.random.normal(jax.random.fold_in(key, 42), (4, D), jnp.float32), -5.0, 5.0)
    return jnp.concatenate([meta_rows, gain_rows], axis=0)


def level_of(key, shape, split, least, largest):
    loudness = 1.0
    for position, shards_of in split:
        steps = jax.random.uniform(jax.random.fold_in(jax.random.fold_in(key, 6), position), (shards_of,), jnp.float32, least / len(split), largest / len(split))
        loudness = loudness * jnp.repeat(jnp.exp(steps), shape[position] // shards_of).reshape((-1,) + (1,) * (len(shape) - 1 - position))
    return loudness


def split_up(number_of, total, reach, lean):
    loads = [(1 << 20) // math.isqrt(standing ** lean) + 1 for standing in range(2, number_of + 1)]
    surplus, given = total - reach - (number_of - 1), [1] * (number_of - 1)
    while surplus > 0:
        movable = [i for i in range(number_of - 1) if given[i] < reach]
        mass, left = sum([loads[i] for i in movable]), surplus
        for i in movable:
            extra = min(reach - given[i], max(1, left * loads[i] // mass), surplus)
            given[i] = given[i] + extra
            surplus = surplus - extra
    return np.array([reach] + given)


def uneven_parts(key, amount, total, bound, skew):
    if amount == 2:
        one = jax.random.randint(key, (), max(1, total - bound), min(bound, total - 1) + 1)
        return jnp.stack([one, total - one])
    sizes = jnp.asarray(split_up(amount, total, bound, skew), jnp.int32)
    twos = (amount - 1) // 2
    source_of, taker = sizes[1:1 + 2 * twos:2], sizes[2:2 + 2 * twos:2]
    margin = jnp.minimum(source_of - 1, bound - taker)
    moved = jax.random.randint(jax.random.fold_in(key, 1), (twos,), 0, 1 << 20) % (margin + 1)
    sizes = sizes.at[1:1 + 2 * twos:2].set(source_of - moved).at[2:2 + 2 * twos:2].set(taker + moved)
    return sizes[jax.random.permutation(jax.random.fold_in(key, 2), amount)]


def normal_values(key, shape, width, reach, cuts=(), kind=jnp.bfloat16):
    result = width * jax.random.normal(key, shape, jnp.float32)
    if cuts:
        result = result * level_of(key, shape, cuts, -0.22, 0.18)
    return jnp.clip(result, -reach, reach).astype(kind)


def setup_inputs(seed: int = 0) -> dict:
    splits = jax.random.split(jax.random.key(seed), 22)
    tokens = normal_values(splits[0], (BATCH, ROW, D), 1.0, 6.0, ((0, 4), (1, 8)))
    cotangent = normal_values(splits[1], (BATCH, ROW, D), 1.0, 6.0, ((0, 4), (1, 8)))
    segments = jax.vmap(lambda own: jnp.searchsorted(jnp.cumsum(uneven_parts(own, 4, ROW, ROW // 2, 2)), jnp.arange(ROW), side="right"))(jax.random.split(splits[2], BATCH)).reshape((BATCH, ROW)).astype(jnp.int32)
    w_qkv = normal_values(splits[3], (D, QKV), D ** -0.5, 0.15625, ((0, 4),))
    m_qkv = draw_m_qkv(jax.random.fold_in(splits[21], 71), 0)
    w_attn_out = normal_values(splits[5], (D, D), D ** -0.5, 0.15625, ((0, 4),))
    m_attn_out = draw_m_attn_out(jax.random.fold_in(splits[21], 71), 0)
    w_mamba_in = normal_values(splits[7], (D, 2 * DI), D ** -0.5, 0.15625, ((0, 4),))
    m_mamba_in = draw_m_mamba_in(jax.random.fold_in(splits[21], 71), 0)
    w_ssm_proj = draw_w_ssm_proj(jax.random.fold_in(splits[21], 71), 0)
    m_ssm_proj = draw_m_ssm_proj(jax.random.fold_in(splits[21], 71), 0)
    w_mamba_out = normal_values(splits[11], (DI, D), DI ** -0.5, 0.109375, ((0, 4),))
    m_mamba_out = draw_m_mamba_out(jax.random.fold_in(splits[21], 71), 0)
    w_gate_up = normal_values(splits[13], (D, 2 * FF), D ** -0.5, 0.15625, ((0, 4),))
    m_gate_up = draw_m_gate_up(jax.random.fold_in(splits[21], 71), 0)
    w_ffn_down = normal_values(splits[15], (FF, D), FF ** -0.5, 0.078125, ((0, 4),))
    m_ffn_down = draw_m_ffn_down(jax.random.fold_in(splits[21], 71), 0)
    ssm_vec = draw_ssm_vec(jax.random.fold_in(splits[21], 71), 0)
    m_ssm_vec = draw_m_ssm_vec(jax.random.fold_in(splits[21], 71), 0)
    embed_small = draw_embed_small(jax.random.fold_in(splits[21], 71), 0)
    m_embed_small = draw_m_embed_small(jax.random.fold_in(splits[21], 71), 0)
    return dict(tokens=tokens, cotangent=cotangent, segments=segments, w_qkv=w_qkv, m_qkv=m_qkv, w_attn_out=w_attn_out, m_attn_out=m_attn_out, w_mamba_in=w_mamba_in, m_mamba_in=m_mamba_in, w_ssm_proj=w_ssm_proj, m_ssm_proj=m_ssm_proj, w_mamba_out=w_mamba_out, m_mamba_out=m_mamba_out, w_gate_up=w_gate_up, m_gate_up=m_gate_up, w_ffn_down=w_ffn_down, m_ffn_down=m_ffn_down, ssm_vec=ssm_vec, m_ssm_vec=m_ssm_vec, embed_small=embed_small, m_embed_small=m_embed_small)


norm_eps = 1e-05
beta_one = 0.9
beta_two = 0.95
learn_rate = 0.01
decay_rate = 0.1
adam_eps = 1e-08
adam_count = 10.0
highest = lax.Precision.HIGHEST

@jax.custom_vjp
def low(v):
    return lax.optimization_barrier(v.astype(jnp.bfloat16)).astype(jnp.float32)

@jax.custom_vjp
def low_back(v):
    return v

def low_keep(v):
    return (low(v), None)

def low_pass(kept, grad):
    return (grad,)

def back_keep(v):
    return (v, None)

def back_low(kept, grad):
    return (low(grad),)
low.defvjp(low_keep, low_pass)
low_back.defvjp(back_keep, back_low)

def rms_norm(values, gain_row):
    return values * lax.rsqrt(lax.optimization_barrier(jnp.mean(values * values, axis=-1, keepdims=True)) + norm_eps) * gain_row

def matmul(operand, partner):
    return jnp.dot(operand, partner, precision=highest, preferred_element_type=jnp.float32)

def matmul_nt(operand, partner):
    return lax.dot_general(operand, partner, (((1,), (1,)), ((), ())), precision=highest, preferred_element_type=jnp.float32)

def conv_silu(extended, conv_taps, seg_ext):
    length_out = extended.shape[0] - conv_taps.shape[0] + 1
    own_seg = seg_ext[conv_taps.shape[0] - 1:]
    summed = jnp.zeros((length_out, extended.shape[1]), jnp.float32)
    for offset in range(conv_taps.shape[0]):
        same_seg = (seg_ext[offset:offset + length_out] == own_seg)[:, None]
        summed = summed + jnp.where(same_seg, extended[offset:offset + length_out] * conv_taps[offset], 0.0)
    return jax.nn.silu(summed)

def ssm_scan(inner_x, pre_delta, proj_b, proj_c, gate_z, ssm_small, starts, start_state):
    step_size = jax.nn.softplus(pre_delta + ssm_small[0])
    decay_rates = -jnp.exp(ssm_small[2:])

    def advance(running, element):
        step_delta, step_inner, step_b, step_c, step_start = element
        retain = jnp.where(step_start, 0.0, jnp.exp(step_delta[None, :] * decay_rates))
        running = retain * running + (step_delta * step_inner)[None, :] * step_b[:, None]
        return (running, lax.optimization_barrier(jnp.sum(running * step_c[:, None], axis=0)))
    last_state, readout = lax.scan(advance, start_state, (step_size, inner_x, proj_b, proj_c, starts))
    chain_decay = jnp.where(jnp.any(starts), 0.0, jnp.exp(decay_rates * lax.optimization_barrier(jnp.sum(step_size, axis=0))[None, :]))
    mixture = (readout + ssm_small[1] * inner_x) * jax.nn.silu(gate_z)
    return (mixture, last_state, chain_decay)

def ssm_row(inner_x, pre_delta, proj_b, proj_c, gate_z, ssm_small, starts):
    rows_total = inner_x.shape[0]
    block_rows = min(256, rows_total)
    count_blocks = rows_total // block_rows

    def to_blocks(values):
        return values.reshape((count_blocks, block_rows) + values.shape[1:])

    def advance_block(running, pieces):
        mixture, last_state, chain_decay = ssm_scan(pieces[0], pieces[1], pieces[2], pieces[3], pieces[4], ssm_small, pieces[5], running)
        return (last_state, mixture)
    blocks = (to_blocks(inner_x), to_blocks(pre_delta), to_blocks(proj_b), to_blocks(proj_c), to_blocks(gate_z), to_blocks(starts))
    _, mixtures = lax.scan(jax.checkpoint(advance_block), jnp.zeros((DS, DI), jnp.float32), blocks)
    return mixtures.reshape(rows_total, DI)

def attend_row(queries, keyval, meta_kv, seg_row):
    rows_total = queries.shape[0]
    block_rows = min(512, rows_total)
    groups = NH // KVH
    scale_factor = HD ** (-0.5)
    padded_kv = jnp.concatenate([jnp.zeros((WINDOW, keyval.shape[1]), jnp.float32), keyval], axis=0)
    padded_seg = jnp.concatenate([jnp.full((WINDOW,), -1, jnp.int32), seg_row], axis=0)

    def one_block(block_index):
        first_row = block_index * block_rows
        block_q = lax.dynamic_slice_in_dim(queries, first_row, block_rows, 0).reshape(block_rows, KVH, groups, HD)
        block_kv = lax.dynamic_slice_in_dim(padded_kv, first_row, block_rows + WINDOW, 0)
        key_seg = lax.dynamic_slice_in_dim(padded_seg, first_row, block_rows + WINDOW, 0)
        query_seg = lax.dynamic_slice_in_dim(seg_row, first_row, block_rows, 0)
        query_pos = first_row + jnp.arange(block_rows, dtype=jnp.int32)
        key_pos = first_row - WINDOW + jnp.arange(block_rows + WINDOW, dtype=jnp.int32)
        allowed = (key_seg[None, :] == query_seg[:, None]) & (key_pos[None, :] <= query_pos[:, None]) & (query_pos[:, None] - key_pos[None, :] < WINDOW)
        allowed = jnp.concatenate([jnp.ones((block_rows, META), jnp.bool_), allowed], axis=1)
        key_rows = jnp.concatenate([meta_kv, block_kv], axis=0)
        key_part = key_rows[:, :KVH * HD].reshape(-1, KVH, HD)
        value_part = key_rows[:, KVH * HD:].reshape(-1, KVH, HD)
        scores = low_back(jnp.einsum('qkgd,lkd->kgql', block_q, key_part, precision=highest) * scale_factor)
        scores = jnp.where(allowed[None, None], scores, -1e+30)
        attention = low(jax.nn.softmax(scores, axis=-1))
        mixture = jnp.einsum('kgql,lkd->qkgd', attention, value_part, precision=highest)
        return mixture.reshape(block_rows, NH * HD)
    outputs = lax.map(jax.checkpoint(one_block), jnp.arange(rows_total // block_rows, dtype=jnp.int32))
    return outputs.reshape(rows_total, NH * HD)

def row_layer(source_row, seg_row, weights):
    w_qkv, w_attn_out, w_mamba_in, w_ssm_proj, w_mamba_out, w_gate_up, w_ffn_down, ssm_vec, embed_small = weights
    meta_rows = embed_small[:META]
    gain_rows = embed_small[META:]
    xproj_dim = DTR + 2 * DS
    normed = low(rms_norm(source_row, gain_rows[0]))
    meta_low = low(rms_norm(meta_rows, gain_rows[0]))
    qkv_out = low(low_back(matmul(normed, w_qkv)))
    meta_kv = low(low_back(matmul(meta_low, w_qkv[:, NH * HD:])))
    attended = low(low_back(attend_row(qkv_out[:, :NH * HD], qkv_out[:, NH * HD:], meta_kv, seg_row)))
    attn_proj = low_back(matmul(attended, w_attn_out))
    attn_branch = rms_norm(attn_proj, gain_rows[1])
    mamba_in = low_back(matmul(normed, w_mamba_in))
    seg_ext = jnp.concatenate([jnp.full((CONV - 1,), -1, jnp.int32), seg_row])
    extended = jnp.concatenate([jnp.zeros((CONV - 1, DI), jnp.float32), mamba_in[:, :DI]], axis=0)
    inner_x = conv_silu(extended, ssm_vec[:CONV], seg_ext)
    inner_low = low(inner_x)
    xproj_out = low_back(matmul(inner_low, w_ssm_proj[:, :xproj_dim]))
    delta_low = low(xproj_out[:, :DTR])
    pre_delta = low_back(matmul_nt(delta_low, w_ssm_proj[:, xproj_dim:]))
    starts = seg_ext[CONV - 1:] != seg_ext[CONV - 2:-1]
    mixture = ssm_row(inner_x, pre_delta, xproj_out[:, DTR:DTR + DS], xproj_out[:, DTR + DS:], mamba_in[:, DI:], ssm_vec[CONV:], starts)
    ssm_proj = low_back(matmul(low(mixture), w_mamba_out))
    ssm_branch = rms_norm(ssm_proj, gain_rows[2])
    residual = source_row + 0.5 * (attn_branch + ssm_branch)
    ffn_in = low(rms_norm(residual, gain_rows[3]))
    gate_up = low_back(matmul(ffn_in, w_gate_up))
    hidden = low(jax.nn.silu(gate_up[:, :FF]) * gate_up[:, FF:])
    return residual + low_back(matmul(hidden, w_ffn_down))

def adam_step(gradient, moments_old, weight_now):
    first_moment = beta_one * moments_old[0] + (1.0 - beta_one) * gradient
    second_moment = beta_two * moments_old[1] + (1.0 - beta_two) * gradient * gradient
    corrected = first_moment / (1.0 - beta_one ** adam_count) / (jnp.sqrt(second_moment / (1.0 - beta_two ** adam_count)) + adam_eps)
    return (second_moment, -learn_rate * (corrected + decay_rate * weight_now))

def reference(tokens, cotangent, segments, w_qkv, m_qkv, w_attn_out, m_attn_out, w_mamba_in, m_mamba_in, w_ssm_proj, m_ssm_proj, w_mamba_out, m_mamba_out, w_gate_up, m_gate_up, w_ffn_down, m_ffn_down, ssm_vec, m_ssm_vec, embed_small, m_embed_small):
    weights = [weight_item.astype(jnp.float32) for weight_item in (w_qkv, w_attn_out, w_mamba_in, w_ssm_proj, w_mamba_out, w_gate_up, w_ffn_down, ssm_vec, embed_small)]
    moments = [m_qkv, m_attn_out, m_mamba_in, m_ssm_proj, m_mamba_out, m_gate_up, m_ffn_down, m_ssm_vec, m_embed_small]

    def forward(source, params):

        def per_row(running, items):
            return (running, row_layer(items[0], items[1], params))
        _, outputs = lax.scan(jax.checkpoint(per_row), jnp.zeros((), jnp.float32), (source, segments))
        return outputs
    outputs, pull_back = jax.vjp(forward, tokens.astype(jnp.float32), weights)
    source_grad, weight_grads = pull_back(cotangent.astype(jnp.float32))
    results = [outputs.astype(jnp.bfloat16), source_grad]
    for weight_item, gradient, moments_old in zip(weights, weight_grads, moments):
        new_second, update = adam_step(gradient, moments_old, weight_item)
        results = results + [gradient, new_second, update]
    return (results[0], results[1], results[2], results[3], results[4], results[5], results[6], results[7], results[8], results[9], results[10], results[11], results[12], results[13], results[14], results[15], results[16], results[17], results[18], results[19], results[20], results[21], results[22], results[23], results[24], results[25], results[26], results[27], results[28])
```

```python
import functools

import jax
import jax.numpy as jnp
from jax import lax
from jax.experimental import pallas as pl
from jax.experimental.pallas import tpu as pltpu
from jax.sharding import PartitionSpec as P

NH = 25
KVH = 5
HD = 64
DI = 3200
DS = 16
DTR = 100
FF = 5504
META = 128
CONV = 4
WINDOW = 1024

norm_eps = 1e-05
beta_one = 0.9
beta_two = 0.95
learn_rate = 0.01
decay_rate = 0.1
adam_eps = 1e-08
adam_count = 10.0

LOG2E = 1.4426950408889634
LN2 = 0.6931471805599453
FAR = 1e30
bf16 = jnp.bfloat16
f32 = jnp.float32
ANY = pl.BlockSpec(memory_space=pl.ANY)
MIB = 1024 * 1024


def ceil_to(value, unit):
    return (value + unit - 1) // unit * unit


def exchange_body(axis, n, reach, modes, *refs):
    count = len(modes)
    ins, outs = refs[:count], refs[count : 2 * count]
    send_sem, recv_sem, own_sem = refs[2 * count :]
    me = lax.axis_index(axis)
    barrier = pltpu.get_barrier_semaphore()
    for d in range(1, n):
        pl.semaphore_signal(
            barrier,
            inc=1,
            device_id={axis: lax.rem(me + d, n)},
            device_id_type=pl.DeviceIdType.MESH,
        )
    pl.semaphore_wait(barrier, n - 1)

    def copy(k, d, source, target, peer):
        return pltpu.make_async_remote_copy(
            src_ref=source,
            dst_ref=target,
            send_sem=send_sem.at[k, d],
            recv_sem=recv_sem.at[k, d],
            device_id={axis: peer},
            device_id_type=pl.DeviceIdType.MESH,
        )

    waits = []
    for k, mode in enumerate(modes):
        src, dst = ins[k], outs[k]
        if mode in ("all", "each"):
            own = pltpu.make_async_copy(
                src.at[me] if mode == "each" else src, dst.at[me], own_sem.at[k]
            )
            own.start()
            waits.append((own.wait, None))
            for d in range(1, n):
                peer = lax.rem(me + d, n)
                c = copy(k, d, src.at[peer] if mode == "each" else src, dst.at[me], peer)
                c.start()
                waits.append((c.wait_send, None))
                waits.append((c.wait_recv, None))
        else:
            for d in range(1, reach + 1):
                up = mode == "next"
                peer = me + d if up else me - d
                sends = peer < n if up else peer >= 0
                takes = me - d >= 0 if up else me + d < n
                source = src.at[d - 1] if mode == "back" else src
                c = copy(k, d, source, dst.at[d - 1], lax.rem(peer + n, n))
                pl.when(sends)(c.start)
                waits.append((c.wait_send, sends))
                waits.append((c.wait_recv, takes))
    for wait, condition in waits:
        if condition is None:
            wait()
        else:
            pl.when(condition)(wait)


def exchange(axis, cid, items, reach=0):
    n = lax.axis_size(axis)
    shapes, modes = [], []
    for value, mode in items:
        lead = {"all": (n,), "next": (reach,), "prev": (reach,)}.get(mode, ())
        shapes.append(jax.ShapeDtypeStruct(lead + value.shape, value.dtype))
        modes.append(mode)
    count = len(items)
    return pl.pallas_call(
        functools.partial(exchange_body, axis, n, reach, tuple(modes)),
        out_shape=tuple(shapes),
        in_specs=[ANY] * count,
        out_specs=(ANY,) * count,
        scratch_shapes=[
            pltpu.SemaphoreType.DMA((count, n)),
            pltpu.SemaphoreType.DMA((count, n)),
            pltpu.SemaphoreType.DMA((count,)),
        ],
        compiler_params=pltpu.CompilerParams(collective_id=cid, has_side_effects=True),
    )(*[value for value, _ in items])


def scan_tail_body(rows, length, step_ref, u_ref, b_ref, rate_ref, last_ref):
    rate = rate_ref[...]

    def advance(i, states):
        new = []
        for r in range(rows):
            keep = jnp.exp2(step_ref[r, pl.ds(i, 1), :] * rate)
            new.append(keep * states[r] + u_ref[r, pl.ds(i, 1), :] * b_ref[r, i])
        return tuple(new)

    start = tuple(jnp.zeros((DS, 128), f32) for _ in range(rows))
    end = lax.fori_loop(0, length, advance, start, unroll=4)
    for r in range(rows):
        last_ref[r] = end[r]


def scan_full_body(
    rows, length, step_ref, u_ref, b_ref, c_ref, rate_ref, entry_ref, read_ref, hist_ref
):
    rate = rate_ref[...]

    def advance(i, states):
        new = []
        for r in range(rows):
            hist_ref[r, i] = states[r]
            keep = jnp.exp2(step_ref[r, pl.ds(i, 1), :] * rate)
            h = keep * states[r] + u_ref[r, pl.ds(i, 1), :] * b_ref[r, i]
            read_ref[r, pl.ds(i, 1), :] = jnp.sum(h * c_ref[r, i], axis=0, keepdims=True)
            new.append(h)
        return tuple(new)

    lax.fori_loop(0, length, advance, tuple(entry_ref[r] for r in range(rows)), unroll=4)


def adjoint_head_body(rows, length, step_ref, dy_ref, c_ref, rate_ref, first_ref):
    rate = rate_ref[...]

    def advance(k, carried):
        i = length - 1 - k
        new = []
        for r in range(rows):
            keep = jnp.exp2(step_ref[r, pl.ds(i, 1), :] * rate)
            new.append(keep * (carried[r] + dy_ref[r, pl.ds(i, 1), :] * c_ref[r, i]))
        return tuple(new)

    start = tuple(jnp.zeros((DS, 128), f32) for _ in range(rows))
    end = lax.fori_loop(0, length, advance, start, unroll=4)
    for r in range(rows):
        first_ref[r] = end[r]


def adjoint_full_body(
    rows,
    length,
    step_ref,
    u_ref,
    dy_ref,
    b_ref,
    c_ref,
    rate_ref,
    hist_ref,
    later_ref,
    du_ref,
    dexp_ref,
    db_ref,
    dc_ref,
    drate_ref,
):
    rate = rate_ref[...]

    @pl.when(pl.program_id(1) == 0)
    def _():
        db_ref[...] = jnp.zeros_like(db_ref)
        dc_ref[...] = jnp.zeros_like(dc_ref)

    def advance(k, carried):
        i = length - 1 - k
        new = []
        drate = carried[rows]
        for r in range(rows):
            step = step_ref[r, pl.ds(i, 1), :]
            u = u_ref[r, pl.ds(i, 1), :]
            dy = dy_ref[r, pl.ds(i, 1), :]
            keep = jnp.exp2(step * rate)
            b = b_ref[r, i]
            kept = keep * hist_ref[r, i]
            g = carried[r] + dy * c_ref[r, i]
            w = g * kept
            dc_ref[r, i] += (kept + u * b) * dy
            db_ref[r, i] += g * u
            du_ref[r, pl.ds(i, 1), :] = jnp.sum(g * b, axis=0, keepdims=True)
            dexp_ref[r, pl.ds(i, 1), :] = jnp.sum(w * rate, axis=0, keepdims=True)
            drate = drate + w * step
            new.append(keep * g)
        return tuple(new) + (drate,)

    start = tuple(later_ref[r] for r in range(rows)) + (jnp.zeros((DS, 128), f32),)
    end = lax.fori_loop(0, length, advance, start, unroll=2)
    drate_ref[0] = end[rows]


def scan_call(body, args, kinds, outs, rows_all, length, width):
    rows = 4 if rows_all % 4 == 0 else rows_all
    single = pl.Buffered(buffer_count=1)

    def spec(kind, one=False):
        extra = {"pipeline_mode": single} if one else {}
        if kind == "seq":
            return pl.BlockSpec((rows, length, 128), lambda r, g: (r, 0, g), **extra)
        if kind == "spread":
            return pl.BlockSpec((rows, length, DS, 128), lambda r, g: (r, 0, 0, 0), **extra)
        if kind == "hist":
            return pl.BlockSpec((rows, length, DS, 128), lambda r, g: (r, 0, 0, g), **extra)
        if kind == "state":
            return pl.BlockSpec((rows, DS, 128), lambda r, g: (r, 0, g), **extra)
        if kind == "rate":
            return pl.BlockSpec((DS, 128), lambda r, g: (0, g), **extra)
        return pl.BlockSpec((1, DS, 128), lambda r, g: (r, 0, g), **extra)

    shape_of = {
        "seq": (rows_all, length, width),
        "spread": (rows_all, length, DS, 128),
        "hist": (rows_all, length, DS, width),
        "state": (rows_all, DS, width),
        "drate": (rows_all // rows, DS, width),
    }
    return pl.pallas_call(
        functools.partial(body, rows, length),
        grid=(rows_all // rows, width // 128),
        in_specs=[spec(k, k == "spread") for k in kinds],
        out_specs=tuple(spec(k, k == "spread") for k in outs),
        out_shape=tuple(jax.ShapeDtypeStruct(shape_of[k], f32) for k in outs),
        compiler_params=pltpu.CompilerParams(vmem_limit_bytes=56 * MIB),
    )(*args)


def rms_norm(values, gain_row):
    return (
        values * lax.rsqrt(jnp.mean(values * values, axis=-1, keepdims=True) + norm_eps) * gain_row
    )


def dense(operand, partner):
    return jnp.dot(operand, partner, preferred_element_type=f32)


def dense_tn(operand, partner):
    return lax.dot_general(
        operand, partner, (((0,), (0,)), ((), ())), preferred_element_type=f32
    )


def dense_nt(operand, partner):
    return lax.dot_general(
        operand, partner, (((1,), (1,)), ((), ())), preferred_element_type=f32
    )


def conv_silu(extended, conv_taps, same_seg):
    length_out = extended.shape[1] - CONV + 1
    summed = jnp.zeros((extended.shape[0], length_out, extended.shape[2]), f32)
    for offset in range(CONV):
        summed = summed + jnp.where(
            same_seg[offset][:, :, None],
            extended[:, offset : offset + length_out] * conv_taps[offset],
            0.0,
        )
    return jax.nn.silu(summed)


def adam_step(gradient, moments_old, weight_now):
    first_moment = beta_one * moments_old[0] + (1.0 - beta_one) * gradient
    second_moment = beta_two * moments_old[1] + (1.0 - beta_two) * gradient * gradient
    corrected = (
        first_moment
        / (1.0 - beta_one**adam_count)
        / (jnp.sqrt(second_moment / (1.0 - beta_two**adam_count)) + adam_eps)
    )
    return (second_moment, -learn_rate * (corrected + decay_rate * weight_now))


def pad_last(values, width):
    return jnp.pad(values, [(0, 0)] * (values.ndim - 1) + [(0, width - values.shape[-1])])


def column_parts(weight, parts, shards_of, width):
    own = weight.shape[1] // parts // shards_of
    return jnp.stack(
        [
            jnp.concatenate(
                [
                    pad_last(weight[:, (p * shards_of + j) * own : (p * shards_of + j + 1) * own], width)
                    for p in range(parts)
                ],
                axis=1,
            )
            for j in range(shards_of)
        ]
    )


def shards(
    tokens,
    cotangent,
    segments,
    w_qkv,
    m_qkv,
    w_attn_out,
    m_attn_out,
    w_mamba_in,
    m_mamba_in,
    w_ssm_proj,
    m_ssm_proj,
    w_mamba_out,
    m_mamba_out,
    w_gate_up,
    m_gate_up,
    w_ffn_down,
    m_ffn_down,
    ssm_vec,
    m_ssm_vec,
    embed_small,
    m_embed_small,
):
    fs, cs = lax.axis_size("fsdp"), lax.axis_size("ctx")
    fi, ci = lax.axis_index("fsdp"), lax.axis_index("ctx")
    tok = tokens.shape[1]
    dim = tokens.shape[2]
    row_len = segments.shape[1]
    halves = cs // fs
    reach = min(row_len // 2, WINDOW) // tok
    metas = META // cs
    chan = DI // fs
    chan_p = ceil_to(chan, 128)
    ffw = FF // fs
    ffw_p = ceil_to(ffw, 128)
    heads_dim = NH * HD
    kv_dim = KVH * HD
    groups = NH // KVH
    scale_factor = HD ** (-0.5)
    xdim = DTR + 2 * DS
    both = ("fsdp", "ctx")

    cross = [
        (f * cs + c, (c // halves) * cs + halves * f + c % halves)
        for f in range(fs)
        for c in range(cs)
    ]

    def crossed(value):
        return lax.ppermute(value, both, cross)

    def weight_block(weight):
        rows, cols = weight.shape[0] // halves, weight.shape[1] // fs
        piece = lax.dynamic_slice(
            weight, ((ci % halves) * rows, (ci // halves) * cols), (rows, cols)
        )
        return crossed(piece)

    gu_send = column_parts(w_gate_up, 2, fs, ffw_p)
    mi_send = column_parts(w_mamba_in, 2, fs, chan_p)
    qkv_send = column_parts(w_qkv, 1, fs, w_qkv.shape[1] // fs)
    gain_rows = embed_small[META:]
    meta_rows = lax.dynamic_slice_in_dim(embed_small, ci * metas, metas, 0)
    source = tokens[0].astype(f32)
    normed_f, norm_pull = jax.vjp(rms_norm, source, gain_rows[0])
    normed = normed_f.astype(bf16)
    meta_f, meta_pull = jax.vjp(rms_norm, meta_rows, gain_rows[0])
    meta_low = meta_f.astype(bf16)

    normed_all, cot_all, seg_all, mi_w, qkv_w = exchange(
        "fsdp",
        0,
        [
            (normed, "all"),
            (cotangent[0], "all"),
            (segments, "all"),
            (mi_send, "each"),
            (qkv_send, "each"),
        ],
    )
    gu_w = lax.all_to_all(gu_send, "fsdp", 0, 0).reshape(dim, 2 * ffw_p)
    mi_w = mi_w.reshape(dim, 2 * chan_p)
    qkv_w = qkv_w.reshape(dim, -1)
    seg_all = seg_all.reshape(fs, row_len)
    seg_row = segments[0]
    normed_all = normed_all.reshape(fs * tok, dim)
    cot_all = cot_all.reshape(fs * tok, dim)
    xp_w = jnp.pad(w_ssm_proj[:, :xdim], ((0, chan_p - chan), (0, 0)))
    dt_w = jnp.pad(w_ssm_proj[:, xdim:], ((0, chan_p - chan), (0, 0)))
    mo_w = jnp.pad(w_mamba_out, ((0, chan_p - chan), (0, 0)))
    vec = pad_last(lax.dynamic_slice_in_dim(ssm_vec, fi * chan, chan, 1), chan_p)

    qkv_tp = dense(jnp.concatenate([normed_all, meta_low], axis=0), qkv_w).astype(bf16)
    qkv_parts = jnp.concatenate(
        [
            qkv_tp[: fs * tok].reshape(fs, tok, -1),
            jnp.broadcast_to(qkv_tp[fs * tok :][None], (fs, metas, qkv_tp.shape[1])),
        ],
        axis=1,
    )
    (qkv_got,) = exchange("fsdp", 1, [(qkv_parts, "each")])
    qkv_own = jnp.concatenate([qkv_got[j] for j in range(fs)], axis=1)
    queries = qkv_own[:tok, :heads_dim]
    keyval = qkv_own[:tok, heads_dim:]
    kv_before, meta_kv = exchange(
        "ctx", 2, [(keyval, "next"), (qkv_own[tok:, heads_dim:], "all")], reach
    )
    kv_before = jnp.where(
        (ci - 1 - jnp.arange(reach) >= 0)[:, None, None], kv_before, jnp.zeros_like(kv_before)
    )
    key_rows = jnp.concatenate(
        [meta_kv.reshape(META, 2 * kv_dim)]
        + [kv_before[d - 1] for d in range(reach, 0, -1)]
        + [keyval],
        axis=0,
    )

    mamba_in = dense(normed_all, mi_w).reshape(fs, tok, 2 * chan_p)
    inner_pre = mamba_in[:, :, :chan_p]
    gate_z = mamba_in[:, :, chan_p:]
    up_ring = [(c, c + 1) for c in range(cs - 1)]
    down_ring = [(c + 1, c) for c in range(cs - 1)]
    tail_rows = lax.ppermute(inner_pre[:, tok - (CONV - 1) :], "ctx", up_ring)
    extended = jnp.concatenate([tail_rows, inner_pre], axis=1)
    seg_ext = lax.dynamic_slice_in_dim(
        jnp.concatenate([jnp.full((fs, CONV - 1), -1, jnp.int32), seg_all], axis=1),
        ci * tok,
        tok + CONV - 1,
        1,
    )
    own_seg = seg_ext[:, CONV - 1 :]
    same_seg = [seg_ext[:, o : o + tok] == own_seg for o in range(CONV)]
    starts = own_seg != seg_ext[:, CONV - 2 : -1]
    inner_x, conv_pull = jax.vjp(
        lambda ext_rows, taps: conv_silu(ext_rows, taps, same_seg), extended, vec[:CONV]
    )
    inner_low = inner_x.astype(bf16).reshape(fs * tok, chan_p)
    xproj_part = pad_last(dense(inner_low, xp_w), ceil_to(xdim, 128))
    (xproj_got,) = exchange("fsdp", 3, [(xproj_part, "all")])
    xproj = jnp.sum(xproj_got, axis=0)
    delta_low = xproj[:, :DTR].astype(bf16)
    pre_delta = dense_nt(delta_low, dt_w).reshape(fs, tok, chan_p) + vec[CONV]
    step = jax.nn.softplus(pre_delta)
    step_far = jnp.where(starts[:, :, None], FAR, step)
    drive = step * inner_x

    def spread(columns):
        return jnp.broadcast_to(columns.reshape(fs, tok, DS, 1), (fs, tok, DS, 128))

    b_wide = spread(xproj[:, DTR : DTR + DS])
    c_wide = spread(xproj[:, DTR + DS : xdim])
    rate = -jnp.exp(vec[CONV + 2 :])
    rate2 = rate * LOG2E
    sizes = (fs, tok, chan_p)
    (last_state,) = scan_call(
        scan_tail_body,
        (step_far, drive, b_wide, rate2),
        ("seq", "seq", "spread", "rate"),
        ("state",),
        *sizes,
    )
    step_sum = jnp.sum(step_far, axis=1)
    state_before, sums = exchange(
        "ctx", 4, [(last_state.astype(bf16), "next"), (step_sum, "all")], reach
    )

    def decay_of(block):
        total = lax.dynamic_index_in_dim(sums, jnp.clip(block, 0, cs - 1), 0, keepdims=False)
        return jnp.exp2(total[:, None, :] * rate2)

    entry = jnp.zeros((fs, DS, chan_p), f32)
    for d in range(reach, 0, -1):
        there = jnp.where(ci >= d, state_before[d - 1].astype(f32), 0.0)
        entry = decay_of(ci - d) * entry + there
    readout, hist = scan_call(
        scan_full_body,
        (step_far, drive, b_wide, c_wide, rate2, entry),
        ("seq", "seq", "spread", "spread", "rate", "state"),
        ("seq", "hist"),
        *sizes,
    )
    skip = vec[CONV + 1]
    pre_mix = readout + skip * inner_x
    gate_s = jax.nn.sigmoid(gate_z)
    gate_silu = gate_z * gate_s
    mixture_low = (pre_mix * gate_silu).astype(bf16).reshape(fs * tok, chan_p)
    ssm_part = dense(mixture_low, mo_w).astype(bf16).reshape(fs, tok, dim)

    key_span = (reach + 1) * tok
    padded_seg = jnp.concatenate([jnp.full((reach * tok,), -1, jnp.int32), seg_row])
    key_seg = lax.dynamic_slice_in_dim(padded_seg, ci * tok, key_span, 0)
    query_seg = lax.dynamic_slice_in_dim(seg_row, ci * tok, tok, 0)
    query_pos = jnp.arange(tok, dtype=jnp.int32) + reach * tok
    key_pos = jnp.arange(key_span, dtype=jnp.int32)
    allowed = (
        (key_seg[None, :] == query_seg[:, None])
        & (key_pos[None, :] <= query_pos[:, None])
        & (query_pos[:, None] - key_pos[None, :] < WINDOW)
    )
    allowed = jnp.concatenate([jnp.ones((tok, META), jnp.bool_), allowed], axis=1)

    def group_scores(group_index):
        group_q = queries[:, group_index * groups * HD : (group_index + 1) * groups * HD].reshape(
            tok, groups, HD
        )
        group_k = key_rows[:, group_index * HD : (group_index + 1) * HD]
        group_v = key_rows[:, kv_dim + group_index * HD : kv_dim + (group_index + 1) * HD]
        raw_scores = (
            jnp.einsum("qhd,kd->hqk", group_q, group_k, preferred_element_type=f32) * scale_factor
        )
        return (group_q, group_k, group_v, jnp.where(allowed[None], raw_scores, -1e30))

    attended_parts = []
    log_totals = []
    for group_index in range(KVH):
        group_q, group_k, group_v, scores = group_scores(group_index)
        row_peak = jnp.max(scores, axis=-1, keepdims=True)
        exponent = jnp.exp(scores - row_peak)
        row_total = jnp.sum(exponent, axis=-1, keepdims=True)
        attention = (exponent / row_total).astype(bf16)
        log_totals.append(row_peak + jnp.log(row_total))
        attended_parts.append(
            jnp.einsum("hqk,kd->qhd", attention, group_v, preferred_element_type=f32).reshape(
                tok, groups * HD
            )
        )
    attended = jnp.concatenate(attended_parts, axis=1).astype(bf16)
    wide = heads_dim // fs
    (att_got,) = exchange(
        "fsdp",
        5,
        [(jnp.stack([attended[:, j * wide : (j + 1) * wide] for j in range(fs)]), "each")],
    )
    att_tp = att_got.reshape(fs * tok, wide)
    attn_part = dense(att_tp, w_attn_out).astype(bf16).reshape(fs, tok, dim)
    attn_got, ssm_got = exchange("fsdp", 6, [(attn_part, "each"), (ssm_part, "each")])
    attn_proj = jnp.sum(attn_got.astype(f32), axis=0)
    ssm_proj = jnp.sum(ssm_got.astype(f32), axis=0)
    attn_branch, attn_pull = jax.vjp(rms_norm, attn_proj, gain_rows[1])
    ssm_branch, ssm_norm_pull = jax.vjp(rms_norm, ssm_proj, gain_rows[2])
    residual = source + 0.5 * (attn_branch + ssm_branch)
    ffn_in_f, ffn_norm_pull = jax.vjp(rms_norm, residual, gain_rows[3])
    (ffn_in,) = exchange("fsdp", 7, [(ffn_in_f.astype(bf16), "all")])
    ffn_in = ffn_in.reshape(fs * tok, dim)

    gate_up = dense(ffn_in, gu_w)
    hidden_f, glu_pull = jax.vjp(
        lambda values: jax.nn.silu(values[:, :ffw_p]) * values[:, ffw_p:], gate_up
    )
    hidden = hidden_f.astype(bf16)[:, :ffw]
    down_part = dense(hidden, w_ffn_down).astype(bf16).reshape(fs, tok, dim)
    hidden_grad = pad_last(dense_nt(cot_all, w_ffn_down), ffw_p)
    gate_up_grad = glu_pull(hidden_grad)[0].astype(bf16)
    ffn_back = dense_nt(gate_up_grad, gu_w).astype(bf16).reshape(fs, tok, dim)
    back_got, down_got = exchange("fsdp", 8, [(ffn_back, "each"), (down_part, "each")])
    output = residual + jnp.sum(down_got.astype(f32), axis=0)
    resid_part, gain_ffn_grad = ffn_norm_pull(jnp.sum(back_got.astype(f32), axis=0))
    residual_grad = cotangent[0].astype(f32) + resid_part
    branch_grad = 0.5 * residual_grad
    attn_proj_grad, gain_attn_grad = attn_pull(branch_grad)
    ssm_proj_grad, gain_ssm_grad = ssm_norm_pull(branch_grad)
    attn_proj_low, ssm_proj_low = exchange(
        "fsdp", 9, [(attn_proj_grad.astype(bf16), "all"), (ssm_proj_grad.astype(bf16), "all")]
    )
    attn_proj_low = attn_proj_low.reshape(fs * tok, dim)
    ssm_proj_low = ssm_proj_low.reshape(fs * tok, dim)
    att_grad_tp = dense_nt(attn_proj_low, w_attn_out).astype(bf16).reshape(fs, tok, wide)
    (att_grad_got,) = exchange("fsdp", 10, [(att_grad_tp, "each")])
    attended_grad = jnp.concatenate([att_grad_got[j] for j in range(fs)], axis=1)

    mixture_grad = dense_nt(ssm_proj_low, mo_w).reshape(fs, tok, chan_p)
    read_grad = mixture_grad * gate_silu
    gate_grad = mixture_grad * pre_mix * (gate_s * (1.0 + gate_z * (1.0 - gate_s)))
    (first_adj,) = scan_call(
        adjoint_head_body,
        (step_far, read_grad, c_wide, rate2),
        ("seq", "seq", "spread", "rate"),
        ("state",),
        *sizes,
    )
    (adj_after,) = exchange("ctx", 11, [(first_adj.astype(bf16), "prev")], reach)
    later = jnp.zeros((fs, DS, chan_p), f32)
    for d in range(reach, 0, -1):
        there = jnp.where(ci + d < cs, adj_after[d - 1].astype(f32), 0.0)
        later = decay_of(ci + d) * later + there
    drive_grad, exp_grad, b_acc, c_acc, rate_grad = scan_call(
        adjoint_full_body,
        (step_far, drive, read_grad, b_wide, c_wide, rate2, hist, later),
        ("seq", "seq", "seq", "spread", "spread", "rate", "hist", "state"),
        ("seq", "seq", "spread", "spread", "drate"),
        *sizes,
    )
    step_grad = drive_grad * inner_x + exp_grad * LN2
    pre_delta_grad = step_grad * jax.nn.sigmoid(pre_delta)
    inner_grad = drive_grad * step + skip * read_grad
    small_grad = jnp.concatenate(
        [
            jnp.sum(pre_delta_grad, axis=(0, 1))[None],
            jnp.sum(inner_x * read_grad, axis=(0, 1))[None],
            jnp.sum(rate_grad, axis=0) * rate,
        ],
        axis=0,
    )
    pre_delta_low = pre_delta_grad.astype(bf16).reshape(fs * tok, chan_p)
    xgrad_part = pad_last(
        jnp.concatenate(
            [
                dense(pre_delta_low, dt_w),
                jnp.sum(b_acc, axis=-1).reshape(fs * tok, DS),
                jnp.sum(c_acc, axis=-1).reshape(fs * tok, DS),
            ],
            axis=1,
        ),
        ceil_to(xdim, 128),
    )
    (xgrad_got,) = exchange("fsdp", 12, [(xgrad_part, "all")])
    xproj_grad = jnp.sum(xgrad_got, axis=0)[:, :xdim].astype(bf16)
    inner_grad = inner_grad + dense_nt(xproj_grad, xp_w).reshape(fs, tok, chan_p)
    ext_grad, taps_grad = conv_pull(inner_grad)
    returned = lax.ppermute(ext_grad[:, : CONV - 1].astype(bf16), "ctx", down_ring).astype(f32)
    inner_pre_grad = ext_grad[:, CONV - 1 :] + jnp.pad(
        returned, ((0, 0), (tok - (CONV - 1), 0), (0, 0))
    )
    mamba_in_grad = (
        jnp.concatenate([inner_pre_grad, gate_grad], axis=2)
        .astype(bf16)
        .reshape(fs * tok, 2 * chan_p)
    )

    query_grads = []
    key_grads = []
    value_grads = []
    for group_index in range(KVH):
        group_q, group_k, group_v, scores = group_scores(group_index)
        attention_f = jnp.exp(scores - log_totals[group_index])
        attention = attention_f.astype(bf16)
        out_slice = attended_grad[
            :, group_index * groups * HD : (group_index + 1) * groups * HD
        ].reshape(tok, groups, HD)
        prob_grad = jnp.einsum("qhd,kd->hqk", out_slice, group_v, preferred_element_type=f32)
        value_grads.append(
            jnp.einsum("hqk,qhd->kd", attention, out_slice, preferred_element_type=f32)
        )
        score_grad = (
            attention_f * (prob_grad - jnp.sum(attention_f * prob_grad, axis=-1, keepdims=True))
        ).astype(bf16)
        query_grads.append(
            (
                jnp.einsum("hqk,kd->qhd", score_grad, group_k, preferred_element_type=f32)
                * scale_factor
            ).reshape(tok, groups * HD)
        )
        key_grads.append(
            jnp.einsum("hqk,qhd->kd", score_grad, group_q, preferred_element_type=f32)
            * scale_factor
        )
    kv_grad_all = jnp.concatenate(key_grads + value_grads, axis=1)
    kv_send = jnp.stack(
        [
            kv_grad_all[META + (reach - d) * tok : META + (reach - d + 1) * tok]
            for d in range(1, reach + 1)
        ]
    ).astype(bf16)
    meta_send = kv_grad_all[:META].astype(bf16).reshape(cs, metas, 2 * kv_dim)
    kv_back, meta_back = exchange("ctx", 13, [(kv_send, "back"), (meta_send, "each")], reach)
    own_kv_grad = kv_grad_all[META + reach * tok :]
    for d in range(1, reach + 1):
        own_kv_grad = own_kv_grad + jnp.where(ci + d < cs, kv_back[d - 1].astype(f32), 0.0)
    meta_kv_grad = jnp.sum(meta_back.astype(f32), axis=0).astype(bf16)
    qkv_grad = jnp.concatenate(
        [
            jnp.concatenate(
                [
                    jnp.concatenate(query_grads, axis=1).astype(bf16),
                    jnp.zeros((metas, heads_dim), bf16),
                ],
                axis=0,
            ),
            jnp.concatenate([own_kv_grad.astype(bf16), meta_kv_grad], axis=0),
        ],
        axis=1,
    )
    (qkv_grad_got,) = exchange(
        "fsdp", 14, [(column_parts(qkv_grad, 1, fs, qkv_grad.shape[1] // fs), "each")]
    )
    qkv_grad_tp = qkv_grad_got.reshape(fs * (tok + metas), -1)
    normed_back = dense_nt(qkv_grad_tp, qkv_w).reshape(fs, tok + metas, dim)
    normed_back = normed_back + jnp.pad(
        dense_nt(mamba_in_grad, mi_w).reshape(fs, tok, dim), ((0, 0), (0, metas), (0, 0))
    )
    (normed_got,) = exchange("fsdp", 15, [(normed_back.astype(bf16), "each")])
    normed_grad = jnp.sum(normed_got.astype(f32), axis=0)
    source_part, gain_in_grad = norm_pull(normed_grad[:tok])
    source_grad = residual_grad + source_part
    meta_grad, gain_in_meta = meta_pull(normed_grad[tok:])

    embed_grad = jnp.concatenate(
        [
            lax.dynamic_update_slice(jnp.zeros((META, dim), f32), meta_grad, (ci * metas, 0)),
            jnp.stack([gain_in_grad + gain_in_meta, gain_attn_grad, gain_ssm_grad, gain_ffn_grad]),
        ],
        axis=0,
    )
    vec_grad = jnp.concatenate([taps_grad, small_grad], axis=0)[:, :chan]
    vec_grad = lax.dynamic_update_slice(
        jnp.zeros((vec_grad.shape[0], DI), f32), vec_grad, (0, fi * chan)
    )
    ssm_total, embed_total = lax.psum((vec_grad, embed_grad), ("fsdp", "ctx"))

    def summed(value):
        return lax.psum_scatter(value, "ctx", scatter_dimension=0, tiled=True)

    def by_columns(operand, partner):
        rows = operand.shape[1] // halves
        cols = partner.shape[1] // fs
        pieces = jnp.stack([partner[:, j * cols : (j + 1) * cols] for j in range(fs)])
        grad = jnp.einsum("tr,jtn->jrn", operand, pieces, preferred_element_type=f32)
        return crossed(summed(grad.astype(bf16).reshape(cs * rows, cols))).astype(f32)

    even = fi % 2 == 0
    low_side = fi < fs // 2
    route_a = [(j, j // 2 if j % 2 == 0 else (fs + j) // 2) for j in range(fs)]
    route_b = [(j, (fs + j) // 2 if j % 2 == 0 else j // 2) for j in range(fs)]

    def paired(operand, partner, width):
        grad = summed(dense_tn(operand, partner).astype(bf16))
        padded = grad.shape[1] // 2
        first, second = grad[:, :padded], grad[:, padded:]
        got_a = lax.ppermute(jnp.where(even, first, second), "fsdp", route_a)
        got_b = lax.ppermute(jnp.where(even, second, first), "fsdp", route_b)
        left = jnp.where(low_side, got_a, got_b)[:, :width]
        right = jnp.where(low_side, got_b, got_a)[:, :width]
        return jnp.concatenate([left, right], axis=1).astype(f32)

    ffn_down_gradient = by_columns(hidden, cot_all)
    gate_up_gradient = paired(ffn_in, gate_up_grad, ffw)
    attn_gradient = by_columns(att_tp, attn_proj_low)
    mamba_out_gradient = by_columns(mixture_low[:, :chan], ssm_proj_low)
    mamba_in_gradient = paired(normed_all, mamba_in_grad, chan)
    ssm_proj_gradient = by_columns(
        jnp.concatenate([inner_low[:, :chan], pre_delta_low[:, :chan]], axis=0),
        jnp.concatenate(
            [
                jnp.pad(xproj_grad, ((0, 0), (0, DTR))),
                jnp.pad(delta_low, ((0, 0), (xdim, 0))),
            ],
            axis=0,
        ),
    )
    qkv_operand = jnp.concatenate(
        [
            normed_all.reshape(fs, tok, dim),
            jnp.broadcast_to(meta_low[None], (fs, metas, dim)),
        ],
        axis=1,
    ).reshape(fs * (tok + metas), dim)
    qkv_gradient = summed(dense_tn(qkv_operand, qkv_grad_tp).astype(bf16)).astype(f32)

    def adam_block(gradient, moments_old, weight):
        return adam_step(gradient, moments_old, weight_block(weight).astype(f32))

    qkv_moments, qkv_update = adam_block(qkv_gradient, m_qkv, w_qkv)
    attn_moments, attn_update = adam_block(attn_gradient, m_attn_out, w_attn_out)
    mamba_in_moments, mamba_in_update = adam_block(mamba_in_gradient, m_mamba_in, w_mamba_in)
    ssm_proj_moments, ssm_proj_update = adam_block(ssm_proj_gradient, m_ssm_proj, w_ssm_proj)
    mamba_out_moments, mamba_out_update = adam_block(mamba_out_gradient, m_mamba_out, w_mamba_out)
    gate_up_moments, gate_up_update = adam_block(gate_up_gradient, m_gate_up, w_gate_up)
    ffn_down_moments, ffn_down_update = adam_block(ffn_down_gradient, m_ffn_down, w_ffn_down)
    ssm_vec_moments, ssm_vec_update = adam_step(ssm_total, m_ssm_vec, ssm_vec)
    embed_moments, embed_update = adam_step(embed_total, m_embed_small, embed_small)
    return (
        output.astype(jnp.bfloat16)[None],
        source_grad[None],
        qkv_gradient,
        qkv_moments,
        qkv_update,
        attn_gradient,
        attn_moments,
        attn_update,
        mamba_in_gradient,
        mamba_in_moments,
        mamba_in_update,
        ssm_proj_gradient,
        ssm_proj_moments,
        ssm_proj_update,
        mamba_out_gradient,
        mamba_out_moments,
        mamba_out_update,
        gate_up_gradient,
        gate_up_moments,
        gate_up_update,
        ffn_down_gradient,
        ffn_down_moments,
        ffn_down_update,
        ssm_total,
        ssm_vec_moments,
        ssm_vec_update,
        embed_total,
        embed_moments,
        embed_update,
    )


def solution(mesh):
    in_specs = (
        P("fsdp", "ctx", None),
        P("fsdp", "ctx", None),
        P("fsdp", None),
        P("fsdp", None),
        P(None, "ctx", "fsdp"),
        P("fsdp", None),
        P(None, "ctx", "fsdp"),
        P("fsdp", None),
        P(None, "ctx", "fsdp"),
        P("fsdp", None),
        P(None, "ctx", "fsdp"),
        P("fsdp", None),
        P(None, "ctx", "fsdp"),
        P("fsdp", None),
        P(None, "ctx", "fsdp"),
        P("fsdp", None),
        P(None, "ctx", "fsdp"),
        P(),
        P(),
        P(),
        P(),
    )
    out_specs = (
        P("fsdp", "ctx", None),
        P("fsdp", "ctx", None),
        P("ctx", "fsdp"),
        P("ctx", "fsdp"),
        P("ctx", "fsdp"),
        P("ctx", "fsdp"),
        P("ctx", "fsdp"),
        P("ctx", "fsdp"),
        P("ctx", "fsdp"),
        P("ctx", "fsdp"),
        P("ctx", "fsdp"),
        P("ctx", "fsdp"),
        P("ctx", "fsdp"),
        P("ctx", "fsdp"),
        P("ctx", "fsdp"),
        P("ctx", "fsdp"),
        P("ctx", "fsdp"),
        P("ctx", "fsdp"),
        P("ctx", "fsdp"),
        P("ctx", "fsdp"),
        P("ctx", "fsdp"),
        P("ctx", "fsdp"),
        P("ctx", "fsdp"),
        P(),
        P(),
        P(),
        P(),
        P(),
        P(),
    )
    return jax.shard_map(shards, mesh=mesh, in_specs=in_specs, out_specs=out_specs, check_vma=False)
```

```python
import functools

import jax
import jax.numpy as jnp
from jax import lax
from jax.experimental import pallas as pl
from jax.experimental.pallas import tpu as pltpu
from jax.sharding import PartitionSpec as P

NH = 25
KVH = 5
HD = 64
DI = 3200
DS = 16
DTR = 100
FF = 5504
META = 128
CONV = 4
WINDOW = 1024

norm_eps = 1e-05
beta_one = 0.9
beta_two = 0.95
learn_rate = 0.01
decay_rate = 0.1
adam_eps = 1e-08
adam_count = 10.0

FSDP = "fsdp"
CTX = "ctx"
EACH = "each"
ALL = "all"
GATHER = "gather"
REDUCE = "reduce"
HALF = "half"
WEIGHTS = "weights"
BOTH = "both"
CROSS = "cross"
PAIR = "pair"
NEXT = "next"
PREV = "prev"
BACK = "back"
LINE = "line"
SEQ = "seq"
SPREAD = "spread"
HIST = "hist"
STATE = "state"
RATE = "rate"
DRATE = "drate"
RING = "ring"
LOG2E = 1.4426950408889634
LN2 = 0.6931471805599453
FAR = 1e30
bf16 = jnp.bfloat16
f32 = jnp.float32
ANY = pl.BlockSpec(memory_space=pltpu.HBM)
MIB = 1024 * 1024


def together(*values):
    return lax.optimization_barrier(values)


def ceil_to(value, unit):
    return (value + unit - 1) // unit * unit


def span_of(axis):
    return lax.axis_size(axis), lax.axis_index(axis)


def ring_spot(ci, cs):
    odd = lax.rem(ci, 2)
    return (ci // 2) * (1 - odd) + (cs - 1 - ci // 2) * odd


def ring_block(spot, cs):
    spot = lax.rem(spot + 2 * cs, cs)
    far = spot // (cs // 2)
    return 2 * spot * (1 - far) + (2 * (cs - 1 - spot) + 1) * far


def when(condition, action):
    if condition is None:
        action()
    else:
        pl.when(condition)(action)


class Ring:
    def __init__(self, chunks, uses):
        self.chunks, self.uses = chunks, uses
        self.got, self.hop = [], 0

    def finish(self):
        block = lax.axis_index(CTX)
        sums = []
        for (k, part, _), got in zip(self.uses, self.got):
            own = lax.dynamic_index_in_dim(self.chunks[k], block, 0, keepdims=False)[part]
            sums.append(got.astype(f32) + own.astype(f32))
        return sums


class Traffic:
    def __init__(self, items, ring=None, hops=0, reach=0):
        self.items, self.ring, self.reach = items, ring, reach
        fs, cs = lax.axis_size(FSDP), lax.axis_size(CTX)
        self.hops = min(hops, cs - 1 - ring.hop) if ring is not None else 0
        self.ins = [value for value, _, _ in items]
        self.outs = []
        dma = pltpu.SemaphoreType.DMA
        most = 2 * max(fs, cs)
        count = max(len(items), 1)
        self.scratch = [dma((count, most)), dma((count, most)), dma((count, 2))]
        self.places = {}

        def own_scratch(k, shapes):
            self.places[k] = len(self.scratch)
            self.scratch += shapes

        for k, (value, mode, axis) in enumerate(items):
            shape = value.shape
            if mode in (ALL, GATHER, LINE):
                shape = (lax.axis_size(axis),) + shape
            elif mode in (NEXT, PREV):
                shape = (reach,) + shape
            elif mode == REDUCE:
                shape = (fs // 2,) + shape[1:]
                own_scratch(k, [pltpu.VMEM(shape, value.dtype)] * 2 + [dma((fs // 2,))])
            elif mode[0] == HALF:
                pieces = mode[2] - mode[1]
                shape = shape[:2] + (pieces,) + shape[3:]
                own_scratch(k, [dma((pieces, 2 * fs)), dma((pieces, 2 * fs))])
            self.outs.append(jax.ShapeDtypeStruct(shape, value.dtype))
        if self.hops:
            self.ins += list(ring.chunks) + list(ring.got)
            uses = len(ring.uses)
            shapes = [dma((uses, self.hops)), dma((uses, self.hops)), dma((uses, self.hops, 2))]
            for k, _, _ in ring.uses:
                shape = ring.chunks[k].shape[2:]
                self.outs += [jax.ShapeDtypeStruct(shape, bf16)] * self.hops
                shapes.append(pltpu.VMEM((self.hops, 2) + shape, bf16))
            own_scratch(RING, shapes)

    def vmem(self):
        total = 4 * MIB
        for held in self.scratch:
            if held.memory_space == pltpu.VMEM:
                size = 2
                for extent in held.shape[:-2]:
                    size *= extent
                total += size * ceil_to(held.shape[-2], 16) * ceil_to(held.shape[-1], 128)
        return total

    def bind(self, ins, outs, scratch):
        self.in_refs, self.out_refs, self.sems = ins, outs, scratch

    def remote(self, source, target, send, take, peer):
        return pltpu.make_async_remote_copy(
            src_ref=source,
            dst_ref=target,
            send_sem=send,
            recv_sem=take,
            device_id=peer,
            device_id_type=pl.DeviceIdType.MESH,
        )

    def greet(self):
        barrier = pltpu.get_barrier_semaphore()
        fs, fi = span_of(FSDP)
        cs, ci = span_of(CTX)

        def signal(peer):
            pl.semaphore_signal(
                barrier, inc=1, device_id=peer, device_id_type=pl.DeviceIdType.MESH
            )

        axes = {axis for _, _, axis in self.items}
        if WEIGHTS in axes:
            axes.add(FSDP)
        total = 0
        for axis in (FSDP, CTX):
            if axis in axes:
                n, me = span_of(axis)
                for d in range(1, n):
                    signal({axis: lax.rem(me + d, n)})
                total += n - 1
        if self.hops and CTX not in axes:
            spot = ring_spot(ci, cs)
            signal({CTX: ring_block(spot + 1, cs)})
            signal({CTX: ring_block(spot - 1, cs)})
            total += 2
        if WEIGHTS in axes and CTX not in axes:
            signal({CTX: ci + 1 - 2 * lax.rem(ci, 2)})
            total += 1
        if BOTH in axes:
            halves = cs // fs
            away = ci // halves != fi

            def meet():
                signal({FSDP: ci // halves, CTX: halves * fi + lax.rem(ci, halves)})

            pl.when(away)(meet)
            if total:
                pl.semaphore_wait(barrier, total + jnp.where(away, 1, 0))
            else:
                pl.when(away)(lambda: pl.semaphore_wait(barrier, 1))
        else:
            pl.semaphore_wait(barrier, total)

    def copies(self):
        starts, relays, waits = [], [], []
        fs, fi = span_of(FSDP)
        cs, ci = span_of(CTX)
        send_sem, take_sem, own_sem = self.sems[:3]
        for k, (_, mode, axis) in enumerate(self.items):
            src, dst = self.in_refs[k], self.out_refs[k]

            def add(copy, sends=None, takes=None):
                starts.append((copy.start, sends))
                waits.append((copy.wait_send, sends))
                waits.append((copy.wait_recv, takes))

            def keep(copy, condition=None):
                starts.append((copy.start, condition))
                waits.append((copy.wait, condition))

            core, chip, chips = lax.rem(fi, 2), fi // 2, fs // 2
            mate = {FSDP: fi + 1 - 2 * core}

            def relay(first, second):
                starts.append((first.start, None))
                relays.append((first.wait_recv, None))
                relays.append((second.start, None))
                waits.append((first.wait_send, None))
                waits.append((second.wait_send, None))
                waits.append((second.wait_recv, None))

            if mode == GATHER:
                for d in range(1, chips):
                    to = 2 * lax.rem(chip + d, chips) + core
                    came = 2 * lax.rem(chip + chips - d, chips) + core
                    relay(
                        self.remote(
                            src, dst.at[fi], send_sem.at[k, d], take_sem.at[k, d], {FSDP: to}
                        ),
                        self.remote(
                            dst.at[came],
                            dst.at[came],
                            send_sem.at[k, chips + d],
                            take_sem.at[k, chips + d],
                            mate,
                        ),
                    )
                add(self.remote(src, dst.at[fi], send_sem.at[k, 0], take_sem.at[k, 0], mate))
                keep(pltpu.make_async_copy(src, dst.at[fi], own_sem.at[k, 0]))
            elif mode == LINE:
                across = {CTX: ci + 1 - 2 * lax.rem(ci, 2)}
                for d in range(1, cs // 2):
                    came = lax.rem(ci + cs - 2 * d, cs)
                    relay(
                        self.remote(
                            src,
                            dst.at[ci],
                            send_sem.at[k, d],
                            take_sem.at[k, d],
                            {CTX: lax.rem(ci + 2 * d, cs)},
                        ),
                        self.remote(
                            dst.at[came],
                            dst.at[came],
                            send_sem.at[k, cs // 2 + d],
                            take_sem.at[k, cs // 2 + d],
                            across,
                        ),
                    )
                add(self.remote(src, dst.at[ci], send_sem.at[k, 0], take_sem.at[k, 0], across))
                keep(pltpu.make_async_copy(src, dst.at[ci], own_sem.at[k, 0]))
            elif mode == REDUCE:
                mine, other, load_sem = self.sems[self.places[k] : self.places[k] + 3]
                for d in list(range(1, chips)) + [0]:
                    to = lax.rem(chip + d, chips)
                    first = self.remote(
                        src.at[2 * to + 1 - core],
                        other.at[to],
                        send_sem.at[k, d],
                        take_sem.at[k, d],
                        mate,
                    )
                    load = pltpu.make_async_copy(
                        src.at[2 * to + core], mine.at[to], load_sem.at[d]
                    )
                    starts.append((first.start, None))
                    starts.append((load.start, None))
                    relays.append((load.wait, None))
                    relays.append((first.wait_recv, None))
                    waits.append((first.wait_send, None))

                    def total(mine=mine, other=other, to=to):
                        mine[to] = mine[to] + other[to]

                    relays.append((total, None))
                    if d:
                        second = self.remote(
                            mine.at[to],
                            dst.at[chip],
                            send_sem.at[k, chips + d],
                            take_sem.at[k, chips + d],
                            {FSDP: 2 * to + core},
                        )
                        waits.append((second.wait_send, None))
                        waits.append((second.wait_recv, None))
                    else:
                        second = pltpu.make_async_copy(mine.at[to], dst.at[to], own_sem.at[k, 0])
                        waits.append((second.wait, None))
                    relays.append((second.start, None))
            elif mode[0] == HALF:
                piece_send, piece_take = self.sems[self.places[k] : self.places[k] + 2]
                side = lax.rem(ci, 2)
                across = {CTX: ci + 1 - 2 * side}
                for q in range(mode[2] - mode[1]):
                    for d in range(1, chips):
                        for b in range(2):
                            to = 2 * lax.rem(chip + d, chips) + lax.rem(core + b, 2)
                            came = 2 * lax.rem(chip + chips - d, chips) + lax.rem(core + b, 2)
                            e = 2 * d + b
                            relay(
                                self.remote(
                                    src.at[to, side, mode[1] + q],
                                    dst.at[fi, side, q],
                                    piece_send.at[q, e],
                                    piece_take.at[q, e],
                                    {FSDP: to},
                                ),
                                self.remote(
                                    dst.at[came, side, q],
                                    dst.at[came, side, q],
                                    piece_send.at[q, fs + e],
                                    piece_take.at[q, fs + e],
                                    across,
                                ),
                            )
                for b in range(2):
                    to = mate[FSDP]
                    add(
                        self.remote(
                            src.at[to, b, mode[1] : mode[2]],
                            dst.at[fi, b],
                            send_sem.at[k, b],
                            take_sem.at[k, b],
                            mate,
                        )
                    )
                    keep(
                        pltpu.make_async_copy(
                            src.at[fi, b, mode[1] : mode[2]], dst.at[fi, b], own_sem.at[k, b]
                        )
                    )
            elif mode in (ALL, EACH):
                n, me = span_of(axis)
                for d in range(1, n):
                    peer = lax.rem(me + d, n)
                    source = src.at[peer] if mode == EACH else src
                    add(
                        self.remote(
                            source, dst.at[me], send_sem.at[k, d], take_sem.at[k, d], {axis: peer}
                        )
                    )
                source = src.at[me] if mode == EACH else src
                keep(pltpu.make_async_copy(source, dst.at[me], own_sem.at[k, 0]))
            elif mode == PAIR:
                for p in range(2):
                    peer = (p * fs + fi) // 2
                    slot = lax.rem(fi, 2)
                    away = peer != fi
                    q = 2 * fi + p
                    comes = lax.rem(q, fs) != fi
                    copy = self.remote(
                        src.at[p],
                        dst.at[slot],
                        send_sem.at[k, p],
                        take_sem.at[k, slot],
                        {FSDP: peer},
                    )
                    starts.append((copy.start, away))
                    waits.append((copy.wait_send, away))
                    taken = self.remote(
                        src.at[p], dst.at[p], send_sem.at[k, p], take_sem.at[k, p], {FSDP: peer}
                    )
                    waits.append((taken.wait_recv, comes))
                    keep(
                        pltpu.make_async_copy(src.at[p], dst.at[slot], own_sem.at[k, p]),
                        peer == fi,
                    )
            elif mode == CROSS:
                halves = cs // fs
                away = ci // halves != fi
                peer = {FSDP: ci // halves, CTX: halves * fi + lax.rem(ci, halves)}
                add(self.remote(src, dst, send_sem.at[k, 0], take_sem.at[k, 0], peer), away, away)
                keep(pltpu.make_async_copy(src, dst, own_sem.at[k, 0]), ci // halves == fi)
            else:
                for d in range(1, self.reach + 1):
                    up = mode == NEXT
                    peer = ci + d if up else ci - d
                    source = src.at[d - 1] if mode == BACK else src
                    add(
                        self.remote(
                            source,
                            dst.at[d - 1],
                            send_sem.at[k, d],
                            take_sem.at[k, d],
                            {CTX: lax.rem(peer + cs, cs)},
                        ),
                        peer < cs if up else peer >= 0,
                        ci - d >= 0 if up else ci + d < cs,
                    )
        return starts, relays, waits

    def ring_refs(self, u):
        base = self.places[RING]
        outs = self.out_refs[len(self.items) + u * self.hops :]
        return self.sems[base], self.sems[base + 1], self.sems[base + 2], self.sems[base + 3 + u], outs

    def hop_copy(self, u, t):
        cs, ci = span_of(CTX)
        spot = ring_spot(ci, cs)
        k, part, way = self.ring.uses[u]
        send, take, _, buffer, outs = self.ring_refs(u)
        if self.ring.hop + t == 0:
            source = self.in_refs[len(self.items) + k].at[ring_block(spot - way, cs), part]
        else:
            source = buffer.at[t, 1]
        return self.remote(
            source, outs[t], send.at[u, t], take.at[u, t], {CTX: ring_block(spot + way, cs)}
        )

    def load_own(self, u, t):
        cs, ci = span_of(CTX)
        k, part, way = self.ring.uses[u]
        _, _, load, buffer, _ = self.ring_refs(u)
        block = ring_block(ring_spot(ci, cs) - way * (self.ring.hop + t + 1), cs)
        return pltpu.make_async_copy(
            self.in_refs[len(self.items) + k].at[block, part], buffer.at[t, 1], load.at[u, t, 1]
        )

    def load_got(self, u, t):
        _, _, load, buffer, outs = self.ring_refs(u)
        if t == 0:
            source = self.in_refs[len(self.items) + len(self.ring.chunks) + u]
        else:
            source = outs[t - 1]
        return pltpu.make_async_copy(source, buffer.at[t, 0], load.at[u, t, 0])

    def hop_step(self, t):
        uses = range(len(self.ring.uses))
        if self.ring.hop + t > 0:
            for u in uses:
                self.load_own(u, t).start()
                if t > 0:
                    self.hop_copy(u, t - 1).wait_recv()
                self.load_got(u, t).start()
        for u in uses:
            if self.ring.hop + t > 0:
                self.load_own(u, t).wait()
                self.load_got(u, t).wait()
                buffer = self.ring_refs(u)[3]
                buffer[t, 1] = buffer[t, 0] + buffer[t, 1]
            self.hop_copy(u, t).start()

    def begin(self):
        self.greet()
        for start, condition in self.copies()[0]:
            when(condition, start)
        if self.hops:
            self.hop_step(0)

    def end(self, hopped=1):
        _, relays, waits = self.copies()
        for step, condition in relays:
            when(condition, step)
        for t in range(hopped, self.hops):
            self.hop_step(t)
        for wait, condition in waits:
            when(condition, wait)
        for u in range(len(self.ring.uses) if self.hops else 0):
            for t in range(self.hops):
                self.hop_copy(u, t).wait_send()
            self.hop_copy(u, self.hops - 1).wait_recv()

    def take(self, results):
        count = len(self.items)
        if self.hops:
            last = count + self.hops - 1
            self.ring.got = [results[last + u * self.hops] for u in range(len(self.ring.uses))]
            self.ring.hop += self.hops
        return tuple(results[:count])


def exchange(cid, items, ring=None, hops=0, reach=0):
    plan = Traffic(items, ring, hops, reach)
    ins, outs = len(plan.ins), len(plan.outs)

    def body(*refs):
        plan.bind(refs[:ins], refs[ins : ins + outs], refs[ins + outs :])
        plan.begin()
        plan.end()

    results = pl.pallas_call(
        body,
        out_shape=tuple(plan.outs),
        in_specs=[ANY] * ins,
        out_specs=(ANY,) * outs,
        scratch_shapes=plan.scratch,
        compiler_params=pltpu.CompilerParams(
            collective_id=cid, has_side_effects=True, vmem_limit_bytes=plan.vmem() + 4 * MIB
        ),
    )(*plan.ins)
    return plan.take(results)


def scan_tail_body(rows, length, step_ref, u_ref, b_ref, rate_ref, last_ref):
    rate = rate_ref[...]

    def advance(i, states):
        new = []
        for r in range(rows):
            keep = jnp.exp2(step_ref[r, pl.ds(i, 1), :] * rate)
            new.append(keep * states[r] + u_ref[r, pl.ds(i, 1), :] * b_ref[r, i])
        return tuple(new)

    start = tuple(jnp.zeros((DS, 128), f32) for _ in range(rows))
    end = lax.fori_loop(0, length, advance, start, unroll=4)
    for r in range(rows):
        last_ref[r] = end[r]


def scan_full_body(
    rows, length, step_ref, u_ref, b_ref, c_ref, rate_ref, entry_ref, read_ref, hist_ref
):
    rate = rate_ref[...]

    def advance(i, states):
        new = []
        for r in range(rows):
            hist_ref[r, i] = states[r]
            keep = jnp.exp2(step_ref[r, pl.ds(i, 1), :] * rate)
            h = keep * states[r] + u_ref[r, pl.ds(i, 1), :] * b_ref[r, i]
            read_ref[r, pl.ds(i, 1), :] = jnp.sum(h * c_ref[r, i], axis=0, keepdims=True)
            new.append(h)
        return tuple(new)

    lax.fori_loop(0, length, advance, tuple(entry_ref[r] for r in range(rows)), unroll=4)


def adjoint_head_body(rows, length, step_ref, dy_ref, c_ref, rate_ref, first_ref):
    rate = rate_ref[...]

    def advance(k, carried):
        i = length - 1 - k
        new = []
        for r in range(rows):
            keep = jnp.exp2(step_ref[r, pl.ds(i, 1), :] * rate)
            new.append(keep * (carried[r] + dy_ref[r, pl.ds(i, 1), :] * c_ref[r, i]))
        return tuple(new)

    start = tuple(jnp.zeros((DS, 128), f32) for _ in range(rows))
    end = lax.fori_loop(0, length, advance, start, unroll=4)
    for r in range(rows):
        first_ref[r] = end[r]


def adjoint_full_body(
    rows,
    length,
    step_ref,
    u_ref,
    dy_ref,
    b_ref,
    c_ref,
    rate_ref,
    hist_ref,
    later_ref,
    du_ref,
    dexp_ref,
    db_ref,
    dc_ref,
    drate_ref,
):
    rate = rate_ref[...]

    @pl.when(pl.program_id(1) == 0)
    def _():
        db_ref[...] = jnp.zeros_like(db_ref)
        dc_ref[...] = jnp.zeros_like(dc_ref)

    def advance(k, carried):
        i = length - 1 - k
        new = []
        drate = carried[rows]
        for r in range(rows):
            step = step_ref[r, pl.ds(i, 1), :]
            u = u_ref[r, pl.ds(i, 1), :]
            dy = dy_ref[r, pl.ds(i, 1), :]
            keep = jnp.exp2(step * rate)
            b = b_ref[r, i]
            kept = keep * hist_ref[r, i]
            g = carried[r] + dy * c_ref[r, i]
            w = g * kept
            dc_ref[r, i] += (kept + u * b) * dy
            db_ref[r, i] += g * u
            du_ref[r, pl.ds(i, 1), :] = jnp.sum(g * b, axis=0, keepdims=True)
            dexp_ref[r, pl.ds(i, 1), :] = jnp.sum(w * rate, axis=0, keepdims=True)
            drate = drate + w * step
            new.append(keep * g)
        return tuple(new) + (drate,)

    start = tuple(later_ref[r] for r in range(rows)) + (jnp.zeros((DS, 128), f32),)
    end = lax.fori_loop(0, length, advance, start, unroll=2)
    drate_ref[0] = end[rows]


def hosted_call(body, grid, in_specs, out_specs, out_shape, args, cid, plan, own_vmem, later=()):
    steps = 1
    for size in grid:
        steps *= size
    n_in, n_out, x_in, x_out = len(args), len(out_shape), len(plan.ins), len(plan.outs)

    def hosted(*refs):
        mine_in, refs = refs[:n_in], refs[n_in:]
        plan_in, refs = refs[:x_in], refs[x_in:]
        mine_out, refs = refs[:n_out], refs[n_out:]
        plan.bind(plan_in, refs[:x_out], refs[x_out:])
        at = pl.program_id(0)
        for k in range(1, len(grid)):
            at = at * grid[k] + pl.program_id(k)
        pl.when(at == 0)(plan.begin)
        for t in range(1, min(plan.hops, len(later) + 1)):
            pl.when(at == later[t - 1])(functools.partial(plan.hop_step, t))
        body(*mine_in, *mine_out)
        pl.when(at == steps - 1)(functools.partial(plan.end, 1 + len(later)))

    results = pl.pallas_call(
        hosted,
        grid=grid,
        in_specs=in_specs + [ANY] * x_in,
        out_specs=tuple(out_specs) + (ANY,) * x_out,
        out_shape=tuple(out_shape) + tuple(plan.outs),
        scratch_shapes=plan.scratch,
        compiler_params=pltpu.CompilerParams(
            vmem_limit_bytes=plan.vmem() + own_vmem, collective_id=cid, has_side_effects=True
        ),
    )(*args, *plan.ins)
    return tuple(results[:n_out]) + plan.take(results[n_out:])


def scan_call(body, args, kinds, outs, rows_all, length, width, cid, plan, later=()):
    rows = 4 if rows_all % 4 == 0 else rows_all
    single = pl.Buffered(buffer_count=1)
    grid = (rows_all // rows, width // 128)

    def spec(kind):
        extra = {"pipeline_mode": single} if kind == SPREAD else {}
        if kind == SEQ:
            return pl.BlockSpec((rows, length, 128), lambda r, g: (r, 0, g), **extra)
        if kind == SPREAD:
            return pl.BlockSpec((rows, length, DS, 128), lambda r, g: (r, 0, 0, 0), **extra)
        if kind == HIST:
            return pl.BlockSpec((rows, length, DS, 128), lambda r, g: (r, 0, 0, g), **extra)
        if kind == STATE:
            return pl.BlockSpec((rows, DS, 128), lambda r, g: (r, 0, g), **extra)
        if kind == RATE:
            return pl.BlockSpec((DS, 128), lambda r, g: (0, g), **extra)
        return pl.BlockSpec((1, DS, 128), lambda r, g: (r, 0, g), **extra)

    def block_bytes(kind):
        wide = rows * length * 128 * 4
        return {SEQ: 2 * wide, SPREAD: DS * wide, HIST: 2 * DS * wide}.get(kind, MIB // 2)

    shape_of = {
        SEQ: (rows_all, length, width),
        SPREAD: (rows_all, length, DS, 128),
        HIST: (rows_all, length, DS, width),
        STATE: (rows_all, DS, width),
        DRATE: (rows_all // rows, DS, width),
    }
    return hosted_call(
        functools.partial(body, rows, length),
        grid,
        [spec(k) for k in kinds],
        [spec(k) for k in outs],
        [jax.ShapeDtypeStruct(shape_of[k], f32) for k in outs],
        args,
        cid,
        plan,
        8 * MIB + sum(block_bytes(k) for k in tuple(kinds) + tuple(outs)),
        later,
    )


def attend_body(heads, q_ref, k_ref, v_ref, bias_ref, out_ref, total_ref):
    keys = k_ref[...].T
    for h in range(heads):
        rows = slice(h * HD, (h + 1) * HD)
        scores = jnp.dot(keys, q_ref[rows], preferred_element_type=f32)
        scores = scores * HD**-0.5 + bias_ref[...]
        peak = jnp.max(scores, axis=0, keepdims=True)
        grown = jnp.exp(scores - peak)
        total = jnp.sum(grown, axis=0, keepdims=True)
        probs = (grown * (1.0 / total)).astype(bf16)
        out_ref[rows] = jnp.dot(v_ref[...], probs, preferred_element_type=f32).astype(bf16)
        total_ref[0, h : h + 1] = peak + jnp.log(total)


def attend_back_body(
    heads, q_ref, k_ref, v_ref, bias_ref, total_ref, grad_ref, dq_ref, dk_ref, dv_ref
):
    keys = k_ref[...].T
    values = v_ref[...].T
    for h in range(heads):
        rows = slice(h * HD, (h + 1) * HD)
        scores = jnp.dot(keys, q_ref[rows], preferred_element_type=f32)
        probs = jnp.exp(scores * HD**-0.5 + bias_ref[...] - total_ref[0, h : h + 1])
        grad = jnp.dot(values, grad_ref[rows], preferred_element_type=f32)
        mean = jnp.sum(probs * grad, axis=0, keepdims=True)
        low = (probs * (grad - mean)).astype(bf16)
        dq = jnp.dot(k_ref[...], low, preferred_element_type=f32)
        dq_ref[rows] = (dq * HD**-0.5).astype(bf16)
        dk = dense_nt(q_ref[rows], low) * HD**-0.5
        dv = dense_nt(grad_ref[rows], probs.astype(bf16))
        if h == 0:
            dk_ref[...] = dk
            dv_ref[...] = dv
        else:
            dk_ref[...] += dk
            dv_ref[...] += dv


def rms_norm(values, gain_row):
    return (
        values * lax.rsqrt(jnp.mean(values * values, axis=-1, keepdims=True) + norm_eps) * gain_row
    )


def dense(operand, partner):
    return jnp.dot(operand, partner, preferred_element_type=f32)


def dense_tn(operand, partner):
    return lax.dot_general(
        operand, partner, (((0,), (0,)), ((), ())), preferred_element_type=f32
    )


def dense_nt(operand, partner):
    return lax.dot_general(
        operand, partner, (((1,), (1,)), ((), ())), preferred_element_type=f32
    )


def conv_silu(extended, conv_taps, same_seg):
    length_out = extended.shape[1] - CONV + 1
    summed = jnp.zeros((extended.shape[0], length_out, extended.shape[2]), f32)
    for offset in range(CONV):
        summed = summed + jnp.where(
            same_seg[offset][:, :, None],
            extended[:, offset : offset + length_out] * conv_taps[offset],
            0.0,
        )
    return jax.nn.silu(summed)


def adam_step(gradient, moments_old, weight_now):
    first_moment = beta_one * moments_old[0] + (1.0 - beta_one) * gradient
    second_moment = beta_two * moments_old[1] + (1.0 - beta_two) * gradient * gradient
    corrected = (
        first_moment
        / (1.0 - beta_one**adam_count)
        / (jnp.sqrt(second_moment / (1.0 - beta_two**adam_count)) + adam_eps)
    )
    return (second_moment, -learn_rate * (corrected + decay_rate * weight_now))


def pad_last(values, width):
    return jnp.pad(values, [(0, 0)] * (values.ndim - 1) + [(0, width - values.shape[-1])])


def column_parts(weight, parts, shards_of, width):
    own = weight.shape[1] // parts // shards_of
    return jnp.stack(
        [
            jnp.concatenate(
                [
                    pad_last(weight[:, (p * shards_of + j) * own : (p * shards_of + j + 1) * own], width)
                    for p in range(parts)
                ],
                axis=1,
            )
            for j in range(shards_of)
        ]
    )


def shards(
    tokens,
    cotangent,
    segments,
    w_qkv,
    m_qkv,
    w_attn_out,
    m_attn_out,
    w_mamba_in,
    m_mamba_in,
    w_ssm_proj,
    m_ssm_proj,
    w_mamba_out,
    m_mamba_out,
    w_gate_up,
    m_gate_up,
    w_ffn_down,
    m_ffn_down,
    ssm_vec,
    m_ssm_vec,
    embed_small,
    m_embed_small,
):
    fs, cs = lax.axis_size(FSDP), lax.axis_size(CTX)
    fi, ci = lax.axis_index(FSDP), lax.axis_index(CTX)
    tok = tokens.shape[1]
    dim = tokens.shape[2]
    row_len = segments.shape[1]
    halves = cs // fs
    reach = min(row_len // 2, WINDOW) // tok
    metas = META // cs
    chan = DI // fs
    chan_p = ceil_to(chan, 128)
    ffw = FF // fs
    ffw_p = ceil_to(ffw, 128)
    heads_dim = NH * HD
    kv_dim = KVH * HD
    groups = NH // KVH
    scale_factor = HD ** (-0.5)
    xdim = DTR + 2 * DS
    both = (FSDP, CTX)

    def row_block(weight):
        rows, cols = weight.shape[0] // halves, weight.shape[1] // fs
        return lax.dynamic_slice(
            weight, ((ci % halves) * rows, (ci // halves) * cols), (rows, cols)
        )

    def unpaired(value, width):
        return jnp.concatenate([value[0][:, :width], value[1][:, :width]], axis=1).astype(f32)

    def spread_hops(weights):
        total, done, out = sum(weights), 0, []
        for k in range(len(weights)):
            upto = (cs - 1) * sum(weights[: k + 1]) // total
            out.append(upto - done)
            done = upto
        return out

    def row_chunks(operand, partner):
        grad = dense_tn(operand, partner).astype(bf16)
        return grad.reshape(cs, 1, grad.shape[0] // cs, grad.shape[1])

    def column_chunks(operand, partner, parts=1):
        cols = partner.shape[1] // fs
        pieces = jnp.stack([partner[:, j * cols : (j + 1) * cols] for j in range(fs)])
        grad = jnp.einsum("tr,jtn->jrn", operand, pieces, preferred_element_type=f32)
        return grad.astype(bf16).reshape(cs, parts, operand.shape[1] // halves // parts, cols)

    def in_blocks(value):
        return value.reshape(fs, 2, 5, value.shape[1] // 10, value.shape[2])

    mi_send = column_parts(w_mamba_in, 2, fs, chan_p)
    qkv_send = column_parts(w_qkv, 1, fs, w_qkv.shape[1] // fs)
    gain_rows = embed_small[META:]
    meta_rows = lax.dynamic_slice_in_dim(embed_small, ci * metas, metas, 0)
    source = tokens[0].astype(f32)
    normed_f, norm_pull = jax.vjp(rms_norm, source, gain_rows[0])
    normed = normed_f.astype(bf16)
    meta_f, meta_pull = jax.vjp(rms_norm, meta_rows, gain_rows[0])
    meta_low = meta_f.astype(bf16)

    blocks = 5
    normed_all, seg_all, mi_w, qkv_w = exchange(
        0,
        [
            (normed, GATHER, FSDP),
            (segments, ALL, FSDP),
            (in_blocks(mi_send), (HALF, 0, blocks), WEIGHTS),
            (in_blocks(qkv_send), (HALF, 0, blocks), WEIGHTS),
        ],
    )
    gu_send = in_blocks(column_parts(w_gate_up, 2, fs, ffw_p))
    mi_w = mi_w.reshape(dim, 2 * chan_p)
    qkv_w = qkv_w.reshape(dim, -1)
    seg_all = seg_all.reshape(fs, row_len)
    seg_row = segments[0]
    normed_all = normed_all.reshape(fs * tok, dim)
    xp_w = jnp.pad(w_ssm_proj[:, :xdim], ((0, chan_p - chan), (0, 0)))
    dt_w = jnp.pad(w_ssm_proj[:, xdim:], ((0, chan_p - chan), (0, 0)))
    mo_w = jnp.pad(w_mamba_out, ((0, chan_p - chan), (0, 0)))
    vec = pad_last(lax.dynamic_slice_in_dim(ssm_vec, fi * chan, chan, 1), chan_p)

    normed_rows = normed_all.reshape(fs, tok, dim)
    qkv_parts = jnp.einsum("ftd,dc->fct", normed_rows, qkv_w, preferred_element_type=f32)
    meta_part = jnp.broadcast_to(
        dense(meta_low, qkv_w).astype(bf16)[None], (fs, metas, qkv_w.shape[1])
    )
    qkv_got, meta_got = exchange(
        1, [(qkv_parts.astype(bf16), EACH, FSDP), (meta_part, EACH, FSDP)]
    )
    qkv_own = qkv_got.reshape(heads_dim + 2 * kv_dim, tok)
    queries = qkv_own[:heads_dim]
    keyval = qkv_own[heads_dim:]
    meta_own = jnp.concatenate([meta_got[j] for j in range(fs)], axis=1)[:, heads_dim:]
    kv_before, meta_kv, gu_0 = exchange(
        2,
        [
            (keyval, NEXT, CTX),
            (meta_own, ALL, CTX),
            (gu_send, (HALF, 0, 1), WEIGHTS),
        ],
        reach=reach,
    )
    kv_before = jnp.where(
        (ci - 1 - jnp.arange(reach) >= 0)[:, None, None], kv_before, jnp.zeros_like(kv_before)
    )
    key_rows = jnp.concatenate(
        [meta_kv.reshape(META, 2 * kv_dim).T]
        + [kv_before[d - 1] for d in range(reach, 0, -1)]
        + [keyval],
        axis=1,
    )

    mamba_in = dense(normed_all, mi_w).reshape(fs, tok, 2 * chan_p)
    inner_pre = mamba_in[:, :, :chan_p]
    gate_z = mamba_in[:, :, chan_p:]
    up_ring = [(c, c + 1) for c in range(cs - 1)]
    down_ring = [(c + 1, c) for c in range(cs - 1)]
    tail_rows = lax.ppermute(inner_pre[:, tok - (CONV - 1) :], CTX, up_ring)
    extended = jnp.concatenate([tail_rows, inner_pre], axis=1)
    seg_ext = lax.dynamic_slice_in_dim(
        jnp.concatenate([jnp.full((fs, CONV - 1), -1, jnp.int32), seg_all], axis=1),
        ci * tok,
        tok + CONV - 1,
        1,
    )
    own_seg = seg_ext[:, CONV - 1 :]
    same_seg = [seg_ext[:, o : o + tok] == own_seg for o in range(CONV)]
    starts = own_seg != seg_ext[:, CONV - 2 : -1]
    inner_x, conv_pull = jax.vjp(
        lambda ext_rows, taps: conv_silu(ext_rows, taps, same_seg), extended, vec[:CONV]
    )
    inner_low = inner_x.astype(bf16).reshape(fs * tok, chan_p)
    xproj_part = lax.dot_general(
        xp_w, inner_low, (((0,), (1,)), ((), ())), preferred_element_type=f32
    )
    xproj_got, attn_old, ssm_proj_old = exchange(
        3,
        [
            (xproj_part, GATHER, FSDP),
            (row_block(w_attn_out), CROSS, BOTH),
            (row_block(w_ssm_proj), CROSS, BOTH),
        ],
    )
    xproj = jnp.sum(xproj_got, axis=0).T
    delta_low = xproj[:, :DTR].astype(bf16)
    pre_delta = dense_nt(delta_low, dt_w).reshape(fs, tok, chan_p) + vec[CONV]
    step = jax.nn.softplus(pre_delta)
    step_far = jnp.where(starts[:, :, None], FAR, step)
    drive = step * inner_x

    def spread(columns):
        return jnp.broadcast_to(columns.reshape(fs, tok, DS, 1), (fs, tok, DS, 128))

    b_wide = spread(xproj[:, DTR : DTR + DS])
    c_wide = spread(xproj[:, DTR + DS : xdim])
    rate = -jnp.exp(vec[CONV + 2 :])
    rate2 = rate * LOG2E
    sizes = (fs, tok, chan_p)
    last_state, mamba_out_old = scan_call(
        scan_tail_body,
        (step_far, drive, b_wide, rate2),
        (SEQ, SEQ, SPREAD, RATE),
        (STATE,),
        *sizes,
        cid=19,
        plan=Traffic([(row_block(w_mamba_out), CROSS, BOTH)]),
    )
    step_sum = jnp.sum(step_far, axis=1)
    state_before, sums, gu_2 = exchange(
        4,
        [
            (last_state.astype(bf16), NEXT, CTX),
            (step_sum, ALL, CTX),
            (gu_send, (HALF, 2, 4), WEIGHTS),
        ],
        reach=reach,
    )

    def decay_of(block):
        total = lax.dynamic_index_in_dim(sums, jnp.clip(block, 0, cs - 1), 0, keepdims=False)
        return jnp.exp2(total[:, None, :] * rate2)

    entry = jnp.zeros((fs, DS, chan_p), f32)
    for d in range(reach, 0, -1):
        there = jnp.where(ci >= d, state_before[d - 1].astype(f32), 0.0)
        entry = decay_of(ci - d) * entry + there
    readout, hist, ffn_down_old = scan_call(
        scan_full_body,
        (step_far, drive, b_wide, c_wide, rate2, entry),
        (SEQ, SEQ, SPREAD, SPREAD, RATE, STATE),
        (SEQ, HIST),
        *sizes,
        cid=20,
        plan=Traffic([(row_block(w_ffn_down), CROSS, BOTH)]),
    )
    skip = vec[CONV + 1]
    pre_mix = readout + skip * inner_x
    gate_s = jax.nn.sigmoid(gate_z)
    gate_silu = gate_z * gate_s
    mixture_low = (pre_mix * gate_silu).astype(bf16).reshape(fs * tok, chan_p)
    ssm_part = dense(mixture_low, mo_w).astype(bf16).reshape(fs, tok, dim)

    key_span = (reach + 1) * tok
    padded_seg = jnp.concatenate([jnp.full((reach * tok,), -1, jnp.int32), seg_row])
    key_seg = lax.dynamic_slice_in_dim(padded_seg, ci * tok, key_span, 0)
    query_seg = lax.dynamic_slice_in_dim(seg_row, ci * tok, tok, 0)
    query_pos = jnp.arange(tok, dtype=jnp.int32) + reach * tok
    key_pos = jnp.arange(key_span, dtype=jnp.int32)
    allowed = (
        (key_seg[:, None] == query_seg[None, :])
        & (key_pos[:, None] <= query_pos[None, :])
        & (query_pos[None, :] - key_pos[:, None] < WINDOW)
    )
    allowed = jnp.concatenate([jnp.ones((META, tok), jnp.bool_), allowed], axis=0)
    bias = jnp.where(allowed, 0.0, -1e30)
    seen = META + key_span
    q_spec = pl.BlockSpec((groups * HD, tok), lambda g: (g, 0))
    k_spec = pl.BlockSpec((HD, seen), lambda g: (g, 0))
    v_spec = pl.BlockSpec((HD, seen), lambda g: (g + KVH, 0))
    bias_spec = pl.BlockSpec((seen, tok), lambda g: (0, 0))
    total_spec = pl.BlockSpec((1, groups, tok), lambda g: (g, 0, 0))
    attended, log_totals, gu_1 = hosted_call(
        functools.partial(attend_body, groups),
        (KVH,),
        [q_spec, k_spec, v_spec, bias_spec],
        [q_spec, total_spec],
        [
            jax.ShapeDtypeStruct((heads_dim, tok), bf16),
            jax.ShapeDtypeStruct((KVH, groups, tok), f32),
        ],
        (queries, key_rows, key_rows, bias),
        16,
        Traffic([(gu_send, (HALF, 1, 2), WEIGHTS)]),
        12 * MIB,
    )
    wide = heads_dim // fs
    att_got, gu_3 = exchange(
        5,
        [
            (attended.reshape(fs, wide, tok), EACH, FSDP),
            (gu_send, (HALF, 4, 5), WEIGHTS),
        ],
    )
    gu_w = jnp.concatenate([gu_0, gu_1, gu_2, gu_3], axis=2).reshape(dim, 2 * ffw_p)
    att_tp = jnp.swapaxes(att_got, 1, 2).reshape(fs * tok, wide)
    attn_part = dense(att_tp, w_attn_out).astype(bf16).reshape(fs, tok, dim)
    attn_got, ssm_got = exchange(
        6, [(attn_part, REDUCE, FSDP), (ssm_part, REDUCE, FSDP)]
    )
    attn_proj = jnp.sum(attn_got.astype(f32), axis=0)
    ssm_proj = jnp.sum(ssm_got.astype(f32), axis=0)
    attn_branch, attn_pull = jax.vjp(rms_norm, attn_proj, gain_rows[1])
    ssm_branch, ssm_norm_pull = jax.vjp(rms_norm, ssm_proj, gain_rows[2])
    residual = source + 0.5 * (attn_branch + ssm_branch)
    ffn_in_f, ffn_norm_pull = jax.vjp(rms_norm, residual, gain_rows[3])
    ffn_in, cot_all = exchange(
        7, [(ffn_in_f.astype(bf16), GATHER, FSDP), (cotangent[0], GATHER, FSDP)]
    )
    cot_all = cot_all.reshape(fs * tok, dim)
    ffn_in = ffn_in.reshape(fs * tok, dim)

    gate_up = dense(ffn_in, gu_w)
    hidden_f, glu_pull = jax.vjp(
        lambda values: jax.nn.silu(values[:, :ffw_p]) * values[:, ffw_p:], gate_up
    )
    hidden = hidden_f.astype(bf16)[:, :ffw]
    down_part = dense(hidden, w_ffn_down).astype(bf16).reshape(fs, tok, dim)
    hidden_grad = pad_last(dense_nt(cot_all, w_ffn_down), ffw_p)
    gate_up_grad = glu_pull(hidden_grad)[0].astype(bf16)
    ring_one = Ring(
        [
            row_chunks(ffn_in, gate_up_grad[:, :ffw_p]),
            row_chunks(ffn_in, gate_up_grad[:, ffw_p:]),
            column_chunks(hidden, cot_all, 2),
        ],
        [(0, 0, 1), (1, 0, -1), (2, 0, 1), (2, 1, -1)],
    )
    hops = spread_hops([1, 1, 1, 1, 2, 1])
    ffn_back = dense_nt(gate_up_grad, gu_w).astype(bf16).reshape(fs, tok, dim)
    (back_got,) = exchange(8, [(ffn_back, REDUCE, FSDP)], ring_one, hops[0])
    resid_part, gain_ffn_grad = ffn_norm_pull(jnp.sum(back_got.astype(f32), axis=0))
    residual_grad = cotangent[0].astype(f32) + resid_part
    branch_grad = 0.5 * residual_grad
    attn_proj_grad, gain_attn_grad = attn_pull(branch_grad)
    ssm_proj_grad, gain_ssm_grad = ssm_norm_pull(branch_grad)
    branch_low = (attn_proj_grad.astype(bf16), ssm_proj_grad.astype(bf16))
    attn_proj_low, ssm_proj_low = exchange(
        9,
        [(branch_low[0], GATHER, FSDP), (branch_low[1], GATHER, FSDP)],
        ring_one,
        hops[1],
    )
    attn_proj_low = attn_proj_low.reshape(fs * tok, dim)
    ssm_proj_low = ssm_proj_low.reshape(fs * tok, dim)
    att_grad_tp = jnp.einsum(
        "ftd,cd->fct",
        attn_proj_low.reshape(fs, tok, dim),
        w_attn_out,
        preferred_element_type=f32,
    ).astype(bf16)
    (att_grad_got,) = exchange(10, [(att_grad_tp, EACH, FSDP)], ring_one, hops[2])

    def own_pair(held, part):
        piece = lax.dynamic_slice_in_dim(held, ci * (dim // cs), dim // cs, 0)
        return jnp.stack([piece[:, :part], piece[:, part:]])

    qkv_old = lax.dynamic_slice_in_dim(qkv_w, ci * (dim // cs), dim // cs, 0)
    attended_grad = att_grad_got.reshape(heads_dim, tok)

    query_grad, key_grad, value_grad, mamba_in_old = hosted_call(
        functools.partial(attend_back_body, groups),
        (KVH,),
        [q_spec, k_spec, v_spec, bias_spec, total_spec, q_spec],
        [q_spec, k_spec, k_spec],
        [
            jax.ShapeDtypeStruct((heads_dim, tok), bf16),
            jax.ShapeDtypeStruct((kv_dim, seen), f32),
            jax.ShapeDtypeStruct((kv_dim, seen), f32),
        ],
        (queries, key_rows, key_rows, bias, log_totals, attended_grad),
        24,
        Traffic([(own_pair(mi_w, chan_p), PAIR, FSDP)], ring_one, hops[3]),
        16 * MIB,
    )
    kv_grad_all = jnp.concatenate([key_grad, value_grad], axis=0)
    kv_send = jnp.stack(
        [
            kv_grad_all[:, META + (reach - d) * tok : META + (reach - d + 1) * tok]
            for d in range(1, reach + 1)
        ]
    ).astype(bf16)
    meta_send = kv_grad_all[:, :META].T.astype(bf16).reshape(cs, metas, 2 * kv_dim)
    kv_back, meta_back, down_got = exchange(
        13,
        [
            (kv_send, BACK, CTX),
            (meta_send, EACH, CTX),
            (down_part, REDUCE, FSDP),
        ],
        ring_one,
        hops[4],
        reach,
    )
    output = residual + jnp.sum(down_got.astype(f32), axis=0)
    own_kv_grad = kv_grad_all[:, META + reach * tok :]
    for d in range(1, reach + 1):
        own_kv_grad = own_kv_grad + jnp.where(ci + d < cs, kv_back[d - 1].astype(f32), 0.0)
    meta_kv_grad = jnp.sum(meta_back.astype(f32), axis=0).astype(bf16)
    meta_grad_parts = column_parts(
        jnp.pad(meta_kv_grad, ((0, 0), (heads_dim, 0))), 1, fs, qkv_w.shape[1]
    )
    qkv_grad = jnp.concatenate([query_grad, own_kv_grad.astype(bf16)], axis=0)
    qkv_grad_tp, meta_grad_tp = exchange(
        14,
        [
            (qkv_grad.reshape(fs, -1, tok), EACH, FSDP),
            (meta_grad_parts, EACH, FSDP),
        ],
        ring_one,
        hops[5],
    )

    mixture_grad = dense_nt(ssm_proj_low, mo_w).reshape(fs, tok, chan_p)
    read_grad = mixture_grad * gate_silu
    gate_grad = mixture_grad * pre_mix * (gate_s * (1.0 + gate_z * (1.0 - gate_s)))
    gate_low = gate_grad.astype(bf16).reshape(fs * tok, chan_p)
    qkv_full = jnp.einsum("ftd,fct->dc", normed_rows, qkv_grad_tp, preferred_element_type=f32)
    qkv_full = qkv_full + jnp.einsum(
        "md,fmc->dc", meta_low, meta_grad_tp, preferred_element_type=f32
    )
    ring_two = Ring(
        [
            row_chunks(normed_all, gate_low),
            qkv_full.astype(bf16).reshape(cs, 1, dim // cs, qkv_w.shape[1]),
            column_chunks(att_tp, attn_proj_low),
            column_chunks(mixture_low[:, :chan], ssm_proj_low, 2),
        ],
        [(0, 0, 1), (1, 0, -1), (2, 0, -1), (3, 0, 1), (3, 1, -1)],
    )
    hops = spread_hops([1, 2, 2, 2])
    gate_sum, up_sum, down_top, down_low = ring_one.finish()
    first_adj, gate_up_old = scan_call(
        adjoint_head_body,
        (step_far, read_grad, c_wide, rate2),
        (SEQ, SEQ, SPREAD, RATE),
        (STATE,),
        *sizes,
        cid=21,
        plan=Traffic([(own_pair(gu_w, ffw_p), PAIR, FSDP)], ring_two, hops[0]),
    )
    adj_after, gate_up_sum = exchange(
        11,
        [
            (first_adj.astype(bf16), PREV, CTX),
            (jnp.stack([gate_sum, up_sum]).astype(bf16), PAIR, FSDP),
        ],
        ring_two,
        hops[1],
        reach,
    )
    gate_up_old = unpaired(gate_up_old, ffw)
    mamba_in_old = unpaired(mamba_in_old, chan)
    later = jnp.zeros((fs, DS, chan_p), f32)
    for d in range(reach, 0, -1):
        there = jnp.where(ci + d < cs, adj_after[d - 1].astype(f32), 0.0)
        later = decay_of(ci + d) * later + there
    drive_grad, exp_grad, b_acc, c_acc, rate_grad = scan_call(
        adjoint_full_body,
        (step_far, drive, read_grad, b_wide, c_wide, rate2, hist, later),
        (SEQ, SEQ, SEQ, SPREAD, SPREAD, RATE, HIST, STATE),
        (SEQ, SEQ, SPREAD, SPREAD, DRATE),
        *sizes,
        cid=22,
        plan=Traffic([], ring_two, hops[2]),
        later=(3,) if hops[2] == 2 else (),
    )
    cross = [
        (f * cs + c, (c // halves) * cs + halves * f + c % halves)
        for f in range(fs)
        for c in range(cs)
    ]
    down_both = jnp.concatenate([down_top, down_low], axis=0).astype(bf16)
    drive_grad, down_both = together(drive_grad, down_both)
    down_sum = lax.ppermute(down_both, (FSDP, CTX), cross)
    step_grad = drive_grad * inner_x + exp_grad * LN2
    pre_delta_grad = step_grad * jax.nn.sigmoid(pre_delta)
    inner_grad = drive_grad * step + skip * read_grad
    small_grad = jnp.concatenate(
        [
            jnp.sum(pre_delta_grad, axis=(0, 1))[None],
            jnp.sum(inner_x * read_grad, axis=(0, 1))[None],
            jnp.sum(rate_grad, axis=0) * rate,
        ],
        axis=0,
    )
    pre_delta_low = pre_delta_grad.astype(bf16).reshape(fs * tok, chan_p)
    xgrad_part = jnp.concatenate(
        [
            lax.dot_general(
                dt_w, pre_delta_low, (((0,), (1,)), ((), ())), preferred_element_type=f32
            ),
            jnp.sum(b_acc, axis=-1).reshape(fs * tok, DS).T,
            jnp.sum(c_acc, axis=-1).reshape(fs * tok, DS).T,
        ],
        axis=0,
    )
    (xgrad_got,) = exchange(12, [(xgrad_part, GATHER, FSDP)], ring_two, hops[3])
    xproj_grad = jnp.sum(xgrad_got, axis=0).T.astype(bf16)
    inner_grad = inner_grad + dense_nt(xproj_grad, xp_w).reshape(fs, tok, chan_p)
    ext_grad, taps_grad = conv_pull(inner_grad)
    returned = lax.ppermute(ext_grad[:, : CONV - 1].astype(bf16), CTX, down_ring).astype(f32)
    inner_pre_grad = ext_grad[:, CONV - 1 :] + jnp.pad(
        returned, ((0, 0), (tok - (CONV - 1), 0), (0, 0))
    )
    inner_pre_low = inner_pre_grad.astype(bf16).reshape(fs * tok, chan_p)
    mamba_in_grad = jnp.concatenate([inner_pre_low, gate_low], axis=1)
    split = ceil_to(chan_p * 9 // 16, 128)
    ring_three = Ring(
        [
            row_chunks(normed_all, inner_pre_low[:, :split]),
            row_chunks(normed_all, inner_pre_low[:, split:]),
            column_chunks(
                jnp.concatenate([inner_low[:, :chan], pre_delta_low[:, :chan]], axis=0),
                jnp.concatenate(
                    [
                        jnp.pad(xproj_grad, ((0, 0), (0, DTR))),
                        jnp.pad(delta_low, ((0, 0), (xdim, 0))),
                    ],
                    axis=0,
                ),
            ),
        ],
        [(0, 0, 1), (1, 0, -1), (2, 0, -1)],
    )
    vec_grad = jnp.concatenate([taps_grad, small_grad], axis=0)
    token_back = jnp.einsum("fct,dc->ftd", qkv_grad_tp, qkv_w, preferred_element_type=f32)
    token_back = token_back + dense_nt(mamba_in_grad, mi_w).reshape(fs, tok, dim)
    meta_back_rows = jnp.einsum("fmc,dc->fmd", meta_grad_tp, qkv_w, preferred_element_type=f32)
    normed_back = jnp.concatenate([token_back.astype(bf16), meta_back_rows.astype(bf16)], axis=1)
    hops = spread_hops([3, 2, 2])
    (normed_got,) = exchange(15, [(normed_back, REDUCE, FSDP)], ring_three, hops[0])
    normed_grad = jnp.sum(normed_got.astype(f32), axis=0)
    source_part, gain_in_grad = norm_pull(normed_grad[:tok])
    source_grad = residual_grad + source_part
    meta_grad, gain_in_meta = meta_pull(normed_grad[tok:])
    embed_part = jnp.concatenate(
        [
            meta_grad,
            jnp.stack([gain_in_grad + gain_in_meta, gain_attn_grad, gain_ssm_grad, gain_ffn_grad]),
        ],
        axis=0,
    )
    (embed_rows,) = exchange(17, [(embed_part, GATHER, FSDP)], ring_three, hops[1])
    embed_got, vec_got = exchange(
        18,
        [
            (jnp.sum(embed_rows, axis=0).astype(bf16), LINE, CTX),
            (vec_grad.astype(bf16), LINE, CTX),
        ],
        ring_three,
        hops[2],
    )
    embed_got = embed_got.astype(f32)
    vec_part = jnp.sum(vec_got.astype(f32), axis=0)
    embed_total = jnp.concatenate(
        [embed_got[:, :metas].reshape(META, dim), jnp.sum(embed_got[:, metas:], axis=0)], axis=0
    )
    gate_half, qkv_gradient, attn_sum, out_top, out_low = ring_two.finish()
    inner_a, inner_b, proj_sum = ring_three.finish()
    mamba_in_sum, attn_sum, mamba_out_sum, proj_sum, vec_all = exchange(
        23,
        [
            (
                jnp.stack([jnp.concatenate([inner_a, inner_b], axis=1), gate_half]).astype(bf16),
                PAIR,
                FSDP,
            ),
            (attn_sum.astype(bf16), CROSS, BOTH),
            (jnp.concatenate([out_top, out_low], axis=0).astype(bf16), CROSS, BOTH),
            (proj_sum.astype(bf16), CROSS, BOTH),
            (vec_part, GATHER, FSDP),
        ],
    )
    ssm_total = jnp.concatenate([vec_all[j, :, :chan] for j in range(fs)], axis=1)
    gate_up_gradient = unpaired(gate_up_sum, ffw)
    mamba_in_gradient = unpaired(mamba_in_sum, chan)
    ffn_down_gradient = down_sum.astype(f32)
    attn_gradient = attn_sum.astype(f32)
    mamba_out_gradient = mamba_out_sum.astype(f32)
    ssm_proj_gradient = proj_sum.astype(f32)

    def adam_block(gradient, moments_old, weight):
        return adam_step(gradient, moments_old, weight.astype(f32))

    qkv_moments, qkv_update = adam_block(qkv_gradient, m_qkv, qkv_old)
    attn_moments, attn_update = adam_block(attn_gradient, m_attn_out, attn_old)
    mamba_in_moments, mamba_in_update = adam_block(mamba_in_gradient, m_mamba_in, mamba_in_old)
    ssm_proj_moments, ssm_proj_update = adam_block(ssm_proj_gradient, m_ssm_proj, ssm_proj_old)
    mamba_out_moments, mamba_out_update = adam_block(
        mamba_out_gradient, m_mamba_out, mamba_out_old
    )
    gate_up_moments, gate_up_update = adam_block(gate_up_gradient, m_gate_up, gate_up_old)
    ffn_down_moments, ffn_down_update = adam_block(ffn_down_gradient, m_ffn_down, ffn_down_old)
    ssm_vec_moments, ssm_vec_update = adam_step(ssm_total, m_ssm_vec, ssm_vec)
    embed_moments, embed_update = adam_step(embed_total, m_embed_small, embed_small)
    return (
        output.astype(jnp.bfloat16)[None],
        source_grad[None],
        qkv_gradient,
        qkv_moments,
        qkv_update,
        attn_gradient,
        attn_moments,
        attn_update,
        mamba_in_gradient,
        mamba_in_moments,
        mamba_in_update,
        ssm_proj_gradient,
        ssm_proj_moments,
        ssm_proj_update,
        mamba_out_gradient,
        mamba_out_moments,
        mamba_out_update,
        gate_up_gradient,
        gate_up_moments,
        gate_up_update,
        ffn_down_gradient,
        ffn_down_moments,
        ffn_down_update,
        ssm_total,
        ssm_vec_moments,
        ssm_vec_update,
        embed_total,
        embed_moments,
        embed_update,
    )


def solution(mesh):
    in_specs = (
        P(FSDP, CTX, None),
        P(FSDP, CTX, None),
        P(FSDP, None),
        P(FSDP, None),
        P(None, CTX, FSDP),
        P(FSDP, None),
        P(None, CTX, FSDP),
        P(FSDP, None),
        P(None, CTX, FSDP),
        P(FSDP, None),
        P(None, CTX, FSDP),
        P(FSDP, None),
        P(None, CTX, FSDP),
        P(FSDP, None),
        P(None, CTX, FSDP),
        P(FSDP, None),
        P(None, CTX, FSDP),
        P(),
        P(),
        P(),
        P(),
    )
    out_specs = (
        P(FSDP, CTX, None),
        P(FSDP, CTX, None),
        P(CTX, FSDP),
        P(CTX, FSDP),
        P(CTX, FSDP),
        P(CTX, FSDP),
        P(CTX, FSDP),
        P(CTX, FSDP),
        P(CTX, FSDP),
        P(CTX, FSDP),
        P(CTX, FSDP),
        P(CTX, FSDP),
        P(CTX, FSDP),
        P(CTX, FSDP),
        P(CTX, FSDP),
        P(CTX, FSDP),
        P(CTX, FSDP),
        P(CTX, FSDP),
        P(CTX, FSDP),
        P(CTX, FSDP),
        P(CTX, FSDP),
        P(CTX, FSDP),
        P(CTX, FSDP),
        P(),
        P(),
        P(),
        P(),
        P(),
        P(),
    )
    return jax.shard_map(shards, mesh=mesh, in_specs=in_specs, out_specs=out_specs, check_vma=False)
```

```python
import functools

import jax
import jax.numpy as jnp
from jax import lax
from jax.experimental import pallas as pl
from jax.experimental.pallas import tpu as pltpu
from jax.sharding import PartitionSpec as P

NH = 25
KVH = 5
HD = 64
DI = 3200
DS = 16
DTR = 100
FF = 5504
META = 128
CONV = 4
WINDOW = 1024

norm_eps = 1e-05
beta_one = 0.9
beta_two = 0.95
learn_rate = 0.01
decay_rate = 0.1
adam_eps = 1e-08
adam_count = 10.0

FSDP = "fsdp"
CTX = "ctx"
EACH = "each"
ALL = "all"
GATHER = "gather"
REDUCE = "reduce"
HALF = "half"
WEIGHTS = "weights"
BOTH = "both"
CROSS = "cross"
PAIR = "pair"
NEXT = "next"
PREV = "prev"
BACK = "back"
LINE = "line"
SEQ = "seq"
SPREAD = "spread"
HIST = "hist"
STATE = "state"
RATE = "rate"
DRATE = "drate"
RING = "ring"
LOG2E = 1.4426950408889634
LN2 = 0.6931471805599453
FAR = 1e30
bf16 = jnp.bfloat16
f32 = jnp.float32
ANY = pl.BlockSpec(memory_space=pltpu.HBM)
MIB = 1024 * 1024


def together(*values):
    return lax.optimization_barrier(values)


def ceil_to(value, unit):
    return (value + unit - 1) // unit * unit


def span_of(axis):
    return lax.axis_size(axis), lax.axis_index(axis)


def ring_spot(ci, cs):
    odd = lax.rem(ci, 2)
    return (ci // 2) * (1 - odd) + (cs - 1 - ci // 2) * odd


def ring_block(spot, cs):
    spot = lax.rem(spot + 2 * cs, cs)
    far = spot // (cs // 2)
    return 2 * spot * (1 - far) + (2 * (cs - 1 - spot) + 1) * far


def when(condition, action):
    if condition is None:
        action()
    else:
        pl.when(condition)(action)


def in_hbm(value):
    return pltpu.with_memory_space_constraint(value, pltpu.HBM)


def piece_edges(mode):
    count = mode[2] - mode[1]
    groups = 5 if count > 10 else 3
    edges = [count * k // groups for k in range(groups + 1)]
    return list(zip(edges[:-1], edges[1:]))


def chunk_shape(value, cs):
    lead, _, rows, cols = value.shape
    return (rows, cols if lead == cs else cols * lead // cs)


def chunk_ref(ref, block, part, cs):
    lead = ref.shape[0]
    if lead == cs:
        return ref.at[block, part]
    cols = ref.shape[3] * lead // cs
    columns = pl.ds(pl.multiple_of(block // lead * cols, 128), cols)
    return ref.at[lax.rem(block, lead), part, :, columns]


class Ring:
    def __init__(self, chunks, uses):
        self.chunks, self.uses = chunks, uses
        self.got, self.hop = [], 0

    def finish(self):
        cs, block = span_of(CTX)
        sums = []
        for (k, part, _), got in zip(self.uses, self.got):
            value = self.chunks[k]
            if value.shape[0] == cs:
                own = lax.dynamic_index_in_dim(value, block, 0, keepdims=False)[part]
            else:
                rows, cols = chunk_shape(value, cs)
                at = (block % value.shape[0], part, 0, block // value.shape[0] * cols)
                own = lax.dynamic_slice(value, at, (1, 1, rows, cols))[0, 0]
            sums.append(got.astype(f32) + own.astype(f32))
        return sums


class Traffic:
    def __init__(self, items, ring=None, hops=0, reach=0):
        self.items, self.ring, self.reach = items, ring, reach
        fs, cs = lax.axis_size(FSDP), lax.axis_size(CTX)
        self.hops = min(hops, cs - 1 - ring.hop) if ring is not None else 0
        self.ins = [value for value, _, _ in items]
        self.outs = []
        dma = pltpu.SemaphoreType.DMA
        most = 2 * max(fs, cs)
        count = max(len(items), 1)
        self.scratch = [dma((count, most)), dma((count, most)), dma((count, 2))]
        self.places = {}

        def own_scratch(k, shapes):
            self.places[k] = len(self.scratch)
            self.scratch += shapes

        for k, (value, mode, axis) in enumerate(items):
            shape = value.shape
            if mode in (ALL, GATHER, LINE):
                shape = (lax.axis_size(axis),) + shape
            elif mode in (NEXT, PREV):
                shape = (reach,) + shape
            elif mode == REDUCE:
                shape = (fs // 2,) + shape[1:]
                own_scratch(k, [pltpu.VMEM(shape, value.dtype)] * 2 + [dma((fs // 2,))])
            elif mode[0] == HALF:
                pieces = len(piece_edges(mode))
                shape = shape[:2] + (mode[2] - mode[1],) + shape[3:]
                own_scratch(k, [dma((pieces, 2 * fs)), dma((pieces, 2 * fs))])
            self.outs.append(jax.ShapeDtypeStruct(shape, value.dtype))
        if self.hops:
            self.ins += [in_hbm(value) for value in ring.chunks + ring.got]
            uses = len(ring.uses)
            shapes = [dma((uses, self.hops)), dma((uses, self.hops)), dma((uses, self.hops, 2))]
            for k, _, _ in ring.uses:
                shape = chunk_shape(ring.chunks[k], cs)
                self.outs += [pltpu.HBM(shape, bf16)] * self.hops
                shapes.append(pltpu.VMEM((self.hops, 2) + shape, bf16))
            own_scratch(RING, shapes)

    def vmem(self):
        total = 4 * MIB
        for held in self.scratch:
            if held.memory_space == pltpu.VMEM:
                size = 2
                for extent in held.shape[:-2]:
                    size *= extent
                total += size * ceil_to(held.shape[-2], 16) * ceil_to(held.shape[-1], 128)
        return total

    def bind(self, ins, outs, scratch):
        self.in_refs, self.out_refs, self.sems = ins, outs, scratch

    def remote(self, source, target, send, take, peer):
        return pltpu.make_async_remote_copy(
            src_ref=source,
            dst_ref=target,
            send_sem=send,
            recv_sem=take,
            device_id=peer,
            device_id_type=pl.DeviceIdType.MESH,
        )

    def greet(self):
        barrier = pltpu.get_barrier_semaphore()
        fs, fi = span_of(FSDP)
        cs, ci = span_of(CTX)

        def signal(peer):
            pl.semaphore_signal(
                barrier, inc=1, device_id=peer, device_id_type=pl.DeviceIdType.MESH
            )

        axes = {axis for _, _, axis in self.items}
        if WEIGHTS in axes:
            axes.add(FSDP)
        total = 0
        for axis in (FSDP, CTX):
            if axis in axes:
                n, me = span_of(axis)
                for d in range(1, n):
                    signal({axis: lax.rem(me + d, n)})
                total += n - 1
        if self.hops and CTX not in axes:
            spot = ring_spot(ci, cs)
            signal({CTX: ring_block(spot + 1, cs)})
            signal({CTX: ring_block(spot - 1, cs)})
            total += 2
        if WEIGHTS in axes and CTX not in axes:
            signal({CTX: ci + 1 - 2 * lax.rem(ci, 2)})
            total += 1
        if BOTH in axes:
            halves = cs // fs
            away = ci // halves != fi

            def meet():
                signal({FSDP: ci // halves, CTX: halves * fi + lax.rem(ci, halves)})

            pl.when(away)(meet)
            if total:
                pl.semaphore_wait(barrier, total + jnp.where(away, 1, 0))
            else:
                pl.when(away)(lambda: pl.semaphore_wait(barrier, 1))
        else:
            pl.semaphore_wait(barrier, total)

    def copies(self):
        starts, relays, waits = [], [], []
        fs, fi = span_of(FSDP)
        cs, ci = span_of(CTX)
        send_sem, take_sem, own_sem = self.sems[:3]
        for k, (_, mode, axis) in enumerate(self.items):
            src, dst = self.in_refs[k], self.out_refs[k]

            def add(copy, sends=None, takes=None):
                starts.append((copy.start, sends))
                waits.append((copy.wait_send, sends))
                waits.append((copy.wait_recv, takes))

            def keep(copy, condition=None):
                starts.append((copy.start, condition))
                waits.append((copy.wait, condition))

            core, chip, chips = lax.rem(fi, 2), fi // 2, fs // 2
            mate = {FSDP: fi + 1 - 2 * core}

            def relay(first, second):
                starts.append((first.start, None))
                relays.append((first.wait_recv, None))
                relays.append((second.start, None))
                waits.append((first.wait_send, None))
                waits.append((second.wait_send, None))
                waits.append((second.wait_recv, None))

            if mode == GATHER:
                for d in range(1, chips):
                    to = 2 * lax.rem(chip + d, chips) + core
                    came = 2 * lax.rem(chip + chips - d, chips) + core
                    relay(
                        self.remote(
                            src, dst.at[fi], send_sem.at[k, d], take_sem.at[k, d], {FSDP: to}
                        ),
                        self.remote(
                            dst.at[came],
                            dst.at[came],
                            send_sem.at[k, chips + d],
                            take_sem.at[k, chips + d],
                            mate,
                        ),
                    )
                add(self.remote(src, dst.at[fi], send_sem.at[k, 0], take_sem.at[k, 0], mate))
                keep(pltpu.make_async_copy(src, dst.at[fi], own_sem.at[k, 0]))
            elif mode == LINE:
                across = {CTX: ci + 1 - 2 * lax.rem(ci, 2)}
                for d in range(1, cs // 2):
                    came = lax.rem(ci + cs - 2 * d, cs)
                    relay(
                        self.remote(
                            src,
                            dst.at[ci],
                            send_sem.at[k, d],
                            take_sem.at[k, d],
                            {CTX: lax.rem(ci + 2 * d, cs)},
                        ),
                        self.remote(
                            dst.at[came],
                            dst.at[came],
                            send_sem.at[k, cs // 2 + d],
                            take_sem.at[k, cs // 2 + d],
                            across,
                        ),
                    )
                add(self.remote(src, dst.at[ci], send_sem.at[k, 0], take_sem.at[k, 0], across))
                keep(pltpu.make_async_copy(src, dst.at[ci], own_sem.at[k, 0]))
            elif mode == REDUCE:
                mine, other, load_sem = self.sems[self.places[k] : self.places[k] + 3]
                for d in list(range(1, chips)) + [0]:
                    to = lax.rem(chip + d, chips)
                    first = self.remote(
                        src.at[2 * to + 1 - core],
                        other.at[to],
                        send_sem.at[k, d],
                        take_sem.at[k, d],
                        mate,
                    )
                    load = pltpu.make_async_copy(
                        src.at[2 * to + core], mine.at[to], load_sem.at[d]
                    )
                    starts.append((first.start, None))
                    starts.append((load.start, None))
                    relays.append((load.wait, None))
                    relays.append((first.wait_recv, None))
                    waits.append((first.wait_send, None))

                    def total(mine=mine, other=other, to=to):
                        mine[to] = mine[to] + other[to]

                    relays.append((total, None))
                    if d:
                        second = self.remote(
                            mine.at[to],
                            dst.at[chip],
                            send_sem.at[k, chips + d],
                            take_sem.at[k, chips + d],
                            {FSDP: 2 * to + core},
                        )
                        waits.append((second.wait_send, None))
                        waits.append((second.wait_recv, None))
                    else:
                        second = pltpu.make_async_copy(mine.at[to], dst.at[to], own_sem.at[k, 0])
                        waits.append((second.wait, None))
                    relays.append((second.start, None))
            elif mode[0] == HALF:
                piece_send, piece_take = self.sems[self.places[k] : self.places[k] + 2]
                side = lax.rem(ci, 2)
                across = {CTX: ci + 1 - 2 * side}
                for q, (low, high) in enumerate(piece_edges(mode)):
                    for d in range(1, chips):
                        for b in range(2):
                            to = 2 * lax.rem(chip + d, chips) + lax.rem(core + b, 2)
                            came = 2 * lax.rem(chip + chips - d, chips) + lax.rem(core + b, 2)
                            e = 2 * d + b
                            relay(
                                self.remote(
                                    src.at[to, side, mode[1] + low : mode[1] + high],
                                    dst.at[fi, side, low:high],
                                    piece_send.at[q, e],
                                    piece_take.at[q, e],
                                    {FSDP: to},
                                ),
                                self.remote(
                                    dst.at[came, side, low:high],
                                    dst.at[came, side, low:high],
                                    piece_send.at[q, fs + e],
                                    piece_take.at[q, fs + e],
                                    across,
                                ),
                            )
                for b in range(2):
                    to = mate[FSDP]
                    add(
                        self.remote(
                            src.at[to, b, mode[1] : mode[2]],
                            dst.at[fi, b],
                            send_sem.at[k, b],
                            take_sem.at[k, b],
                            mate,
                        )
                    )
                    keep(
                        pltpu.make_async_copy(
                            src.at[fi, b, mode[1] : mode[2]], dst.at[fi, b], own_sem.at[k, b]
                        )
                    )
            elif mode in (ALL, EACH):
                n, me = span_of(axis)
                for d in range(1, n):
                    peer = lax.rem(me + d, n)
                    source = src.at[peer] if mode == EACH else src
                    add(
                        self.remote(
                            source, dst.at[me], send_sem.at[k, d], take_sem.at[k, d], {axis: peer}
                        )
                    )
                source = src.at[me] if mode == EACH else src
                keep(pltpu.make_async_copy(source, dst.at[me], own_sem.at[k, 0]))
            elif mode == PAIR:
                for p in range(2):
                    peer = (p * fs + fi) // 2
                    slot = lax.rem(fi, 2)
                    away = peer != fi
                    q = 2 * fi + p
                    comes = lax.rem(q, fs) != fi
                    copy = self.remote(
                        src.at[p],
                        dst.at[slot],
                        send_sem.at[k, p],
                        take_sem.at[k, slot],
                        {FSDP: peer},
                    )
                    starts.append((copy.start, away))
                    waits.append((copy.wait_send, away))
                    taken = self.remote(
                        src.at[p], dst.at[p], send_sem.at[k, p], take_sem.at[k, p], {FSDP: peer}
                    )
                    waits.append((taken.wait_recv, comes))
                    keep(
                        pltpu.make_async_copy(src.at[p], dst.at[slot], own_sem.at[k, p]),
                        peer == fi,
                    )
            elif mode == CROSS:
                halves = cs // fs
                away = ci // halves != fi
                peer = {FSDP: ci // halves, CTX: halves * fi + lax.rem(ci, halves)}
                add(self.remote(src, dst, send_sem.at[k, 0], take_sem.at[k, 0], peer), away, away)
                keep(pltpu.make_async_copy(src, dst, own_sem.at[k, 0]), ci // halves == fi)
            else:
                for d in range(1, self.reach + 1):
                    up = mode == NEXT
                    peer = ci + d if up else ci - d
                    source = src.at[d - 1] if mode == BACK else src
                    add(
                        self.remote(
                            source,
                            dst.at[d - 1],
                            send_sem.at[k, d],
                            take_sem.at[k, d],
                            {CTX: lax.rem(peer + cs, cs)},
                        ),
                        peer < cs if up else peer >= 0,
                        ci - d >= 0 if up else ci + d < cs,
                    )
        return starts, relays, waits

    def ring_refs(self, u):
        base = self.places[RING]
        outs = self.out_refs[len(self.items) + u * self.hops :]
        return self.sems[base], self.sems[base + 1], self.sems[base + 2], self.sems[base + 3 + u], outs

    def hop_copy(self, u, t):
        cs, ci = span_of(CTX)
        spot = ring_spot(ci, cs)
        k, part, way = self.ring.uses[u]
        send, take, _, buffer, outs = self.ring_refs(u)
        if self.ring.hop + t == 0:
            source = chunk_ref(
                self.in_refs[len(self.items) + k], ring_block(spot - way, cs), part, cs
            )
        else:
            source = buffer.at[t, 1]
        return self.remote(
            source, outs[t], send.at[u, t], take.at[u, t], {CTX: ring_block(spot + way, cs)}
        )

    def load_own(self, u, t):
        cs, ci = span_of(CTX)
        k, part, way = self.ring.uses[u]
        _, _, load, buffer, _ = self.ring_refs(u)
        block = ring_block(ring_spot(ci, cs) - way * (self.ring.hop + t + 1), cs)
        return pltpu.make_async_copy(
            chunk_ref(self.in_refs[len(self.items) + k], block, part, cs),
            buffer.at[t, 1],
            load.at[u, t, 1],
        )

    def load_got(self, u, t):
        _, _, load, buffer, outs = self.ring_refs(u)
        if t == 0:
            source = self.in_refs[len(self.items) + len(self.ring.chunks) + u]
        else:
            source = outs[t - 1]
        return pltpu.make_async_copy(source, buffer.at[t, 0], load.at[u, t, 0])

    def hop_step(self, t):
        uses = range(len(self.ring.uses))
        if self.ring.hop + t > 0:
            for u in uses:
                self.load_own(u, t).start()
                if t > 0:
                    self.hop_copy(u, t - 1).wait_recv()
                self.load_got(u, t).start()
        for u in uses:
            if self.ring.hop + t > 0:
                self.load_own(u, t).wait()
                self.load_got(u, t).wait()
                buffer = self.ring_refs(u)[3]
                buffer[t, 1] = buffer[t, 0] + buffer[t, 1]
            self.hop_copy(u, t).start()

    def begin(self):
        self.greet()
        for start, condition in self.copies()[0]:
            when(condition, start)
        if self.hops:
            self.hop_step(0)

    def end(self, hopped=1):
        _, relays, waits = self.copies()
        for step, condition in relays:
            when(condition, step)
        for t in range(hopped, self.hops):
            self.hop_step(t)
        for wait, condition in waits:
            when(condition, wait)
        for u in range(len(self.ring.uses) if self.hops else 0):
            for t in range(self.hops):
                self.hop_copy(u, t).wait_send()
            self.hop_copy(u, self.hops - 1).wait_recv()

    def take(self, results):
        count = len(self.items)
        if self.hops:
            last = count + self.hops - 1
            self.ring.got = [results[last + u * self.hops] for u in range(len(self.ring.uses))]
            self.ring.hop += self.hops
        return tuple(results[:count])


def exchange(cid, items, ring=None, hops=0, reach=0):
    plan = Traffic(items, ring, hops, reach)
    ins, outs = len(plan.ins), len(plan.outs)

    def body(*refs):
        plan.bind(refs[:ins], refs[ins : ins + outs], refs[ins + outs :])
        plan.begin()
        plan.end()

    results = pl.pallas_call(
        body,
        out_shape=tuple(plan.outs),
        in_specs=[ANY] * ins,
        out_specs=(ANY,) * outs,
        scratch_shapes=plan.scratch,
        compiler_params=pltpu.CompilerParams(
            collective_id=cid, has_side_effects=True, vmem_limit_bytes=plan.vmem() + 4 * MIB
        ),
    )(*plan.ins)
    return plan.take(results)


def scan_tail_body(rows, length, step_ref, u_ref, b_ref, rate_ref, last_ref):
    rate = rate_ref[...]

    def advance(i, states):
        new = []
        for r in range(rows):
            keep = jnp.exp2(step_ref[r, pl.ds(i, 1), :] * rate)
            new.append(keep * states[r] + u_ref[r, pl.ds(i, 1), :] * b_ref[r, i])
        return tuple(new)

    start = tuple(jnp.zeros((DS, 128), f32) for _ in range(rows))
    end = lax.fori_loop(0, length, advance, start, unroll=4)
    for r in range(rows):
        last_ref[r] = end[r]


def scan_full_body(
    rows, length, step_ref, u_ref, b_ref, c_ref, rate_ref, entry_ref, read_ref, hist_ref
):
    rate = rate_ref[...]

    def advance(i, states):
        new = []
        for r in range(rows):
            hist_ref[r, i] = states[r]
            keep = jnp.exp2(step_ref[r, pl.ds(i, 1), :] * rate)
            h = keep * states[r] + u_ref[r, pl.ds(i, 1), :] * b_ref[r, i]
            read_ref[r, pl.ds(i, 1), :] = jnp.sum(h * c_ref[r, i], axis=0, keepdims=True)
            new.append(h)
        return tuple(new)

    lax.fori_loop(0, length, advance, tuple(entry_ref[r] for r in range(rows)), unroll=4)


def adjoint_head_body(rows, length, step_ref, dy_ref, c_ref, rate_ref, first_ref):
    rate = rate_ref[...]

    def advance(k, carried):
        i = length - 1 - k
        new = []
        for r in range(rows):
            keep = jnp.exp2(step_ref[r, pl.ds(i, 1), :] * rate)
            new.append(keep * (carried[r] + dy_ref[r, pl.ds(i, 1), :] * c_ref[r, i]))
        return tuple(new)

    start = tuple(jnp.zeros((DS, 128), f32) for _ in range(rows))
    end = lax.fori_loop(0, length, advance, start, unroll=4)
    for r in range(rows):
        first_ref[r] = end[r]


def adjoint_full_body(
    rows,
    length,
    step_ref,
    u_ref,
    dy_ref,
    b_ref,
    c_ref,
    rate_ref,
    hist_ref,
    later_ref,
    du_ref,
    dexp_ref,
    db_ref,
    dc_ref,
    drate_ref,
):
    rate = rate_ref[...]

    @pl.when(pl.program_id(1) == 0)
    def _():
        db_ref[...] = jnp.zeros_like(db_ref)
        dc_ref[...] = jnp.zeros_like(dc_ref)

    def advance(k, carried):
        i = length - 1 - k
        new = []
        drate = carried[rows]
        for r in range(rows):
            step = step_ref[r, pl.ds(i, 1), :]
            u = u_ref[r, pl.ds(i, 1), :]
            dy = dy_ref[r, pl.ds(i, 1), :]
            keep = jnp.exp2(step * rate)
            b = b_ref[r, i]
            kept = keep * hist_ref[r, i]
            g = carried[r] + dy * c_ref[r, i]
            w = g * kept
            dc_ref[r, i] += (kept + u * b) * dy
            db_ref[r, i] += g * u
            du_ref[r, pl.ds(i, 1), :] = jnp.sum(g * b, axis=0, keepdims=True)
            dexp_ref[r, pl.ds(i, 1), :] = jnp.sum(w * rate, axis=0, keepdims=True)
            drate = drate + w * step
            new.append(keep * g)
        return tuple(new) + (drate,)

    start = tuple(later_ref[r] for r in range(rows)) + (jnp.zeros((DS, 128), f32),)
    end = lax.fori_loop(0, length, advance, start, unroll=2)
    drate_ref[0] = end[rows]


def hosted_call(body, grid, in_specs, out_specs, out_shape, args, cid, plan, own_vmem, later=()):
    steps = 1
    for size in grid:
        steps *= size
    n_in, n_out, x_in, x_out = len(args), len(out_shape), len(plan.ins), len(plan.outs)

    def hosted(*refs):
        mine_in, refs = refs[:n_in], refs[n_in:]
        plan_in, refs = refs[:x_in], refs[x_in:]
        mine_out, refs = refs[:n_out], refs[n_out:]
        plan.bind(plan_in, refs[:x_out], refs[x_out:])
        at = pl.program_id(0)
        for k in range(1, len(grid)):
            at = at * grid[k] + pl.program_id(k)
        pl.when(at == 0)(plan.begin)
        for t in range(1, min(plan.hops, len(later) + 1)):
            pl.when(at == later[t - 1])(functools.partial(plan.hop_step, t))
        body(*mine_in, *mine_out)
        pl.when(at == steps - 1)(functools.partial(plan.end, 1 + len(later)))

    results = pl.pallas_call(
        hosted,
        grid=grid,
        in_specs=in_specs + [ANY] * x_in,
        out_specs=tuple(out_specs) + (ANY,) * x_out,
        out_shape=tuple(out_shape) + tuple(plan.outs),
        scratch_shapes=plan.scratch,
        compiler_params=pltpu.CompilerParams(
            vmem_limit_bytes=plan.vmem() + own_vmem, collective_id=cid, has_side_effects=True
        ),
    )(*args, *plan.ins)
    return tuple(results[:n_out]) + plan.take(results[n_out:])


def scan_call(body, args, kinds, outs, rows_all, length, width, cid, plan, later=()):
    rows = 4 if rows_all % 4 == 0 else rows_all
    single = pl.Buffered(buffer_count=1)
    grid = (rows_all // rows, width // 128)

    def spec(kind):
        extra = {"pipeline_mode": single} if kind == SPREAD else {}
        if kind == SEQ:
            return pl.BlockSpec((rows, length, 128), lambda r, g: (r, 0, g), **extra)
        if kind == SPREAD:
            return pl.BlockSpec((rows, length, DS, 128), lambda r, g: (r, 0, 0, 0), **extra)
        if kind == HIST:
            return pl.BlockSpec((rows, length, DS, 128), lambda r, g: (r, 0, 0, g), **extra)
        if kind == STATE:
            return pl.BlockSpec((rows, DS, 128), lambda r, g: (r, 0, g), **extra)
        if kind == RATE:
            return pl.BlockSpec((DS, 128), lambda r, g: (0, g), **extra)
        return pl.BlockSpec((1, DS, 128), lambda r, g: (r, 0, g), **extra)

    def block_bytes(kind):
        wide = rows * length * 128 * 4
        return {SEQ: 2 * wide, SPREAD: DS * wide, HIST: 2 * DS * wide}.get(kind, MIB // 2)

    shape_of = {
        SEQ: (rows_all, length, width),
        SPREAD: (rows_all, length, DS, 128),
        HIST: (rows_all, length, DS, width),
        STATE: (rows_all, DS, width),
        DRATE: (rows_all // rows, DS, width),
    }
    return hosted_call(
        functools.partial(body, rows, length),
        grid,
        [spec(k) for k in kinds],
        [spec(k) for k in outs],
        [jax.ShapeDtypeStruct(shape_of[k], f32) for k in outs],
        args,
        cid,
        plan,
        8 * MIB + sum(block_bytes(k) for k in tuple(kinds) + tuple(outs)),
        later,
    )


def attend_body(heads, q_ref, k_ref, v_ref, bias_ref, out_ref, total_ref):
    keys = k_ref[...].T
    for h in range(heads):
        rows = slice(h * HD, (h + 1) * HD)
        scores = jnp.dot(keys, q_ref[rows], preferred_element_type=f32)
        scores = scores * HD**-0.5 + bias_ref[...]
        peak = jnp.max(scores, axis=0, keepdims=True)
        grown = jnp.exp(scores - peak)
        total = jnp.sum(grown, axis=0, keepdims=True)
        probs = (grown * (1.0 / total)).astype(bf16)
        out_ref[rows] = jnp.dot(v_ref[...], probs, preferred_element_type=f32).astype(bf16)
        total_ref[0, h : h + 1] = peak + jnp.log(total)


def attend_back_body(
    heads, q_ref, k_ref, v_ref, bias_ref, total_ref, grad_ref, dq_ref, dk_ref, dv_ref
):
    keys = k_ref[...].T
    values = v_ref[...].T
    for h in range(heads):
        rows = slice(h * HD, (h + 1) * HD)
        scores = jnp.dot(keys, q_ref[rows], preferred_element_type=f32)
        probs = jnp.exp(scores * HD**-0.5 + bias_ref[...] - total_ref[0, h : h + 1])
        grad = jnp.dot(values, grad_ref[rows], preferred_element_type=f32)
        mean = jnp.sum(probs * grad, axis=0, keepdims=True)
        low = (probs * (grad - mean)).astype(bf16)
        dq = jnp.dot(k_ref[...], low, preferred_element_type=f32)
        dq_ref[rows] = (dq * HD**-0.5).astype(bf16)
        dk = dense_nt(q_ref[rows], low) * HD**-0.5
        dv = dense_nt(grad_ref[rows], probs.astype(bf16))
        if h == 0:
            dk_ref[...] = dk
            dv_ref[...] = dv
        else:
            dk_ref[...] += dk
            dv_ref[...] += dv


def rows_matmul(values, weight, swapped=False):
    count, tokens, depth = values.shape
    if swapped:
        tokens, depth = depth, tokens
    real, width = weight.shape

    def body(value_ref, weight_ref, out_ref):
        value = value_ref[0].T if swapped else value_ref[0][:, :real]
        out_ref[0] = jnp.dot(value, weight_ref[...], preferred_element_type=f32).astype(bf16)

    return pl.pallas_call(
        body,
        grid=(count,),
        in_specs=[
            pl.BlockSpec((1,) + values.shape[1:], lambda r: (r, 0, 0)),
            pl.BlockSpec(weight.shape, lambda r: (0, 0), pipeline_mode=pl.Buffered(buffer_count=1)),
        ],
        out_specs=pl.BlockSpec((1, tokens, width), lambda r: (r, 0, 0)),
        out_shape=jax.ShapeDtypeStruct((count, tokens, width), bf16),
        compiler_params=pltpu.CompilerParams(vmem_limit_bytes=24 * MIB),
    )(values, weight)


def rms_norm(values, gain_row):
    return (
        values * lax.rsqrt(jnp.mean(values * values, axis=-1, keepdims=True) + norm_eps) * gain_row
    )


def dense(operand, partner):
    return jnp.dot(operand, partner, preferred_element_type=f32)


def dense_tn(operand, partner):
    return lax.dot_general(
        operand, partner, (((0,), (0,)), ((), ())), preferred_element_type=f32
    )


def dense_nt(operand, partner):
    return lax.dot_general(
        operand, partner, (((1,), (1,)), ((), ())), preferred_element_type=f32
    )


def conv_silu(extended, conv_taps, same_seg):
    length_out = extended.shape[1] - CONV + 1
    summed = jnp.zeros((extended.shape[0], length_out, extended.shape[2]), f32)
    for offset in range(CONV):
        summed = summed + jnp.where(
            same_seg[offset][:, :, None],
            extended[:, offset : offset + length_out] * conv_taps[offset],
            0.0,
        )
    return jax.nn.silu(summed)


def adam_step(gradient, moments_old, weight_now):
    first_moment = beta_one * moments_old[0] + (1.0 - beta_one) * gradient
    second_moment = beta_two * moments_old[1] + (1.0 - beta_two) * gradient * gradient
    corrected = (
        first_moment
        / (1.0 - beta_one**adam_count)
        / (jnp.sqrt(second_moment / (1.0 - beta_two**adam_count)) + adam_eps)
    )
    return (second_moment, -learn_rate * (corrected + decay_rate * weight_now))


def pad_last(values, width):
    return jnp.pad(values, [(0, 0)] * (values.ndim - 1) + [(0, width - values.shape[-1])])


def column_parts(weight, parts, shards_of, width):
    own = weight.shape[1] // parts // shards_of
    return jnp.stack(
        [
            jnp.concatenate(
                [
                    pad_last(weight[:, (p * shards_of + j) * own : (p * shards_of + j + 1) * own], width)
                    for p in range(parts)
                ],
                axis=1,
            )
            for j in range(shards_of)
        ]
    )


def shards(
    tokens,
    cotangent,
    segments,
    w_qkv,
    m_qkv,
    w_attn_out,
    m_attn_out,
    w_mamba_in,
    m_mamba_in,
    w_ssm_proj,
    m_ssm_proj,
    w_mamba_out,
    m_mamba_out,
    w_gate_up,
    m_gate_up,
    w_ffn_down,
    m_ffn_down,
    ssm_vec,
    m_ssm_vec,
    embed_small,
    m_embed_small,
):
    fs, cs = lax.axis_size(FSDP), lax.axis_size(CTX)
    fi, ci = lax.axis_index(FSDP), lax.axis_index(CTX)
    tok = tokens.shape[1]
    dim = tokens.shape[2]
    row_len = segments.shape[1]
    halves = cs // fs
    reach = min(row_len // 2, WINDOW) // tok
    metas = META // cs
    chan = DI // fs
    chan_p = ceil_to(chan, 128)
    ffw = FF // fs
    ffw_p = ceil_to(ffw, 128)
    heads_dim = NH * HD
    kv_dim = KVH * HD
    groups = NH // KVH
    scale_factor = HD ** (-0.5)
    xdim = DTR + 2 * DS
    both = (FSDP, CTX)

    def row_block(weight):
        rows, cols = weight.shape[0] // halves, weight.shape[1] // fs
        return lax.dynamic_slice(
            weight, ((ci % halves) * rows, (ci // halves) * cols), (rows, cols)
        )

    def unpaired(value, width):
        return jnp.concatenate([value[0][:, :width], value[1][:, :width]], axis=1).astype(f32)

    def spread_hops(weights):
        total, done, out = sum(weights), 0, []
        for k in range(len(weights)):
            upto = (cs - 1) * sum(weights[: k + 1]) // total
            out.append(upto - done)
            done = upto
        return out

    def row_chunks(operand, partner):
        grad = dense_tn(operand, partner).astype(bf16)
        return grad.reshape(cs, 1, grad.shape[0] // cs, grad.shape[1])

    def column_chunks(operand, partner, parts=1):
        cols = partner.shape[1] // fs
        wide = jnp.concatenate(
            [
                pad_last(partner[:, j * cols : (j + 1) * cols], ceil_to(cols, 128))
                for j in range(fs)
            ],
            axis=1,
        )
        grad = dense_tn(operand, wide).astype(bf16)
        return grad.reshape(halves, parts, -1, grad.shape[1])

    def by_rows(value):
        return value.astype(bf16).reshape(fs, tok, -1)

    blocks = 25

    def in_blocks(value):
        return value.reshape(fs, 2, blocks, value.shape[1] // (2 * blocks), value.shape[2])

    mi_send = column_parts(w_mamba_in, 2, fs, chan_p)
    qkv_send = column_parts(w_qkv, 1, fs, w_qkv.shape[1] // fs)
    gain_rows = embed_small[META:]
    meta_rows = lax.dynamic_slice_in_dim(embed_small, ci * metas, metas, 0)
    source = tokens[0].astype(f32)
    normed_f, norm_pull = jax.vjp(rms_norm, source, gain_rows[0])
    normed = normed_f.astype(bf16)
    meta_f, meta_pull = jax.vjp(rms_norm, meta_rows, gain_rows[0])
    meta_low = meta_f.astype(bf16)

    normed_all, seg_all, mi_w, qkv_w = exchange(
        0,
        [
            (normed, GATHER, FSDP),
            (segments, ALL, FSDP),
            (in_blocks(mi_send), (HALF, 0, blocks), WEIGHTS),
            (in_blocks(qkv_send), (HALF, 0, blocks), WEIGHTS),
        ],
    )
    gu_send = in_hbm(in_blocks(column_parts(w_gate_up, 2, fs, ffw_p)))
    mi_w = mi_w.reshape(dim, 2 * chan_p)
    qkv_w = qkv_w.reshape(dim, -1)
    seg_all = seg_all.reshape(fs, row_len)
    seg_row = segments[0]
    normed_all = normed_all.reshape(fs * tok, dim)
    xp_w = jnp.pad(w_ssm_proj[:, :xdim], ((0, chan_p - chan), (0, 0)))
    dt_w = jnp.pad(w_ssm_proj[:, xdim:], ((0, chan_p - chan), (0, 0)))
    mo_w = jnp.pad(w_mamba_out, ((0, chan_p - chan), (0, 0)))
    vec = pad_last(lax.dynamic_slice_in_dim(ssm_vec, fi * chan, chan, 1), chan_p)

    normed_rows = normed_all.reshape(fs, tok, dim)
    qkv_parts = jnp.einsum("ftd,dc->fct", normed_rows, qkv_w, preferred_element_type=f32)
    meta_part = jnp.broadcast_to(
        dense(meta_low, qkv_w).astype(bf16)[None], (fs, metas, qkv_w.shape[1])
    )
    qkv_got, meta_got = exchange(
        1, [(qkv_parts.astype(bf16), EACH, FSDP), (meta_part, EACH, FSDP)]
    )
    qkv_own = qkv_got.reshape(heads_dim + 2 * kv_dim, tok)
    queries = qkv_own[:heads_dim]
    keyval = qkv_own[heads_dim:]
    meta_own = jnp.concatenate([meta_got[j] for j in range(fs)], axis=1)[:, heads_dim:]
    kv_before, meta_kv, gu_0 = exchange(
        2,
        [
            (keyval, NEXT, CTX),
            (meta_own, ALL, CTX),
            (gu_send, (HALF, 0, 5), WEIGHTS),
        ],
        reach=reach,
    )
    kv_before = jnp.where(
        (ci - 1 - jnp.arange(reach) >= 0)[:, None, None], kv_before, jnp.zeros_like(kv_before)
    )
    key_rows = jnp.concatenate(
        [meta_kv.reshape(META, 2 * kv_dim).T]
        + [kv_before[d - 1] for d in range(reach, 0, -1)]
        + [keyval],
        axis=1,
    )

    mamba_in = dense(normed_all, mi_w).reshape(fs, tok, 2 * chan_p)
    inner_pre = mamba_in[:, :, :chan_p]
    gate_z = mamba_in[:, :, chan_p:]
    up_ring = [(c, c + 1) for c in range(cs - 1)]
    down_ring = [(c + 1, c) for c in range(cs - 1)]
    tail_rows = lax.ppermute(inner_pre[:, tok - (CONV - 1) :], CTX, up_ring)
    extended = jnp.concatenate([tail_rows, inner_pre], axis=1)
    seg_ext = lax.dynamic_slice_in_dim(
        jnp.concatenate([jnp.full((fs, CONV - 1), -1, jnp.int32), seg_all], axis=1),
        ci * tok,
        tok + CONV - 1,
        1,
    )
    own_seg = seg_ext[:, CONV - 1 :]
    same_seg = [seg_ext[:, o : o + tok] == own_seg for o in range(CONV)]
    starts = own_seg != seg_ext[:, CONV - 2 : -1]
    inner_x, conv_pull = jax.vjp(
        lambda ext_rows, taps: conv_silu(ext_rows, taps, same_seg), extended, vec[:CONV]
    )
    inner_low = inner_x.astype(bf16).reshape(fs * tok, chan_p)
    xproj_part = lax.dot_general(
        xp_w, inner_low, (((0,), (1,)), ((), ())), preferred_element_type=f32
    )
    xproj_got, attn_old, ssm_proj_old = exchange(
        3,
        [
            (xproj_part, GATHER, FSDP),
            (row_block(w_attn_out), CROSS, BOTH),
            (row_block(w_ssm_proj), CROSS, BOTH),
        ],
    )
    xproj = jnp.sum(xproj_got, axis=0).T
    delta_low = xproj[:, :DTR].astype(bf16)
    pre_delta = dense_nt(delta_low, dt_w).reshape(fs, tok, chan_p) + vec[CONV]
    step = jax.nn.softplus(pre_delta)
    step_far = jnp.where(starts[:, :, None], FAR, step)
    drive = step * inner_x

    def spread(columns):
        return jnp.broadcast_to(columns.reshape(fs, tok, DS, 1), (fs, tok, DS, 128))

    b_wide = spread(xproj[:, DTR : DTR + DS])
    c_wide = spread(xproj[:, DTR + DS : xdim])
    rate = -jnp.exp(vec[CONV + 2 :])
    rate2 = rate * LOG2E
    sizes = (fs, tok, chan_p)
    last_state, mamba_out_old = scan_call(
        scan_tail_body,
        (step_far, drive, b_wide, rate2),
        (SEQ, SEQ, SPREAD, RATE),
        (STATE,),
        *sizes,
        cid=19,
        plan=Traffic([(row_block(w_mamba_out), CROSS, BOTH)]),
    )
    step_sum = jnp.sum(step_far, axis=1)
    state_before, sums, gu_2 = exchange(
        4,
        [
            (last_state.astype(bf16), NEXT, CTX),
            (step_sum, ALL, CTX),
            (gu_send, (HALF, 10, 19), WEIGHTS),
        ],
        reach=reach,
    )

    def decay_of(block):
        total = lax.dynamic_index_in_dim(sums, jnp.clip(block, 0, cs - 1), 0, keepdims=False)
        return jnp.exp2(total[:, None, :] * rate2)

    entry = jnp.zeros((fs, DS, chan_p), f32)
    for d in range(reach, 0, -1):
        there = jnp.where(ci >= d, state_before[d - 1].astype(f32), 0.0)
        entry = decay_of(ci - d) * entry + there
    readout, hist, ffn_down_old = scan_call(
        scan_full_body,
        (step_far, drive, b_wide, c_wide, rate2, entry),
        (SEQ, SEQ, SPREAD, SPREAD, RATE, STATE),
        (SEQ, HIST),
        *sizes,
        cid=20,
        plan=Traffic([(row_block(w_ffn_down), CROSS, BOTH)]),
    )
    skip = vec[CONV + 1]
    pre_mix = readout + skip * inner_x
    gate_s = jax.nn.sigmoid(gate_z)
    gate_silu = gate_z * gate_s
    mixture_low = (pre_mix * gate_silu).astype(bf16).reshape(fs * tok, chan_p)
    ssm_part = rows_matmul(mixture_low.reshape(fs, tok, chan_p), w_mamba_out)

    key_span = (reach + 1) * tok
    padded_seg = jnp.concatenate([jnp.full((reach * tok,), -1, jnp.int32), seg_row])
    key_seg = lax.dynamic_slice_in_dim(padded_seg, ci * tok, key_span, 0)
    query_seg = lax.dynamic_slice_in_dim(seg_row, ci * tok, tok, 0)
    query_pos = jnp.arange(tok, dtype=jnp.int32) + reach * tok
    key_pos = jnp.arange(key_span, dtype=jnp.int32)
    allowed = (
        (key_seg[:, None] == query_seg[None, :])
        & (key_pos[:, None] <= query_pos[None, :])
        & (query_pos[None, :] - key_pos[:, None] < WINDOW)
    )
    allowed = jnp.concatenate([jnp.ones((META, tok), jnp.bool_), allowed], axis=0)
    bias = jnp.where(allowed, 0.0, -1e30)
    seen = META + key_span
    q_spec = pl.BlockSpec((groups * HD, tok), lambda g: (g, 0))
    k_spec = pl.BlockSpec((HD, seen), lambda g: (g, 0))
    v_spec = pl.BlockSpec((HD, seen), lambda g: (g + KVH, 0))
    bias_spec = pl.BlockSpec((seen, tok), lambda g: (0, 0))
    total_spec = pl.BlockSpec((1, groups, tok), lambda g: (g, 0, 0))
    attended, log_totals, gu_1 = hosted_call(
        functools.partial(attend_body, groups),
        (KVH,),
        [q_spec, k_spec, v_spec, bias_spec],
        [q_spec, total_spec],
        [
            jax.ShapeDtypeStruct((heads_dim, tok), bf16),
            jax.ShapeDtypeStruct((KVH, groups, tok), f32),
        ],
        (queries, key_rows, key_rows, bias),
        16,
        Traffic([(gu_send, (HALF, 5, 10), WEIGHTS)]),
        12 * MIB,
    )
    wide = heads_dim // fs
    att_got, gu_3 = exchange(
        5,
        [
            (attended.reshape(fs, wide, tok), EACH, FSDP),
            (gu_send, (HALF, 19, 25), WEIGHTS),
        ],
    )
    gu_w = jnp.concatenate([gu_0, gu_1, gu_2, gu_3], axis=2).reshape(dim, 2 * ffw_p)
    att_tp = jnp.swapaxes(att_got, 1, 2).reshape(fs * tok, wide)
    attn_part = rows_matmul(att_got, w_attn_out, True)
    attn_got, ssm_got = exchange(
        6, [(attn_part, REDUCE, FSDP), (ssm_part, REDUCE, FSDP)]
    )
    attn_proj = jnp.sum(attn_got.astype(f32), axis=0)
    ssm_proj = jnp.sum(ssm_got.astype(f32), axis=0)
    attn_branch, attn_pull = jax.vjp(rms_norm, attn_proj, gain_rows[1])
    ssm_branch, ssm_norm_pull = jax.vjp(rms_norm, ssm_proj, gain_rows[2])
    residual = source + 0.5 * (attn_branch + ssm_branch)
    ffn_in_f, ffn_norm_pull = jax.vjp(rms_norm, residual, gain_rows[3])
    ffn_in, cot_all = exchange(
        7, [(ffn_in_f.astype(bf16), GATHER, FSDP), (cotangent[0], GATHER, FSDP)]
    )
    cot_all = cot_all.reshape(fs * tok, dim)
    ffn_in = ffn_in.reshape(fs * tok, dim)

    gate_up = dense(ffn_in, gu_w)
    hidden_f, glu_pull = jax.vjp(
        lambda values: jax.nn.silu(values[:, :ffw_p]) * values[:, ffw_p:], gate_up
    )
    hidden_wide = hidden_f.astype(bf16)
    hidden = hidden_wide[:, :ffw]
    down_part = rows_matmul(hidden_wide.reshape(fs, tok, ffw_p), w_ffn_down)
    hidden_grad = pad_last(dense_nt(cot_all, w_ffn_down), ffw_p)
    gate_up_grad = glu_pull(hidden_grad)[0].astype(bf16)
    ring_one = Ring(
        [
            row_chunks(ffn_in, gate_up_grad[:, :ffw_p]),
            row_chunks(ffn_in, gate_up_grad[:, ffw_p:]),
            column_chunks(hidden, cot_all, 2),
        ],
        [(0, 0, 1), (1, 0, -1), (2, 0, 1), (2, 1, -1)],
    )
    hops = spread_hops([1, 1, 1, 1, 2, 1])
    ffn_back = by_rows(dense_nt(gate_up_grad, gu_w))
    (back_got,) = exchange(8, [(ffn_back, REDUCE, FSDP)], ring_one, hops[0])
    resid_part, gain_ffn_grad = ffn_norm_pull(jnp.sum(back_got.astype(f32), axis=0))
    residual_grad = cotangent[0].astype(f32) + resid_part
    branch_grad = 0.5 * residual_grad
    attn_proj_grad, gain_attn_grad = attn_pull(branch_grad)
    ssm_proj_grad, gain_ssm_grad = ssm_norm_pull(branch_grad)
    branch_low = (attn_proj_grad.astype(bf16), ssm_proj_grad.astype(bf16))
    attn_proj_low, ssm_proj_low = exchange(
        9,
        [(branch_low[0], GATHER, FSDP), (branch_low[1], GATHER, FSDP)],
        ring_one,
        hops[1],
    )
    attn_proj_low = attn_proj_low.reshape(fs * tok, dim)
    ssm_proj_low = ssm_proj_low.reshape(fs * tok, dim)
    att_grad_tp = jnp.einsum(
        "ftd,cd->fct",
        attn_proj_low.reshape(fs, tok, dim),
        w_attn_out,
        preferred_element_type=f32,
    ).astype(bf16)
    (att_grad_got,) = exchange(10, [(att_grad_tp, EACH, FSDP)], ring_one, hops[2])

    def own_pair(held, part):
        piece = lax.dynamic_slice_in_dim(held, ci * (dim // cs), dim // cs, 0)
        return jnp.stack([piece[:, :part], piece[:, part:]])

    qkv_old = lax.dynamic_slice_in_dim(qkv_w, ci * (dim // cs), dim // cs, 0)
    attended_grad = att_grad_got.reshape(heads_dim, tok)

    query_grad, key_grad, value_grad, mamba_in_old = hosted_call(
        functools.partial(attend_back_body, groups),
        (KVH,),
        [q_spec, k_spec, v_spec, bias_spec, total_spec, q_spec],
        [q_spec, k_spec, k_spec],
        [
            jax.ShapeDtypeStruct((heads_dim, tok), bf16),
            jax.ShapeDtypeStruct((kv_dim, seen), f32),
            jax.ShapeDtypeStruct((kv_dim, seen), f32),
        ],
        (queries, key_rows, key_rows, bias, log_totals, attended_grad),
        24,
        Traffic([(own_pair(mi_w, chan_p), PAIR, FSDP)], ring_one, hops[3]),
        16 * MIB,
    )
    kv_grad_all = jnp.concatenate([key_grad, value_grad], axis=0)
    kv_send = jnp.stack(
        [
            kv_grad_all[:, META + (reach - d) * tok : META + (reach - d + 1) * tok]
            for d in range(1, reach + 1)
        ]
    ).astype(bf16)
    meta_send = kv_grad_all[:, :META].T.astype(bf16).reshape(cs, metas, 2 * kv_dim)
    kv_back, meta_back, down_got = exchange(
        13,
        [
            (kv_send, BACK, CTX),
            (meta_send, EACH, CTX),
            (down_part, REDUCE, FSDP),
        ],
        ring_one,
        hops[4],
        reach,
    )
    output = residual + jnp.sum(down_got.astype(f32), axis=0)
    own_kv_grad = kv_grad_all[:, META + reach * tok :]
    for d in range(1, reach + 1):
        own_kv_grad = own_kv_grad + jnp.where(ci + d < cs, kv_back[d - 1].astype(f32), 0.0)
    meta_kv_grad = jnp.sum(meta_back.astype(f32), axis=0).astype(bf16)
    meta_grad_parts = column_parts(
        jnp.pad(meta_kv_grad, ((0, 0), (heads_dim, 0))), 1, fs, qkv_w.shape[1]
    )
    qkv_grad = jnp.concatenate([query_grad, own_kv_grad.astype(bf16)], axis=0)
    qkv_grad_tp, meta_grad_tp = exchange(
        14,
        [
            (qkv_grad.reshape(fs, -1, tok), EACH, FSDP),
            (meta_grad_parts, EACH, FSDP),
        ],
        ring_one,
        hops[5],
    )

    mixture_grad = dense_nt(ssm_proj_low, mo_w).reshape(fs, tok, chan_p)
    read_grad = mixture_grad * gate_silu
    gate_grad = mixture_grad * pre_mix * (gate_s * (1.0 + gate_z * (1.0 - gate_s)))
    gate_low = gate_grad.astype(bf16).reshape(fs * tok, chan_p)
    qkv_full = jnp.einsum("ftd,fct->dc", normed_rows, qkv_grad_tp, preferred_element_type=f32)
    qkv_full = qkv_full + jnp.einsum(
        "md,fmc->dc", meta_low, meta_grad_tp, preferred_element_type=f32
    )
    ring_two = Ring(
        [
            row_chunks(normed_all, gate_low),
            qkv_full.astype(bf16).reshape(cs, 1, dim // cs, qkv_w.shape[1]),
            column_chunks(att_tp, attn_proj_low),
            column_chunks(mixture_low[:, :chan], ssm_proj_low),
        ],
        [(0, 0, 1), (1, 0, 1), (2, 0, -1), (3, 0, -1)],
    )
    hops = spread_hops([1, 2, 2, 2])
    gate_sum, up_sum, down_top, down_low = ring_one.finish()
    first_adj, gate_up_old = scan_call(
        adjoint_head_body,
        (step_far, read_grad, c_wide, rate2),
        (SEQ, SEQ, SPREAD, RATE),
        (STATE,),
        *sizes,
        cid=21,
        plan=Traffic([(own_pair(gu_w, ffw_p), PAIR, FSDP)], ring_two, hops[0]),
    )
    adj_after, gate_up_sum = exchange(
        11,
        [
            (first_adj.astype(bf16), PREV, CTX),
            (jnp.stack([gate_sum, up_sum]).astype(bf16), PAIR, FSDP),
        ],
        ring_two,
        hops[1],
        reach,
    )
    gate_up_old = unpaired(gate_up_old, ffw)
    mamba_in_old = unpaired(mamba_in_old, chan)
    later = jnp.zeros((fs, DS, chan_p), f32)
    for d in range(reach, 0, -1):
        there = jnp.where(ci + d < cs, adj_after[d - 1].astype(f32), 0.0)
        later = decay_of(ci + d) * later + there
    drive_grad, exp_grad, b_acc, c_acc, rate_grad = scan_call(
        adjoint_full_body,
        (step_far, drive, read_grad, b_wide, c_wide, rate2, hist, later),
        (SEQ, SEQ, SEQ, SPREAD, SPREAD, RATE, HIST, STATE),
        (SEQ, SEQ, SPREAD, SPREAD, DRATE),
        *sizes,
        cid=22,
        plan=Traffic([], ring_two, hops[2]),
        later=(3,) if hops[2] == 2 else (),
    )
    cross = [
        (f * cs + c, (c // halves) * cs + halves * f + c % halves)
        for f in range(fs)
        for c in range(cs)
    ]
    down_both = jnp.concatenate([down_top, down_low], axis=0).astype(bf16)
    drive_grad, down_both = together(drive_grad, down_both)
    down_sum = lax.ppermute(down_both, (FSDP, CTX), cross)
    step_grad = drive_grad * inner_x + exp_grad * LN2
    pre_delta_grad = step_grad * jax.nn.sigmoid(pre_delta)
    inner_grad = drive_grad * step + skip * read_grad
    small_grad = jnp.concatenate(
        [
            jnp.sum(pre_delta_grad, axis=(0, 1))[None],
            jnp.sum(inner_x * read_grad, axis=(0, 1))[None],
            jnp.sum(rate_grad, axis=0) * rate,
        ],
        axis=0,
    )
    pre_delta_low = pre_delta_grad.astype(bf16).reshape(fs * tok, chan_p)
    xgrad_part = jnp.concatenate(
        [
            lax.dot_general(
                dt_w, pre_delta_low, (((0,), (1,)), ((), ())), preferred_element_type=f32
            ),
            jnp.sum(b_acc, axis=-1).reshape(fs * tok, DS).T,
            jnp.sum(c_acc, axis=-1).reshape(fs * tok, DS).T,
        ],
        axis=0,
    )
    (xgrad_got,) = exchange(12, [(xgrad_part, GATHER, FSDP)], ring_two, hops[3])
    xproj_grad = jnp.sum(xgrad_got, axis=0).T.astype(bf16)
    inner_grad = inner_grad + dense_nt(xproj_grad, xp_w).reshape(fs, tok, chan_p)
    ext_grad, taps_grad = conv_pull(inner_grad)
    returned = lax.ppermute(ext_grad[:, : CONV - 1].astype(bf16), CTX, down_ring).astype(f32)
    inner_pre_grad = ext_grad[:, CONV - 1 :] + jnp.pad(
        returned, ((0, 0), (tok - (CONV - 1), 0), (0, 0))
    )
    inner_pre_low = inner_pre_grad.astype(bf16).reshape(fs * tok, chan_p)
    mamba_in_grad = jnp.concatenate([inner_pre_low, gate_low], axis=1)
    split = ceil_to(chan_p * 9 // 16, 128)
    ring_three = Ring(
        [
            row_chunks(normed_all, inner_pre_low[:, :split]),
            row_chunks(normed_all, inner_pre_low[:, split:]),
            column_chunks(
                jnp.concatenate([inner_low[:, :chan], pre_delta_low[:, :chan]], axis=0),
                jnp.concatenate(
                    [
                        jnp.pad(xproj_grad, ((0, 0), (0, DTR))),
                        jnp.pad(delta_low, ((0, 0), (xdim, 0))),
                    ],
                    axis=0,
                ),
            ),
        ],
        [(0, 0, 1), (1, 0, -1), (2, 0, -1)],
    )
    vec_grad = jnp.concatenate([taps_grad, small_grad], axis=0)
    token_back = jnp.einsum("fct,dc->ftd", qkv_grad_tp, qkv_w, preferred_element_type=f32)
    token_back = token_back + dense_nt(mamba_in_grad, mi_w).reshape(fs, tok, dim)
    meta_back_rows = jnp.einsum("fmc,dc->fmd", meta_grad_tp, qkv_w, preferred_element_type=f32)
    token_back = by_rows(token_back)
    hops = spread_hops([3, 2, 2])
    token_got, meta_rows_got = exchange(
        15,
        [(token_back, REDUCE, FSDP), (meta_back_rows.astype(bf16), REDUCE, FSDP)],
        ring_three,
        hops[0],
    )
    source_part, gain_in_grad = norm_pull(jnp.sum(token_got.astype(f32), axis=0))
    source_grad = residual_grad + source_part
    meta_grad, gain_in_meta = meta_pull(jnp.sum(meta_rows_got.astype(f32), axis=0))
    embed_part = jnp.concatenate(
        [
            meta_grad,
            jnp.stack([gain_in_grad + gain_in_meta, gain_attn_grad, gain_ssm_grad, gain_ffn_grad]),
        ],
        axis=0,
    )
    (embed_rows,) = exchange(17, [(embed_part, GATHER, FSDP)], ring_three, hops[1])
    embed_got, vec_got = exchange(
        18,
        [
            (jnp.sum(embed_rows, axis=0).astype(bf16), LINE, CTX),
            (vec_grad.astype(bf16), LINE, CTX),
        ],
        ring_three,
        hops[2],
    )
    embed_got = embed_got.astype(f32)
    vec_part = jnp.sum(vec_got.astype(f32), axis=0)
    embed_total = jnp.concatenate(
        [embed_got[:, :metas].reshape(META, dim), jnp.sum(embed_got[:, metas:], axis=0)], axis=0
    )
    gate_half, qkv_gradient, attn_sum, mamba_out_sum = ring_two.finish()
    inner_a, inner_b, proj_sum = ring_three.finish()
    mamba_in_sum, attn_sum, mamba_out_sum, proj_sum, vec_all = exchange(
        23,
        [
            (
                jnp.stack([jnp.concatenate([inner_a, inner_b], axis=1), gate_half]).astype(bf16),
                PAIR,
                FSDP,
            ),
            (attn_sum.astype(bf16), CROSS, BOTH),
            (mamba_out_sum.astype(bf16), CROSS, BOTH),
            (proj_sum.astype(bf16), CROSS, BOTH),
            (vec_part, GATHER, FSDP),
        ],
    )
    ssm_total = jnp.concatenate([vec_all[j, :, :chan] for j in range(fs)], axis=1)
    gate_up_gradient = unpaired(gate_up_sum, ffw)
    mamba_in_gradient = unpaired(mamba_in_sum, chan)
    ffn_down_gradient = down_sum[:, : dim // fs].astype(f32)
    attn_gradient = attn_sum[:, : dim // fs].astype(f32)
    mamba_out_gradient = mamba_out_sum[:, : dim // fs].astype(f32)
    ssm_proj_gradient = proj_sum[:, : w_ssm_proj.shape[1] // fs].astype(f32)

    def adam_block(gradient, moments_old, weight):
        return adam_step(gradient, moments_old, weight.astype(f32))

    qkv_moments, qkv_update = adam_block(qkv_gradient, m_qkv, qkv_old)
    attn_moments, attn_update = adam_block(attn_gradient, m_attn_out, attn_old)
    mamba_in_moments, mamba_in_update = adam_block(mamba_in_gradient, m_mamba_in, mamba_in_old)
    ssm_proj_moments, ssm_proj_update = adam_block(ssm_proj_gradient, m_ssm_proj, ssm_proj_old)
    mamba_out_moments, mamba_out_update = adam_block(
        mamba_out_gradient, m_mamba_out, mamba_out_old
    )
    gate_up_moments, gate_up_update = adam_block(gate_up_gradient, m_gate_up, gate_up_old)
    ffn_down_moments, ffn_down_update = adam_block(ffn_down_gradient, m_ffn_down, ffn_down_old)
    ssm_vec_moments, ssm_vec_update = adam_step(ssm_total, m_ssm_vec, ssm_vec)
    embed_moments, embed_update = adam_step(embed_total, m_embed_small, embed_small)
    return (
        output.astype(jnp.bfloat16)[None],
        source_grad[None],
        qkv_gradient,
        qkv_moments,
        qkv_update,
        attn_gradient,
        attn_moments,
        attn_update,
        mamba_in_gradient,
        mamba_in_moments,
        mamba_in_update,
        ssm_proj_gradient,
        ssm_proj_moments,
        ssm_proj_update,
        mamba_out_gradient,
        mamba_out_moments,
        mamba_out_update,
        gate_up_gradient,
        gate_up_moments,
        gate_up_update,
        ffn_down_gradient,
        ffn_down_moments,
        ffn_down_update,
        ssm_total,
        ssm_vec_moments,
        ssm_vec_update,
        embed_total,
        embed_moments,
        embed_update,
    )


def solution(mesh):
    in_specs = (
        P(FSDP, CTX, None),
        P(FSDP, CTX, None),
        P(FSDP, None),
        P(FSDP, None),
        P(None, CTX, FSDP),
        P(FSDP, None),
        P(None, CTX, FSDP),
        P(FSDP, None),
        P(None, CTX, FSDP),
        P(FSDP, None),
        P(None, CTX, FSDP),
        P(FSDP, None),
        P(None, CTX, FSDP),
        P(FSDP, None),
        P(None, CTX, FSDP),
        P(FSDP, None),
        P(None, CTX, FSDP),
        P(),
        P(),
        P(),
        P(),
    )
    out_specs = (
        P(FSDP, CTX, None),
        P(FSDP, CTX, None),
        P(CTX, FSDP),
        P(CTX, FSDP),
        P(CTX, FSDP),
        P(CTX, FSDP),
        P(CTX, FSDP),
        P(CTX, FSDP),
        P(CTX, FSDP),
        P(CTX, FSDP),
        P(CTX, FSDP),
        P(CTX, FSDP),
        P(CTX, FSDP),
        P(CTX, FSDP),
        P(CTX, FSDP),
        P(CTX, FSDP),
        P(CTX, FSDP),
        P(CTX, FSDP),
        P(CTX, FSDP),
        P(CTX, FSDP),
        P(CTX, FSDP),
        P(CTX, FSDP),
        P(CTX, FSDP),
        P(),
        P(),
        P(),
        P(),
        P(),
        P(),
    )
    return jax.shard_map(shards, mesh=mesh, in_specs=in_specs, out_specs=out_specs, check_vma=False)
```

```python
import functools

import jax
import jax.numpy as jnp
from jax import lax
from jax.experimental import pallas as pl
from jax.experimental.pallas import tpu as pltpu
from jax.sharding import PartitionSpec as P

NH = 25
KVH = 5
HD = 64
DI = 3200
DS = 16
DTR = 100
FF = 5504
META = 128
CONV = 4
WINDOW = 1024

norm_eps = 1e-05
beta_one = 0.9
beta_two = 0.95
learn_rate = 0.01
decay_rate = 0.1
adam_eps = 1e-08
adam_count = 10.0

FSDP = "fsdp"
CTX = "ctx"
EACH = "each"
ALL = "all"
GATHER = "gather"
REDUCE = "reduce"
HALF = "half"
WEIGHTS = "weights"
BOTH = "both"
CROSS = "cross"
PAIR = "pair"
NEXT = "next"
PREV = "prev"
BACK = "back"
LINE = "line"
SEQ = "seq"
SPREAD = "spread"
HIST = "hist"
STATE = "state"
RATE = "rate"
DRATE = "drate"
RING = "ring"
LOG2E = 1.4426950408889634
LN2 = 0.6931471805599453
FAR = 1e30
bf16 = jnp.bfloat16
f32 = jnp.float32
ANY = pl.BlockSpec(memory_space=pltpu.HBM)
MIB = 1024 * 1024


def together(*values):
    return lax.optimization_barrier(values)


def ceil_to(value, unit):
    return (value + unit - 1) // unit * unit


def span_of(axis):
    return lax.axis_size(axis), lax.axis_index(axis)


def ring_spot(ci, cs):
    odd = lax.rem(ci, 2)
    return (ci // 2) * (1 - odd) + (cs - 1 - ci // 2) * odd


def ring_block(spot, cs):
    spot = lax.rem(spot + 2 * cs, cs)
    far = spot // (cs // 2)
    return 2 * spot * (1 - far) + (2 * (cs - 1 - spot) + 1) * far


def when(condition, action):
    if condition is None:
        action()
    else:
        pl.when(condition)(action)


def in_hbm(value):
    return pltpu.with_memory_space_constraint(value, pltpu.HBM)


def piece_edges(mode):
    count = mode[2] - mode[1]
    groups = 5 if count > 10 else 3
    edges = [count * k // groups for k in range(groups + 1)]
    return list(zip(edges[:-1], edges[1:]))


def chunk_shape(value, cs):
    lead, _, rows, cols = value.shape
    return (rows, cols if lead == cs else cols * lead // cs)


def chunk_ref(ref, block, part, cs):
    lead = ref.shape[0]
    if lead == cs:
        return ref.at[block, part]
    cols = ref.shape[3] * lead // cs
    columns = pl.ds(pl.multiple_of(block // lead * cols, 128), cols)
    return ref.at[lax.rem(block, lead), part, :, columns]


class Ring:
    def __init__(self, chunks, uses):
        self.chunks, self.uses = chunks, uses
        self.got, self.hop = [], 0

    def finish(self):
        cs, block = span_of(CTX)
        sums = []
        for (k, part, _), got in zip(self.uses, self.got):
            value = self.chunks[k]
            if value.shape[0] == cs:
                own = lax.dynamic_index_in_dim(value, block, 0, keepdims=False)[part]
            else:
                rows, cols = chunk_shape(value, cs)
                at = (block % value.shape[0], part, 0, block // value.shape[0] * cols)
                own = lax.dynamic_slice(value, at, (1, 1, rows, cols))[0, 0]
            sums.append(got.astype(f32) + own.astype(f32))
        return sums


class Traffic:
    def __init__(self, items, ring=None, hops=0, reach=0):
        self.items, self.ring, self.reach = items, ring, reach
        fs, cs = lax.axis_size(FSDP), lax.axis_size(CTX)
        self.hops = min(hops, cs - 1 - ring.hop) if ring is not None else 0
        self.ins = [value for value, _, _ in items]
        self.outs = []
        dma = pltpu.SemaphoreType.DMA
        most = 2 * max(fs, cs)
        count = max(len(items), 1)
        self.scratch = [dma((count, most)), dma((count, most)), dma((count, 2))]
        self.places = {}

        def own_scratch(k, shapes):
            self.places[k] = len(self.scratch)
            self.scratch += shapes

        for k, (value, mode, axis) in enumerate(items):
            shape = value.shape
            if mode in (ALL, GATHER, LINE):
                shape = (lax.axis_size(axis),) + shape
            elif mode in (NEXT, PREV):
                shape = (reach,) + shape
            elif mode == REDUCE:
                shape = (fs // 2,) + shape[1:]
                own_scratch(k, [pltpu.VMEM(shape, value.dtype)] * 2 + [dma((fs // 2,))])
            elif mode[0] == HALF:
                pieces = len(piece_edges(mode))
                shape = shape[:2] + (mode[2] - mode[1],) + shape[3:]
                own_scratch(k, [dma((pieces, 2 * fs)), dma((pieces, 2 * fs))])
            self.outs.append(jax.ShapeDtypeStruct(shape, value.dtype))
        if self.hops:
            self.ins += [in_hbm(value) for value in ring.chunks + ring.got]
            uses = len(ring.uses)
            shapes = [dma((uses, self.hops)), dma((uses, self.hops)), dma((uses, self.hops, 2))]
            for k, _, _ in ring.uses:
                shape = chunk_shape(ring.chunks[k], cs)
                self.outs += [pltpu.HBM(shape, bf16)] * self.hops
                shapes.append(pltpu.VMEM((self.hops, 2) + shape, bf16))
            own_scratch(RING, shapes)

    def vmem(self):
        total = 4 * MIB
        for held in self.scratch:
            if held.memory_space == pltpu.VMEM:
                size = 2
                for extent in held.shape[:-2]:
                    size *= extent
                total += size * ceil_to(held.shape[-2], 16) * ceil_to(held.shape[-1], 128)
        return total

    def bind(self, ins, outs, scratch):
        self.in_refs, self.out_refs, self.sems = ins, outs, scratch

    def remote(self, source, target, send, take, peer):
        return pltpu.make_async_remote_copy(
            src_ref=source,
            dst_ref=target,
            send_sem=send,
            recv_sem=take,
            device_id=peer,
            device_id_type=pl.DeviceIdType.MESH,
        )

    def greet(self):
        barrier = pltpu.get_barrier_semaphore()
        fs, fi = span_of(FSDP)
        cs, ci = span_of(CTX)

        def signal(peer):
            pl.semaphore_signal(
                barrier, inc=1, device_id=peer, device_id_type=pl.DeviceIdType.MESH
            )

        axes = {axis for _, _, axis in self.items}
        if WEIGHTS in axes:
            axes.add(FSDP)
        total = 0
        for axis in (FSDP, CTX):
            if axis in axes:
                n, me = span_of(axis)
                for d in range(1, n):
                    signal({axis: lax.rem(me + d, n)})
                total += n - 1
        if self.hops and CTX not in axes:
            spot = ring_spot(ci, cs)
            signal({CTX: ring_block(spot + 1, cs)})
            signal({CTX: ring_block(spot - 1, cs)})
            total += 2
        if WEIGHTS in axes and CTX not in axes:
            signal({CTX: ci + 1 - 2 * lax.rem(ci, 2)})
            total += 1
        if BOTH in axes:
            halves = cs // fs
            away = ci // halves != fi

            def meet():
                signal({FSDP: ci // halves, CTX: halves * fi + lax.rem(ci, halves)})

            pl.when(away)(meet)
            if total:
                pl.semaphore_wait(barrier, total + jnp.where(away, 1, 0))
            else:
                pl.when(away)(lambda: pl.semaphore_wait(barrier, 1))
        else:
            pl.semaphore_wait(barrier, total)

    def copies(self):
        starts, relays, waits = [], [], []
        fs, fi = span_of(FSDP)
        cs, ci = span_of(CTX)
        send_sem, take_sem, own_sem = self.sems[:3]
        for k, (_, mode, axis) in enumerate(self.items):
            src, dst = self.in_refs[k], self.out_refs[k]

            def add(copy, sends=None, takes=None):
                starts.append((copy.start, sends))
                waits.append((copy.wait_send, sends))
                waits.append((copy.wait_recv, takes))

            def keep(copy, condition=None):
                starts.append((copy.start, condition))
                waits.append((copy.wait, condition))

            core, chip, chips = lax.rem(fi, 2), fi // 2, fs // 2
            mate = {FSDP: fi + 1 - 2 * core}

            def relay(first, second):
                starts.append((first.start, None))
                relays.append((first.wait_recv, None))
                relays.append((second.start, None))
                waits.append((first.wait_send, None))
                waits.append((second.wait_send, None))
                waits.append((second.wait_recv, None))

            if mode == GATHER:
                for d in range(1, chips):
                    to = 2 * lax.rem(chip + d, chips) + core
                    came = 2 * lax.rem(chip + chips - d, chips) + core
                    relay(
                        self.remote(
                            src, dst.at[fi], send_sem.at[k, d], take_sem.at[k, d], {FSDP: to}
                        ),
                        self.remote(
                            dst.at[came],
                            dst.at[came],
                            send_sem.at[k, chips + d],
                            take_sem.at[k, chips + d],
                            mate,
                        ),
                    )
                add(self.remote(src, dst.at[fi], send_sem.at[k, 0], take_sem.at[k, 0], mate))
                keep(pltpu.make_async_copy(src, dst.at[fi], own_sem.at[k, 0]))
            elif mode == LINE:
                across = {CTX: ci + 1 - 2 * lax.rem(ci, 2)}
                for d in range(1, cs // 2):
                    came = lax.rem(ci + cs - 2 * d, cs)
                    relay(
                        self.remote(
                            src,
                            dst.at[ci],
                            send_sem.at[k, d],
                            take_sem.at[k, d],
                            {CTX: lax.rem(ci + 2 * d, cs)},
                        ),
                        self.remote(
                            dst.at[came],
                            dst.at[came],
                            send_sem.at[k, cs // 2 + d],
                            take_sem.at[k, cs // 2 + d],
                            across,
                        ),
                    )
                add(self.remote(src, dst.at[ci], send_sem.at[k, 0], take_sem.at[k, 0], across))
                keep(pltpu.make_async_copy(src, dst.at[ci], own_sem.at[k, 0]))
            elif mode == REDUCE:
                mine, other, load_sem = self.sems[self.places[k] : self.places[k] + 3]
                for d in list(range(1, chips)) + [0]:
                    to = lax.rem(chip + d, chips)
                    first = self.remote(
                        src.at[2 * to + 1 - core],
                        other.at[to],
                        send_sem.at[k, d],
                        take_sem.at[k, d],
                        mate,
                    )
                    load = pltpu.make_async_copy(
                        src.at[2 * to + core], mine.at[to], load_sem.at[d]
                    )
                    starts.append((first.start, None))
                    starts.append((load.start, None))
                    relays.append((load.wait, None))
                    relays.append((first.wait_recv, None))
                    waits.append((first.wait_send, None))

                    def total(mine=mine, other=other, to=to):
                        mine[to] = mine[to] + other[to]

                    relays.append((total, None))
                    if d:
                        second = self.remote(
                            mine.at[to],
                            dst.at[chip],
                            send_sem.at[k, chips + d],
                            take_sem.at[k, chips + d],
                            {FSDP: 2 * to + core},
                        )
                        waits.append((second.wait_send, None))
                        waits.append((second.wait_recv, None))
                    else:
                        second = pltpu.make_async_copy(mine.at[to], dst.at[to], own_sem.at[k, 0])
                        waits.append((second.wait, None))
                    relays.append((second.start, None))
            elif mode[0] == HALF:
                piece_send, piece_take = self.sems[self.places[k] : self.places[k] + 2]
                side = lax.rem(ci, 2)
                across = {CTX: ci + 1 - 2 * side}
                for q, (low, high) in enumerate(piece_edges(mode)):
                    for d in range(1, chips):
                        for b in range(2):
                            to = 2 * lax.rem(chip + d, chips) + lax.rem(core + b, 2)
                            came = 2 * lax.rem(chip + chips - d, chips) + lax.rem(core + b, 2)
                            e = 2 * d + b
                            relay(
                                self.remote(
                                    src.at[to, side, mode[1] + low : mode[1] + high],
                                    dst.at[fi, side, low:high],
                                    piece_send.at[q, e],
                                    piece_take.at[q, e],
                                    {FSDP: to},
                                ),
                                self.remote(
                                    dst.at[came, side, low:high],
                                    dst.at[came, side, low:high],
                                    piece_send.at[q, fs + e],
                                    piece_take.at[q, fs + e],
                                    across,
                                ),
                            )
                for b in range(2):
                    to = mate[FSDP]
                    add(
                        self.remote(
                            src.at[to, b, mode[1] : mode[2]],
                            dst.at[fi, b],
                            send_sem.at[k, b],
                            take_sem.at[k, b],
                            mate,
                        )
                    )
                    keep(
                        pltpu.make_async_copy(
                            src.at[fi, b, mode[1] : mode[2]], dst.at[fi, b], own_sem.at[k, b]
                        )
                    )
            elif mode in (ALL, EACH):
                n, me = span_of(axis)
                for d in range(1, n):
                    peer = lax.rem(me + d, n)
                    source = src.at[peer] if mode == EACH else src
                    add(
                        self.remote(
                            source, dst.at[me], send_sem.at[k, d], take_sem.at[k, d], {axis: peer}
                        )
                    )
                source = src.at[me] if mode == EACH else src
                keep(pltpu.make_async_copy(source, dst.at[me], own_sem.at[k, 0]))
            elif mode == PAIR:
                for p in range(2):
                    peer = (p * fs + fi) // 2
                    slot = lax.rem(fi, 2)
                    away = peer != fi
                    q = 2 * fi + p
                    comes = lax.rem(q, fs) != fi
                    copy = self.remote(
                        src.at[p],
                        dst.at[slot],
                        send_sem.at[k, p],
                        take_sem.at[k, slot],
                        {FSDP: peer},
                    )
                    starts.append((copy.start, away))
                    waits.append((copy.wait_send, away))
                    taken = self.remote(
                        src.at[p], dst.at[p], send_sem.at[k, p], take_sem.at[k, p], {FSDP: peer}
                    )
                    waits.append((taken.wait_recv, comes))
                    keep(
                        pltpu.make_async_copy(src.at[p], dst.at[slot], own_sem.at[k, p]),
                        peer == fi,
                    )
            elif mode == CROSS:
                halves = cs // fs
                away = ci // halves != fi
                peer = {FSDP: ci // halves, CTX: halves * fi + lax.rem(ci, halves)}
                add(self.remote(src, dst, send_sem.at[k, 0], take_sem.at[k, 0], peer), away, away)
                keep(pltpu.make_async_copy(src, dst, own_sem.at[k, 0]), ci // halves == fi)
            elif mode in (NEXT, PREV):
                reach = self.reach
                m = ci if mode == NEXT else cs - 1 - ci
                odd = lax.rem(m, 2)

                def at(spot):
                    spot = lax.rem(spot + cs, cs)
                    return {CTX: spot if mode == NEXT else cs - 1 - spot}

                def on_line(e, m=m, src=src, dst=dst, k=k, at=at):
                    source = src if e == 2 else dst.at[e - 3]
                    return self.remote(
                        source, dst.at[e - 1], send_sem.at[k, e], take_sem.at[k, e], at(m + 2)
                    )

                def to_mate(g, e, m=m, odd=odd, src=src, dst=dst, k=k, at=at, reach=reach):
                    source = src if e == 0 else dst.at[e - 1]
                    spot = reach + 1 + g
                    return self.remote(
                        source,
                        dst.at[g - 1],
                        send_sem.at[k, spot],
                        take_sem.at[k, spot],
                        at(m + 1 - 2 * odd),
                    )

                starts.append((on_line(2).start, m + 2 < cs))
                waits.append((on_line(2).wait_send, m + 2 < cs))
                starts.append((to_mate(1, 0).start, odd == 0))
                waits.append((to_mate(1, 0).wait_send, odd == 0))
                for e in range(2, reach + 1, 2):
                    here = m - e >= 0
                    relays.append((on_line(e).wait_recv, here))
                    if e + 2 <= reach:
                        goes = here & (m + 2 < cs)
                        relays.append((on_line(e + 2).start, goes))
                        waits.append((on_line(e + 2).wait_send, goes))
                    if e + 1 < reach:
                        relays.append((to_mate(e + 1, e).start, here & (odd == 0)))
                        waits.append((to_mate(e + 1, e).wait_send, here & (odd == 0)))
                    relays.append((to_mate(e - 1, e).start, here & (odd == 1)))
                    waits.append((to_mate(e - 1, e).wait_send, here & (odd == 1)))
                for g in range(1, reach, 2):
                    waits.append((to_mate(g, 0).wait_recv, m - g >= 0))
            else:
                for d in range(1, self.reach + 1):
                    add(
                        self.remote(
                            src.at[d - 1],
                            dst.at[d - 1],
                            send_sem.at[k, d],
                            take_sem.at[k, d],
                            {CTX: lax.rem(ci - d + cs, cs)},
                        ),
                        ci - d >= 0,
                        ci + d < cs,
                    )
        return starts, relays, waits

    def ring_refs(self, u):
        base = self.places[RING]
        outs = self.out_refs[len(self.items) + u * self.hops :]
        return self.sems[base], self.sems[base + 1], self.sems[base + 2], self.sems[base + 3 + u], outs

    def hop_copy(self, u, t):
        cs, ci = span_of(CTX)
        spot = ring_spot(ci, cs)
        k, part, way = self.ring.uses[u]
        send, take, _, buffer, outs = self.ring_refs(u)
        if self.ring.hop + t == 0:
            source = chunk_ref(
                self.in_refs[len(self.items) + k], ring_block(spot - way, cs), part, cs
            )
        else:
            source = buffer.at[t, 1]
        return self.remote(
            source, outs[t], send.at[u, t], take.at[u, t], {CTX: ring_block(spot + way, cs)}
        )

    def load_own(self, u, t):
        cs, ci = span_of(CTX)
        k, part, way = self.ring.uses[u]
        _, _, load, buffer, _ = self.ring_refs(u)
        block = ring_block(ring_spot(ci, cs) - way * (self.ring.hop + t + 1), cs)
        return pltpu.make_async_copy(
            chunk_ref(self.in_refs[len(self.items) + k], block, part, cs),
            buffer.at[t, 1],
            load.at[u, t, 1],
        )

    def load_got(self, u, t):
        _, _, load, buffer, outs = self.ring_refs(u)
        if t == 0:
            source = self.in_refs[len(self.items) + len(self.ring.chunks) + u]
        else:
            source = outs[t - 1]
        return pltpu.make_async_copy(source, buffer.at[t, 0], load.at[u, t, 0])

    def hop_step(self, t):
        uses = range(len(self.ring.uses))
        if self.ring.hop + t > 0:
            for u in uses:
                self.load_own(u, t).start()
                if t > 0:
                    self.hop_copy(u, t - 1).wait_recv()
                self.load_got(u, t).start()
        for u in uses:
            if self.ring.hop + t > 0:
                self.load_own(u, t).wait()
                self.load_got(u, t).wait()
                buffer = self.ring_refs(u)[3]
                buffer[t, 1] = buffer[t, 0] + buffer[t, 1]
            self.hop_copy(u, t).start()

    def begin(self):
        self.greet()
        for start, condition in self.copies()[0]:
            when(condition, start)
        if self.hops:
            self.hop_step(0)

    def end(self, hopped=1):
        _, relays, waits = self.copies()
        for step, condition in relays:
            when(condition, step)
        for t in range(hopped, self.hops):
            self.hop_step(t)
        for wait, condition in waits:
            when(condition, wait)
        for u in range(len(self.ring.uses) if self.hops else 0):
            for t in range(self.hops):
                self.hop_copy(u, t).wait_send()
            self.hop_copy(u, self.hops - 1).wait_recv()

    def take(self, results):
        count = len(self.items)
        if self.hops:
            last = count + self.hops - 1
            self.ring.got = [results[last + u * self.hops] for u in range(len(self.ring.uses))]
            self.ring.hop += self.hops
        return tuple(results[:count])


def exchange(cid, items, ring=None, hops=0, reach=0):
    plan = Traffic(items, ring, hops, reach)
    ins, outs = len(plan.ins), len(plan.outs)

    def body(*refs):
        plan.bind(refs[:ins], refs[ins : ins + outs], refs[ins + outs :])
        plan.begin()
        plan.end()

    results = pl.pallas_call(
        body,
        out_shape=tuple(plan.outs),
        in_specs=[ANY] * ins,
        out_specs=(ANY,) * outs,
        scratch_shapes=plan.scratch,
        compiler_params=pltpu.CompilerParams(
            collective_id=cid, has_side_effects=True, vmem_limit_bytes=plan.vmem() + 4 * MIB
        ),
    )(*plan.ins)
    return plan.take(results)


def scan_tail_body(rows, length, step_ref, u_ref, b_ref, rate_ref, last_ref):
    rate = rate_ref[...]

    def advance(i, states):
        new = []
        for r in range(rows):
            keep = jnp.exp2(step_ref[r, pl.ds(i, 1), :] * rate)
            new.append(keep * states[r] + u_ref[r, pl.ds(i, 1), :] * b_ref[r, i])
        return tuple(new)

    start = tuple(jnp.zeros((DS, 128), f32) for _ in range(rows))
    end = lax.fori_loop(0, length, advance, start, unroll=4)
    for r in range(rows):
        last_ref[r] = end[r]


def scan_full_body(
    rows, length, step_ref, u_ref, b_ref, c_ref, rate_ref, entry_ref, read_ref, hist_ref
):
    rate = rate_ref[...]

    def advance(i, states):
        new = []
        for r in range(rows):
            hist_ref[r, i] = states[r]
            keep = jnp.exp2(step_ref[r, pl.ds(i, 1), :] * rate)
            h = keep * states[r] + u_ref[r, pl.ds(i, 1), :] * b_ref[r, i]
            read_ref[r, pl.ds(i, 1), :] = jnp.sum(h * c_ref[r, i], axis=0, keepdims=True)
            new.append(h)
        return tuple(new)

    lax.fori_loop(0, length, advance, tuple(entry_ref[r] for r in range(rows)), unroll=4)


def adjoint_head_body(rows, length, step_ref, dy_ref, c_ref, rate_ref, first_ref):
    rate = rate_ref[...]

    def advance(k, carried):
        i = length - 1 - k
        new = []
        for r in range(rows):
            keep = jnp.exp2(step_ref[r, pl.ds(i, 1), :] * rate)
            new.append(keep * (carried[r] + dy_ref[r, pl.ds(i, 1), :] * c_ref[r, i]))
        return tuple(new)

    start = tuple(jnp.zeros((DS, 128), f32) for _ in range(rows))
    end = lax.fori_loop(0, length, advance, start, unroll=4)
    for r in range(rows):
        first_ref[r] = end[r]


def adjoint_full_body(
    rows,
    length,
    step_ref,
    u_ref,
    dy_ref,
    b_ref,
    c_ref,
    rate_ref,
    hist_ref,
    later_ref,
    du_ref,
    dexp_ref,
    db_ref,
    dc_ref,
    drate_ref,
):
    rate = rate_ref[...]

    @pl.when(pl.program_id(1) == 0)
    def _():
        db_ref[...] = jnp.zeros_like(db_ref)
        dc_ref[...] = jnp.zeros_like(dc_ref)

    def advance(k, carried):
        i = length - 1 - k
        new = []
        drate = carried[rows]
        for r in range(rows):
            step = step_ref[r, pl.ds(i, 1), :]
            u = u_ref[r, pl.ds(i, 1), :]
            dy = dy_ref[r, pl.ds(i, 1), :]
            keep = jnp.exp2(step * rate)
            b = b_ref[r, i]
            kept = keep * hist_ref[r, i]
            g = carried[r] + dy * c_ref[r, i]
            w = g * kept
            dc_ref[r, i] += (kept + u * b) * dy
            db_ref[r, i] += g * u
            du_ref[r, pl.ds(i, 1), :] = jnp.sum(g * b, axis=0, keepdims=True)
            dexp_ref[r, pl.ds(i, 1), :] = jnp.sum(w * rate, axis=0, keepdims=True)
            drate = drate + w * step
            new.append(keep * g)
        return tuple(new) + (drate,)

    start = tuple(later_ref[r] for r in range(rows)) + (jnp.zeros((DS, 128), f32),)
    end = lax.fori_loop(0, length, advance, start, unroll=2)
    drate_ref[0] = end[rows]


def hosted_call(body, grid, in_specs, out_specs, out_shape, args, cid, plan, own_vmem, later=()):
    steps = 1
    for size in grid:
        steps *= size
    n_in, n_out, x_in, x_out = len(args), len(out_shape), len(plan.ins), len(plan.outs)

    def hosted(*refs):
        mine_in, refs = refs[:n_in], refs[n_in:]
        plan_in, refs = refs[:x_in], refs[x_in:]
        mine_out, refs = refs[:n_out], refs[n_out:]
        plan.bind(plan_in, refs[:x_out], refs[x_out:])
        at = pl.program_id(0)
        for k in range(1, len(grid)):
            at = at * grid[k] + pl.program_id(k)
        pl.when(at == 0)(plan.begin)
        for t in range(1, min(plan.hops, len(later) + 1)):
            pl.when(at == later[t - 1])(functools.partial(plan.hop_step, t))
        body(*mine_in, *mine_out)
        pl.when(at == steps - 1)(functools.partial(plan.end, 1 + len(later)))

    results = pl.pallas_call(
        hosted,
        grid=grid,
        in_specs=in_specs + [ANY] * x_in,
        out_specs=tuple(out_specs) + (ANY,) * x_out,
        out_shape=tuple(out_shape) + tuple(plan.outs),
        scratch_shapes=plan.scratch,
        compiler_params=pltpu.CompilerParams(
            vmem_limit_bytes=plan.vmem() + own_vmem, collective_id=cid, has_side_effects=True
        ),
    )(*args, *plan.ins)
    return tuple(results[:n_out]) + plan.take(results[n_out:])


def scan_call(body, args, kinds, outs, rows_all, length, width, cid, plan, later=()):
    rows = 4 if rows_all % 4 == 0 else rows_all
    single = pl.Buffered(buffer_count=1)
    grid = (rows_all // rows, width // 128)

    def spec(kind):
        extra = {"pipeline_mode": single} if kind == SPREAD else {}
        if kind == SEQ:
            return pl.BlockSpec((rows, length, 128), lambda r, g: (r, 0, g), **extra)
        if kind == SPREAD:
            return pl.BlockSpec((rows, length, DS, 128), lambda r, g: (r, 0, 0, 0), **extra)
        if kind == HIST:
            return pl.BlockSpec((rows, length, DS, 128), lambda r, g: (r, 0, 0, g), **extra)
        if kind == STATE:
            return pl.BlockSpec((rows, DS, 128), lambda r, g: (r, 0, g), **extra)
        if kind == RATE:
            return pl.BlockSpec((DS, 128), lambda r, g: (0, g), **extra)
        return pl.BlockSpec((1, DS, 128), lambda r, g: (r, 0, g), **extra)

    def block_bytes(kind):
        wide = rows * length * 128 * 4
        return {SEQ: 2 * wide, SPREAD: DS * wide, HIST: 2 * DS * wide}.get(kind, MIB // 2)

    shape_of = {
        SEQ: (rows_all, length, width),
        SPREAD: (rows_all, length, DS, 128),
        HIST: (rows_all, length, DS, width),
        STATE: (rows_all, DS, width),
        DRATE: (rows_all // rows, DS, width),
    }
    return hosted_call(
        functools.partial(body, rows, length),
        grid,
        [spec(k) for k in kinds],
        [spec(k) for k in outs],
        [jax.ShapeDtypeStruct(shape_of[k], f32) for k in outs],
        args,
        cid,
        plan,
        8 * MIB + sum(block_bytes(k) for k in tuple(kinds) + tuple(outs)),
        later,
    )


def attend_body(heads, q_ref, k_ref, v_ref, bias_ref, out_ref, total_ref):
    keys = k_ref[...].T
    for h in range(heads):
        rows = slice(h * HD, (h + 1) * HD)
        scores = jnp.dot(keys, q_ref[rows], preferred_element_type=f32)
        scores = scores * HD**-0.5 + bias_ref[...]
        peak = jnp.max(scores, axis=0, keepdims=True)
        grown = jnp.exp(scores - peak)
        total = jnp.sum(grown, axis=0, keepdims=True)
        probs = (grown * (1.0 / total)).astype(bf16)
        out_ref[rows] = jnp.dot(v_ref[...], probs, preferred_element_type=f32).astype(bf16)
        total_ref[0, h : h + 1] = peak + jnp.log(total)


def attend_back_body(
    heads, q_ref, k_ref, v_ref, bias_ref, total_ref, grad_ref, dq_ref, dk_ref, dv_ref
):
    keys = k_ref[...].T
    values = v_ref[...].T
    for h in range(heads):
        rows = slice(h * HD, (h + 1) * HD)
        scores = jnp.dot(keys, q_ref[rows], preferred_element_type=f32)
        probs = jnp.exp(scores * HD**-0.5 + bias_ref[...] - total_ref[0, h : h + 1])
        grad = jnp.dot(values, grad_ref[rows], preferred_element_type=f32)
        mean = jnp.sum(probs * grad, axis=0, keepdims=True)
        low = (probs * (grad - mean)).astype(bf16)
        dq = jnp.dot(k_ref[...], low, preferred_element_type=f32)
        dq_ref[rows] = (dq * HD**-0.5).astype(bf16)
        dk = dense_nt(q_ref[rows], low) * HD**-0.5
        dv = dense_nt(grad_ref[rows], probs.astype(bf16))
        if h == 0:
            dk_ref[...] = dk
            dv_ref[...] = dv
        else:
            dk_ref[...] += dk
            dv_ref[...] += dv


def rows_matmul(values, weight, swapped=False):
    count, tokens, depth = values.shape
    if swapped:
        tokens, depth = depth, tokens
    real, width = weight.shape
    turned = real > tokens * 8
    if turned:
        weight = weight.T

    def body(value_ref, weight_ref, out_ref):
        value = value_ref[0].T if swapped else value_ref[0][:, :real]
        product = dense_nt if turned else dense
        out_ref[0] = product(value, weight_ref[...]).astype(bf16)

    return pl.pallas_call(
        body,
        grid=(count,),
        in_specs=[
            pl.BlockSpec((1,) + values.shape[1:], lambda r: (r, 0, 0)),
            pl.BlockSpec(weight.shape, lambda r: (0, 0), pipeline_mode=pl.Buffered(buffer_count=1)),
        ],
        out_specs=pl.BlockSpec((1, tokens, width), lambda r: (r, 0, 0)),
        out_shape=jax.ShapeDtypeStruct((count, tokens, width), bf16),
        compiler_params=pltpu.CompilerParams(vmem_limit_bytes=24 * MIB),
    )(values, weight)


def rms_norm(values, gain_row):
    return (
        values * lax.rsqrt(jnp.mean(values * values, axis=-1, keepdims=True) + norm_eps) * gain_row
    )


def dense(operand, partner):
    return jnp.dot(operand, partner, preferred_element_type=f32)


def dense_tn(operand, partner):
    return lax.dot_general(
        operand, partner, (((0,), (0,)), ((), ())), preferred_element_type=f32
    )


def dense_nt(operand, partner):
    return lax.dot_general(
        operand, partner, (((1,), (1,)), ((), ())), preferred_element_type=f32
    )


def conv_silu(extended, conv_taps, same_seg):
    length_out = extended.shape[1] - CONV + 1
    summed = jnp.zeros((extended.shape[0], length_out, extended.shape[2]), f32)
    for offset in range(CONV):
        summed = summed + jnp.where(
            same_seg[offset][:, :, None],
            extended[:, offset : offset + length_out] * conv_taps[offset],
            0.0,
        )
    return jax.nn.silu(summed)


def adam_step(gradient, moments_old, weight_now):
    first_moment = beta_one * moments_old[0] + (1.0 - beta_one) * gradient
    second_moment = beta_two * moments_old[1] + (1.0 - beta_two) * gradient * gradient
    corrected = (
        first_moment
        / (1.0 - beta_one**adam_count)
        / (jnp.sqrt(second_moment / (1.0 - beta_two**adam_count)) + adam_eps)
    )
    return (second_moment, -learn_rate * (corrected + decay_rate * weight_now))


def pad_last(values, width):
    return jnp.pad(values, [(0, 0)] * (values.ndim - 1) + [(0, width - values.shape[-1])])


def column_parts(weight, parts, shards_of, width):
    own = weight.shape[1] // parts // shards_of
    return jnp.stack(
        [
            jnp.concatenate(
                [
                    pad_last(weight[:, (p * shards_of + j) * own : (p * shards_of + j + 1) * own], width)
                    for p in range(parts)
                ],
                axis=1,
            )
            for j in range(shards_of)
        ]
    )


def shards(
    tokens,
    cotangent,
    segments,
    w_qkv,
    m_qkv,
    w_attn_out,
    m_attn_out,
    w_mamba_in,
    m_mamba_in,
    w_ssm_proj,
    m_ssm_proj,
    w_mamba_out,
    m_mamba_out,
    w_gate_up,
    m_gate_up,
    w_ffn_down,
    m_ffn_down,
    ssm_vec,
    m_ssm_vec,
    embed_small,
    m_embed_small,
):
    fs, cs = lax.axis_size(FSDP), lax.axis_size(CTX)
    fi, ci = lax.axis_index(FSDP), lax.axis_index(CTX)
    tok = tokens.shape[1]
    dim = tokens.shape[2]
    row_len = segments.shape[1]
    halves = cs // fs
    reach = min(row_len // 2, WINDOW) // tok
    metas = META // cs
    chan = DI // fs
    chan_p = ceil_to(chan, 128)
    ffw = FF // fs
    ffw_p = ceil_to(ffw, 128)
    heads_dim = NH * HD
    kv_dim = KVH * HD
    groups = NH // KVH
    scale_factor = HD ** (-0.5)
    xdim = DTR + 2 * DS
    both = (FSDP, CTX)

    def row_block(weight):
        rows, cols = weight.shape[0] // halves, weight.shape[1] // fs
        return lax.dynamic_slice(
            weight, ((ci % halves) * rows, (ci // halves) * cols), (rows, cols)
        )

    def unpaired(value, width):
        return jnp.concatenate([value[0][:, :width], value[1][:, :width]], axis=1).astype(f32)

    def spread_hops(weights):
        total, done, out = sum(weights), 0, []
        for k in range(len(weights)):
            upto = (cs - 1) * sum(weights[: k + 1]) // total
            out.append(upto - done)
            done = upto
        return out

    def row_chunks(operand, partner):
        grad = dense_tn(operand, partner).astype(bf16)
        return grad.reshape(cs, 1, grad.shape[0] // cs, grad.shape[1])

    def column_chunks(operand, partner, parts=1):
        cols = partner.shape[1] // fs
        wide = jnp.concatenate(
            [
                pad_last(partner[:, j * cols : (j + 1) * cols], ceil_to(cols, 128))
                for j in range(fs)
            ],
            axis=1,
        )
        grad = dense_tn(operand, wide).astype(bf16)
        return grad.reshape(halves, parts, -1, grad.shape[1])

    def by_rows(value):
        return value.astype(bf16).reshape(fs, tok, -1)

    blocks = 25

    def in_blocks(value):
        return value.reshape(fs, 2, blocks, value.shape[1] // (2 * blocks), value.shape[2])

    mi_send = column_parts(w_mamba_in, 2, fs, chan_p)
    qkv_send = column_parts(w_qkv, 1, fs, w_qkv.shape[1] // fs)
    gain_rows = embed_small[META:]
    meta_rows = lax.dynamic_slice_in_dim(embed_small, ci * metas, metas, 0)
    source = tokens[0].astype(f32)
    normed_f, norm_pull = jax.vjp(rms_norm, source, gain_rows[0])
    normed = normed_f.astype(bf16)
    meta_f, meta_pull = jax.vjp(rms_norm, meta_rows, gain_rows[0])
    meta_low = meta_f.astype(bf16)

    normed_all, seg_all, mi_w, qkv_w = exchange(
        0,
        [
            (normed, GATHER, FSDP),
            (segments, ALL, FSDP),
            (in_blocks(mi_send), (HALF, 0, blocks), WEIGHTS),
            (in_blocks(qkv_send), (HALF, 0, blocks), WEIGHTS),
        ],
    )
    gu_send = in_hbm(in_blocks(column_parts(w_gate_up, 2, fs, ffw_p)))
    mi_w = mi_w.reshape(dim, 2 * chan_p)
    qkv_w = qkv_w.reshape(dim, -1)
    seg_all = seg_all.reshape(fs, row_len)
    seg_row = segments[0]
    normed_all = normed_all.reshape(fs * tok, dim)
    xp_w = jnp.pad(w_ssm_proj[:, :xdim], ((0, chan_p - chan), (0, 0)))
    dt_w = jnp.pad(w_ssm_proj[:, xdim:], ((0, chan_p - chan), (0, 0)))
    vec = pad_last(lax.dynamic_slice_in_dim(ssm_vec, fi * chan, chan, 1), chan_p)

    normed_rows = normed_all.reshape(fs, tok, dim)
    qkv_parts = jnp.einsum("ftd,dc->fct", normed_rows, qkv_w, preferred_element_type=f32)
    meta_part = jnp.broadcast_to(
        dense(meta_low, qkv_w).astype(bf16)[None], (fs, metas, qkv_w.shape[1])
    )
    qkv_got, meta_got = exchange(
        1, [(qkv_parts.astype(bf16), EACH, FSDP), (meta_part, EACH, FSDP)]
    )
    qkv_own = qkv_got.reshape(heads_dim + 2 * kv_dim, tok)
    queries = qkv_own[:heads_dim]
    keyval = qkv_own[heads_dim:]
    meta_own = jnp.concatenate([meta_got[j] for j in range(fs)], axis=1)[:, heads_dim:]
    kv_before, meta_kv, gu_0 = exchange(
        2,
        [
            (keyval, NEXT, CTX),
            (meta_own, ALL, CTX),
            (gu_send, (HALF, 0, 5), WEIGHTS),
        ],
        reach=reach,
    )
    kv_before = jnp.where(
        (ci - 1 - jnp.arange(reach) >= 0)[:, None, None], kv_before, jnp.zeros_like(kv_before)
    )
    key_rows = jnp.concatenate(
        [meta_kv.reshape(META, 2 * kv_dim).T]
        + [kv_before[d - 1] for d in range(reach, 0, -1)]
        + [keyval],
        axis=1,
    )

    mamba_in = dense(normed_all, mi_w).reshape(fs, tok, 2 * chan_p)
    inner_pre = mamba_in[:, :, :chan_p]
    gate_z = mamba_in[:, :, chan_p:]
    up_ring = [(c, c + 1) for c in range(cs - 1)]
    down_ring = [(c + 1, c) for c in range(cs - 1)]
    tail_rows = lax.ppermute(inner_pre[:, tok - (CONV - 1) :], CTX, up_ring)
    extended = jnp.concatenate([tail_rows, inner_pre], axis=1)
    seg_ext = lax.dynamic_slice_in_dim(
        jnp.concatenate([jnp.full((fs, CONV - 1), -1, jnp.int32), seg_all], axis=1),
        ci * tok,
        tok + CONV - 1,
        1,
    )
    own_seg = seg_ext[:, CONV - 1 :]
    same_seg = [seg_ext[:, o : o + tok] == own_seg for o in range(CONV)]
    starts = own_seg != seg_ext[:, CONV - 2 : -1]
    inner_x, conv_pull = jax.vjp(
        lambda ext_rows, taps: conv_silu(ext_rows, taps, same_seg), extended, vec[:CONV]
    )
    inner_low = inner_x.astype(bf16).reshape(fs * tok, chan_p)
    xproj_part = lax.dot_general(
        xp_w, inner_low, (((0,), (1,)), ((), ())), preferred_element_type=f32
    )
    xproj_got, attn_old = exchange(
        3,
        [
            (xproj_part, GATHER, FSDP),
            (row_block(w_attn_out), CROSS, BOTH),
        ],
    )
    xproj = jnp.sum(xproj_got, axis=0).T
    delta_low = xproj[:, :DTR].astype(bf16)
    pre_delta = dense_nt(delta_low, dt_w).reshape(fs, tok, chan_p) + vec[CONV]
    step = jax.nn.softplus(pre_delta)
    step_far = jnp.where(starts[:, :, None], FAR, step)
    drive = step * inner_x

    def spread(columns):
        return jnp.broadcast_to(columns.reshape(fs, tok, DS, 1), (fs, tok, DS, 128))

    b_wide = spread(xproj[:, DTR : DTR + DS])
    c_wide = spread(xproj[:, DTR + DS : xdim])
    rate = -jnp.exp(vec[CONV + 2 :])
    rate2 = rate * LOG2E
    sizes = (fs, tok, chan_p)
    last_state, ssm_proj_old = scan_call(
        scan_tail_body,
        (step_far, drive, b_wide, rate2),
        (SEQ, SEQ, SPREAD, RATE),
        (STATE,),
        *sizes,
        cid=19,
        plan=Traffic([(row_block(w_ssm_proj), CROSS, BOTH)]),
    )
    step_sum = jnp.sum(step_far, axis=1)
    state_before, sums, gu_2 = exchange(
        4,
        [
            (last_state.astype(bf16), NEXT, CTX),
            (step_sum, ALL, CTX),
            (gu_send, (HALF, 10, 19), WEIGHTS),
        ],
        reach=reach,
    )

    def decay_of(block):
        total = lax.dynamic_index_in_dim(sums, jnp.clip(block, 0, cs - 1), 0, keepdims=False)
        return jnp.exp2(total[:, None, :] * rate2)

    entry = jnp.zeros((fs, DS, chan_p), f32)
    for d in range(reach, 0, -1):
        there = jnp.where(ci >= d, state_before[d - 1].astype(f32), 0.0)
        entry = decay_of(ci - d) * entry + there
    readout, hist, mamba_out_old = scan_call(
        scan_full_body,
        (step_far, drive, b_wide, c_wide, rate2, entry),
        (SEQ, SEQ, SPREAD, SPREAD, RATE, STATE),
        (SEQ, HIST),
        *sizes,
        cid=20,
        plan=Traffic([(row_block(w_mamba_out), CROSS, BOTH)]),
    )
    skip = vec[CONV + 1]
    pre_mix = readout + skip * inner_x
    gate_s = jax.nn.sigmoid(gate_z)
    gate_silu = gate_z * gate_s
    mixture_low = (pre_mix * gate_silu).astype(bf16).reshape(fs * tok, chan_p)
    ssm_part = rows_matmul(mixture_low.reshape(fs, tok, chan_p), w_mamba_out)

    key_span = (reach + 1) * tok
    padded_seg = jnp.concatenate([jnp.full((reach * tok,), -1, jnp.int32), seg_row])
    key_seg = lax.dynamic_slice_in_dim(padded_seg, ci * tok, key_span, 0)
    query_seg = lax.dynamic_slice_in_dim(seg_row, ci * tok, tok, 0)
    query_pos = jnp.arange(tok, dtype=jnp.int32) + reach * tok
    key_pos = jnp.arange(key_span, dtype=jnp.int32)
    allowed = (
        (key_seg[:, None] == query_seg[None, :])
        & (key_pos[:, None] <= query_pos[None, :])
        & (query_pos[None, :] - key_pos[:, None] < WINDOW)
    )
    allowed = jnp.concatenate([jnp.ones((META, tok), jnp.bool_), allowed], axis=0)
    bias = jnp.where(allowed, 0.0, -1e30)
    seen = META + key_span
    q_spec = pl.BlockSpec((groups * HD, tok), lambda g: (g, 0))
    k_spec = pl.BlockSpec((HD, seen), lambda g: (g, 0))
    v_spec = pl.BlockSpec((HD, seen), lambda g: (g + KVH, 0))
    bias_spec = pl.BlockSpec((seen, tok), lambda g: (0, 0))
    total_spec = pl.BlockSpec((1, groups, tok), lambda g: (g, 0, 0))
    attended, log_totals, gu_1, ffn_down_old = hosted_call(
        functools.partial(attend_body, groups),
        (KVH,),
        [q_spec, k_spec, v_spec, bias_spec],
        [q_spec, total_spec],
        [
            jax.ShapeDtypeStruct((heads_dim, tok), bf16),
            jax.ShapeDtypeStruct((KVH, groups, tok), f32),
        ],
        (queries, key_rows, key_rows, bias),
        16,
        Traffic([(gu_send, (HALF, 5, 10), WEIGHTS), (row_block(w_ffn_down), CROSS, BOTH)]),
        12 * MIB,
    )
    wide = heads_dim // fs
    att_got, gu_3 = exchange(
        5,
        [
            (attended.reshape(fs, wide, tok), EACH, FSDP),
            (gu_send, (HALF, 19, 25), WEIGHTS),
        ],
    )
    gu_w = jnp.concatenate([gu_0, gu_1, gu_2, gu_3], axis=2).reshape(dim, 2 * ffw_p)
    att_tp = jnp.swapaxes(att_got, 1, 2).reshape(fs * tok, wide)
    attn_part = rows_matmul(att_got, w_attn_out, True)
    attn_got, ssm_got = exchange(
        6, [(attn_part, REDUCE, FSDP), (ssm_part, REDUCE, FSDP)]
    )
    attn_proj = jnp.sum(attn_got.astype(f32), axis=0)
    ssm_proj = jnp.sum(ssm_got.astype(f32), axis=0)
    attn_branch, attn_pull = jax.vjp(rms_norm, attn_proj, gain_rows[1])
    ssm_branch, ssm_norm_pull = jax.vjp(rms_norm, ssm_proj, gain_rows[2])
    residual = source + 0.5 * (attn_branch + ssm_branch)
    ffn_in_f, ffn_norm_pull = jax.vjp(rms_norm, residual, gain_rows[3])
    ffn_in, cot_all = exchange(
        7, [(ffn_in_f.astype(bf16), GATHER, FSDP), (cotangent[0], GATHER, FSDP)]
    )
    cot_all = cot_all.reshape(fs * tok, dim)
    ffn_in = ffn_in.reshape(fs * tok, dim)

    gate_up = dense(ffn_in, gu_w)
    hidden_f, glu_pull = jax.vjp(
        lambda values: jax.nn.silu(values[:, :ffw_p]) * values[:, ffw_p:], gate_up
    )
    hidden_wide = hidden_f.astype(bf16)
    hidden = hidden_wide[:, :ffw]
    down_part = rows_matmul(hidden_wide.reshape(fs, tok, ffw_p), w_ffn_down)
    hidden_grad = pad_last(dense_nt(cot_all, w_ffn_down), ffw_p)
    gate_up_grad = glu_pull(hidden_grad)[0].astype(bf16)
    ring_one = Ring(
        [
            row_chunks(ffn_in, gate_up_grad[:, :ffw_p]),
            row_chunks(ffn_in, gate_up_grad[:, ffw_p:]),
            column_chunks(hidden, cot_all, 2),
        ],
        [(0, 0, 1), (1, 0, -1), (2, 0, 1), (2, 1, -1)],
    )
    hops = spread_hops([1, 1, 1, 1, 2, 1])
    ffn_back = by_rows(dense_nt(gate_up_grad, gu_w))
    (back_got,) = exchange(8, [(ffn_back, REDUCE, FSDP)], ring_one, hops[0])
    resid_part, gain_ffn_grad = ffn_norm_pull(jnp.sum(back_got.astype(f32), axis=0))
    residual_grad = cotangent[0].astype(f32) + resid_part
    branch_grad = 0.5 * residual_grad
    attn_proj_grad, gain_attn_grad = attn_pull(branch_grad)
    ssm_proj_grad, gain_ssm_grad = ssm_norm_pull(branch_grad)
    branch_low = (attn_proj_grad.astype(bf16), ssm_proj_grad.astype(bf16))
    attn_proj_low, ssm_proj_low = exchange(
        9,
        [(branch_low[0], GATHER, FSDP), (branch_low[1], GATHER, FSDP)],
        ring_one,
        hops[1],
    )
    attn_proj_low = attn_proj_low.reshape(fs * tok, dim)
    ssm_proj_low = ssm_proj_low.reshape(fs * tok, dim)
    att_grad_tp = jnp.einsum(
        "ftd,cd->fct",
        attn_proj_low.reshape(fs, tok, dim),
        w_attn_out,
        preferred_element_type=f32,
    ).astype(bf16)
    (att_grad_got,) = exchange(10, [(att_grad_tp, EACH, FSDP)], ring_one, hops[2])

    def own_pair(held, part):
        piece = lax.dynamic_slice_in_dim(held, ci * (dim // cs), dim // cs, 0)
        return jnp.stack([piece[:, :part], piece[:, part:]])

    qkv_old = lax.dynamic_slice_in_dim(qkv_w, ci * (dim // cs), dim // cs, 0)
    attended_grad = att_grad_got.reshape(heads_dim, tok)

    query_grad, key_grad, value_grad, mamba_in_old = hosted_call(
        functools.partial(attend_back_body, groups),
        (KVH,),
        [q_spec, k_spec, v_spec, bias_spec, total_spec, q_spec],
        [q_spec, k_spec, k_spec],
        [
            jax.ShapeDtypeStruct((heads_dim, tok), bf16),
            jax.ShapeDtypeStruct((kv_dim, seen), f32),
            jax.ShapeDtypeStruct((kv_dim, seen), f32),
        ],
        (queries, key_rows, key_rows, bias, log_totals, attended_grad),
        24,
        Traffic([(own_pair(mi_w, chan_p), PAIR, FSDP)], ring_one, hops[3]),
        16 * MIB,
    )
    kv_grad_all = jnp.concatenate([key_grad, value_grad], axis=0)
    kv_send = jnp.stack(
        [
            kv_grad_all[:, META + (reach - d) * tok : META + (reach - d + 1) * tok]
            for d in range(1, reach + 1)
        ]
    ).astype(bf16)
    meta_send = kv_grad_all[:, :META].T.astype(bf16).reshape(cs, metas, 2 * kv_dim)
    kv_back, meta_back, down_got = exchange(
        13,
        [
            (kv_send, BACK, CTX),
            (meta_send, EACH, CTX),
            (down_part, REDUCE, FSDP),
        ],
        ring_one,
        hops[4],
        reach,
    )
    output = residual + jnp.sum(down_got.astype(f32), axis=0)
    own_kv_grad = kv_grad_all[:, META + reach * tok :]
    for d in range(1, reach + 1):
        own_kv_grad = own_kv_grad + jnp.where(ci + d < cs, kv_back[d - 1].astype(f32), 0.0)
    meta_kv_grad = jnp.sum(meta_back.astype(f32), axis=0).astype(bf16)
    meta_grad_parts = column_parts(
        jnp.pad(meta_kv_grad, ((0, 0), (heads_dim, 0))), 1, fs, qkv_w.shape[1]
    )
    qkv_grad = jnp.concatenate([query_grad, own_kv_grad.astype(bf16)], axis=0)
    qkv_grad_tp, meta_grad_tp = exchange(
        14,
        [
            (qkv_grad.reshape(fs, -1, tok), EACH, FSDP),
            (meta_grad_parts, EACH, FSDP),
        ],
        ring_one,
        hops[5],
    )

    mixture_grad = pad_last(dense_nt(ssm_proj_low, w_mamba_out), chan_p).reshape(fs, tok, chan_p)
    read_grad = mixture_grad * gate_silu
    gate_grad = mixture_grad * pre_mix * (gate_s * (1.0 + gate_z * (1.0 - gate_s)))
    gate_low = gate_grad.astype(bf16).reshape(fs * tok, chan_p)
    qkv_full = jnp.einsum("ftd,fct->dc", normed_rows, qkv_grad_tp, preferred_element_type=f32)
    qkv_full = qkv_full + jnp.einsum(
        "md,fmc->dc", meta_low, meta_grad_tp, preferred_element_type=f32
    )
    ring_two = Ring(
        [
            row_chunks(normed_all, gate_low),
            qkv_full.astype(bf16).reshape(cs, 1, dim // cs, qkv_w.shape[1]),
            column_chunks(att_tp, attn_proj_low),
            column_chunks(mixture_low[:, :chan], ssm_proj_low),
        ],
        [(0, 0, 1), (1, 0, 1), (2, 0, -1), (3, 0, -1)],
    )
    hops = spread_hops([1, 2, 2, 2])
    gate_sum, up_sum, down_top, down_low = ring_one.finish()
    first_adj, gate_up_old = scan_call(
        adjoint_head_body,
        (step_far, read_grad, c_wide, rate2),
        (SEQ, SEQ, SPREAD, RATE),
        (STATE,),
        *sizes,
        cid=21,
        plan=Traffic([(own_pair(gu_w, ffw_p), PAIR, FSDP)], ring_two, hops[0]),
    )
    adj_after, gate_up_sum = exchange(
        11,
        [
            (first_adj.astype(bf16), PREV, CTX),
            (jnp.stack([gate_sum, up_sum]).astype(bf16), PAIR, FSDP),
        ],
        ring_two,
        hops[1],
        reach,
    )
    gate_up_old = unpaired(gate_up_old, ffw)
    mamba_in_old = unpaired(mamba_in_old, chan)
    later = jnp.zeros((fs, DS, chan_p), f32)
    for d in range(reach, 0, -1):
        there = jnp.where(ci + d < cs, adj_after[d - 1].astype(f32), 0.0)
        later = decay_of(ci + d) * later + there
    drive_grad, exp_grad, b_acc, c_acc, rate_grad = scan_call(
        adjoint_full_body,
        (step_far, drive, read_grad, b_wide, c_wide, rate2, hist, later),
        (SEQ, SEQ, SEQ, SPREAD, SPREAD, RATE, HIST, STATE),
        (SEQ, SEQ, SPREAD, SPREAD, DRATE),
        *sizes,
        cid=22,
        plan=Traffic([], ring_two, hops[2]),
        later=(3,) if hops[2] == 2 else (),
    )
    cross = [
        (f * cs + c, (c // halves) * cs + halves * f + c % halves)
        for f in range(fs)
        for c in range(cs)
    ]
    down_both = jnp.concatenate([down_top, down_low], axis=0).astype(bf16)
    drive_grad, down_both = together(drive_grad, down_both)
    down_sum = lax.ppermute(down_both, (FSDP, CTX), cross)
    step_grad = drive_grad * inner_x + exp_grad * LN2
    pre_delta_grad = step_grad * jax.nn.sigmoid(pre_delta)
    inner_grad = drive_grad * step + skip * read_grad
    small_grad = jnp.concatenate(
        [
            jnp.sum(pre_delta_grad, axis=(0, 1))[None],
            jnp.sum(inner_x * read_grad, axis=(0, 1))[None],
            jnp.sum(rate_grad, axis=0) * rate,
        ],
        axis=0,
    )
    pre_delta_low = pre_delta_grad.astype(bf16).reshape(fs * tok, chan_p)
    xgrad_part = jnp.concatenate(
        [
            lax.dot_general(
                dt_w, pre_delta_low, (((0,), (1,)), ((), ())), preferred_element_type=f32
            ),
            jnp.sum(b_acc, axis=-1).reshape(fs * tok, DS).T,
            jnp.sum(c_acc, axis=-1).reshape(fs * tok, DS).T,
        ],
        axis=0,
    )
    (xgrad_got,) = exchange(12, [(xgrad_part, GATHER, FSDP)], ring_two, hops[3])
    xproj_grad = jnp.sum(xgrad_got, axis=0).T.astype(bf16)
    inner_grad = inner_grad + dense_nt(xproj_grad, xp_w).reshape(fs, tok, chan_p)
    ext_grad, taps_grad = conv_pull(inner_grad)
    returned = lax.ppermute(ext_grad[:, : CONV - 1].astype(bf16), CTX, down_ring).astype(f32)
    inner_pre_grad = ext_grad[:, CONV - 1 :] + jnp.pad(
        returned, ((0, 0), (tok - (CONV - 1), 0), (0, 0))
    )
    inner_pre_low = inner_pre_grad.astype(bf16).reshape(fs * tok, chan_p)
    mamba_in_grad = jnp.concatenate([inner_pre_low, gate_low], axis=1)
    split = ceil_to(chan_p * 9 // 16, 128)
    ring_three = Ring(
        [
            row_chunks(normed_all, inner_pre_low[:, :split]),
            row_chunks(normed_all, inner_pre_low[:, split:]),
            column_chunks(
                jnp.concatenate([inner_low[:, :chan], pre_delta_low[:, :chan]], axis=0),
                jnp.concatenate(
                    [
                        jnp.pad(xproj_grad, ((0, 0), (0, DTR))),
                        jnp.pad(delta_low, ((0, 0), (xdim, 0))),
                    ],
                    axis=0,
                ),
            ),
        ],
        [(0, 0, 1), (1, 0, -1), (2, 0, -1)],
    )
    vec_grad = jnp.concatenate([taps_grad, small_grad], axis=0)
    token_back = jnp.einsum("fct,dc->ftd", qkv_grad_tp, qkv_w, preferred_element_type=f32)
    token_back = token_back + dense_nt(mamba_in_grad, mi_w).reshape(fs, tok, dim)
    meta_back_rows = jnp.einsum("fmc,dc->fmd", meta_grad_tp, qkv_w, preferred_element_type=f32)
    token_back = by_rows(token_back)
    hops = spread_hops([3, 2, 2])
    token_got, meta_rows_got = exchange(
        15,
        [(token_back, REDUCE, FSDP), (meta_back_rows.astype(bf16), REDUCE, FSDP)],
        ring_three,
        hops[0],
    )
    source_part, gain_in_grad = norm_pull(jnp.sum(token_got.astype(f32), axis=0))
    source_grad = residual_grad + source_part
    meta_grad, gain_in_meta = meta_pull(jnp.sum(meta_rows_got.astype(f32), axis=0))
    embed_part = jnp.concatenate(
        [
            meta_grad,
            jnp.stack([gain_in_grad + gain_in_meta, gain_attn_grad, gain_ssm_grad, gain_ffn_grad]),
        ],
        axis=0,
    )
    (embed_rows,) = exchange(17, [(embed_part, GATHER, FSDP)], ring_three, hops[1])
    embed_got, vec_got = exchange(
        18,
        [
            (jnp.sum(embed_rows, axis=0).astype(bf16), LINE, CTX),
            (vec_grad.astype(bf16), LINE, CTX),
        ],
        ring_three,
        hops[2],
    )
    embed_got = embed_got.astype(f32)
    vec_part = jnp.sum(vec_got.astype(f32), axis=0)
    embed_total = jnp.concatenate(
        [embed_got[:, :metas].reshape(META, dim), jnp.sum(embed_got[:, metas:], axis=0)], axis=0
    )
    gate_half, qkv_gradient, attn_sum, mamba_out_sum = ring_two.finish()
    inner_a, inner_b, proj_sum = ring_three.finish()
    mamba_in_sum, attn_sum, mamba_out_sum, proj_sum, vec_all = exchange(
        23,
        [
            (
                jnp.stack([jnp.concatenate([inner_a, inner_b], axis=1), gate_half]).astype(bf16),
                PAIR,
                FSDP,
            ),
            (attn_sum.astype(bf16), CROSS, BOTH),
            (mamba_out_sum.astype(bf16), CROSS, BOTH),
            (proj_sum.astype(bf16), CROSS, BOTH),
            (vec_part, GATHER, FSDP),
        ],
    )
    ssm_total = jnp.concatenate([vec_all[j, :, :chan] for j in range(fs)], axis=1)
    gate_up_gradient = unpaired(gate_up_sum, ffw)
    mamba_in_gradient = unpaired(mamba_in_sum, chan)
    ffn_down_gradient = down_sum[:, : dim // fs].astype(f32)
    attn_gradient = attn_sum[:, : dim // fs].astype(f32)
    mamba_out_gradient = mamba_out_sum[:, : dim // fs].astype(f32)
    ssm_proj_gradient = proj_sum[:, : w_ssm_proj.shape[1] // fs].astype(f32)

    def adam_block(gradient, moments_old, weight):
        return adam_step(gradient, moments_old, weight.astype(f32))

    qkv_moments, qkv_update = adam_block(qkv_gradient, m_qkv, qkv_old)
    attn_moments, attn_update = adam_block(attn_gradient, m_attn_out, attn_old)
    mamba_in_moments, mamba_in_update = adam_block(mamba_in_gradient, m_mamba_in, mamba_in_old)
    ssm_proj_moments, ssm_proj_update = adam_block(ssm_proj_gradient, m_ssm_proj, ssm_proj_old)
    mamba_out_moments, mamba_out_update = adam_block(
        mamba_out_gradient, m_mamba_out, mamba_out_old
    )
    gate_up_moments, gate_up_update = adam_block(gate_up_gradient, m_gate_up, gate_up_old)
    ffn_down_moments, ffn_down_update = adam_block(ffn_down_gradient, m_ffn_down, ffn_down_old)
    ssm_vec_moments, ssm_vec_update = adam_step(ssm_total, m_ssm_vec, ssm_vec)
    embed_moments, embed_update = adam_step(embed_total, m_embed_small, embed_small)
    return (
        output.astype(jnp.bfloat16)[None],
        source_grad[None],
        qkv_gradient,
        qkv_moments,
        qkv_update,
        attn_gradient,
        attn_moments,
        attn_update,
        mamba_in_gradient,
        mamba_in_moments,
        mamba_in_update,
        ssm_proj_gradient,
        ssm_proj_moments,
        ssm_proj_update,
        mamba_out_gradient,
        mamba_out_moments,
        mamba_out_update,
        gate_up_gradient,
        gate_up_moments,
        gate_up_update,
        ffn_down_gradient,
        ffn_down_moments,
        ffn_down_update,
        ssm_total,
        ssm_vec_moments,
        ssm_vec_update,
        embed_total,
        embed_moments,
        embed_update,
    )


def solution(mesh):
    in_specs = (
        P(FSDP, CTX, None),
        P(FSDP, CTX, None),
        P(FSDP, None),
        P(FSDP, None),
        P(None, CTX, FSDP),
        P(FSDP, None),
        P(None, CTX, FSDP),
        P(FSDP, None),
        P(None, CTX, FSDP),
        P(FSDP, None),
        P(None, CTX, FSDP),
        P(FSDP, None),
        P(None, CTX, FSDP),
        P(FSDP, None),
        P(None, CTX, FSDP),
        P(FSDP, None),
        P(None, CTX, FSDP),
        P(),
        P(),
        P(),
        P(),
    )
    out_specs = (
        P(FSDP, CTX, None),
        P(FSDP, CTX, None),
        P(CTX, FSDP),
        P(CTX, FSDP),
        P(CTX, FSDP),
        P(CTX, FSDP),
        P(CTX, FSDP),
        P(CTX, FSDP),
        P(CTX, FSDP),
        P(CTX, FSDP),
        P(CTX, FSDP),
        P(CTX, FSDP),
        P(CTX, FSDP),
        P(CTX, FSDP),
        P(CTX, FSDP),
        P(CTX, FSDP),
        P(CTX, FSDP),
        P(CTX, FSDP),
        P(CTX, FSDP),
        P(CTX, FSDP),
        P(CTX, FSDP),
        P(CTX, FSDP),
        P(CTX, FSDP),
        P(),
        P(),
        P(),
        P(),
        P(),
        P(),
    )
    return jax.shard_map(shards, mesh=mesh, in_specs=in_specs, out_specs=out_specs, check_vma=False)
```

```python
import functools

import jax
import jax.numpy as jnp
from jax import lax
from jax.experimental import pallas as pl
from jax.experimental.pallas import tpu as pltpu
from jax.sharding import PartitionSpec as P

NH = 25
KVH = 5
HD = 64
DI = 3200
DS = 16
DTR = 100
FF = 5504
META = 128
CONV = 4
WINDOW = 1024

norm_eps = 1e-05
beta_one = 0.9
beta_two = 0.95
learn_rate = 0.01
decay_rate = 0.1
adam_eps = 1e-08
adam_count = 10.0

FSDP = "fsdp"
CTX = "ctx"
EACH = "each"
ALL = "all"
GATHER = "gather"
REDUCE = "reduce"
HALF = "half"
WEIGHTS = "weights"
BOTH = "both"
CROSS = "cross"
PAIR = "pair"
NEXT = "next"
PREV = "prev"
BACK = "back"
LINE = "line"
SEQ = "seq"
SPREAD = "spread"
HIST = "hist"
STATE = "state"
RATE = "rate"
DRATE = "drate"
RING = "ring"
LOG2E = 1.4426950408889634
LN2 = 0.6931471805599453
FAR = 1e30
bf16 = jnp.bfloat16
f32 = jnp.float32
ANY = pl.BlockSpec(memory_space=pltpu.HBM)
MIB = 1024 * 1024


def together(*values):
    return lax.optimization_barrier(values)


def ceil_to(value, unit):
    return (value + unit - 1) // unit * unit


def span_of(axis):
    return lax.axis_size(axis), lax.axis_index(axis)


def ring_spot(ci, cs):
    odd = lax.rem(ci, 2)
    return (ci // 2) * (1 - odd) + (cs - 1 - ci // 2) * odd


def ring_block(spot, cs):
    spot = lax.rem(spot + 2 * cs, cs)
    far = spot // (cs // 2)
    return 2 * spot * (1 - far) + (2 * (cs - 1 - spot) + 1) * far


def when(condition, action):
    if condition is None:
        action()
    else:
        pl.when(condition)(action)


def in_hbm(value):
    return pltpu.with_memory_space_constraint(value, pltpu.HBM)


def piece_edges(mode):
    count = mode[2] - mode[1]
    groups = 5 if count > 10 else 3
    edges = [count * k // groups for k in range(groups + 1)]
    return list(zip(edges[:-1], edges[1:]))


def chunk_shape(value, cs):
    lead, _, rows, cols = value.shape
    return (rows, cols if lead == cs else cols * lead // cs)


def chunk_ref(ref, block, part, cs):
    lead = ref.shape[0]
    if lead == cs:
        return ref.at[block, part]
    cols = ref.shape[3] * lead // cs
    columns = pl.ds(pl.multiple_of(block // lead * cols, 128), cols)
    return ref.at[lax.rem(block, lead), part, :, columns]


class Ring:
    def __init__(self, chunks, uses):
        self.chunks, self.uses = chunks, uses
        self.got, self.hop = [], 0

    def finish(self):
        cs, block = span_of(CTX)
        sums = []
        for (k, part, _), got in zip(self.uses, self.got):
            value = self.chunks[k]
            if value.shape[0] == cs:
                own = lax.dynamic_index_in_dim(value, block, 0, keepdims=False)[part]
            else:
                rows, cols = chunk_shape(value, cs)
                at = (block % value.shape[0], part, 0, block // value.shape[0] * cols)
                own = lax.dynamic_slice(value, at, (1, 1, rows, cols))[0, 0]
            sums.append(got.astype(f32) + own.astype(f32))
        return sums


class Traffic:
    def __init__(self, items, ring=None, hops=0, reach=0):
        self.items, self.ring, self.reach = items, ring, reach
        fs, cs = lax.axis_size(FSDP), lax.axis_size(CTX)
        self.hops = min(hops, cs - 1 - ring.hop) if ring is not None else 0
        self.ins = [value for value, _, _ in items]
        self.outs = []
        dma = pltpu.SemaphoreType.DMA
        most = 2 * max(fs, cs)
        count = max(len(items), 1)
        self.scratch = [dma((count, most)), dma((count, most)), dma((count, 2))]
        self.places = {}

        def own_scratch(k, shapes):
            self.places[k] = len(self.scratch)
            self.scratch += shapes

        for k, (value, mode, axis) in enumerate(items):
            shape = value.shape
            if mode in (ALL, GATHER, LINE):
                shape = (lax.axis_size(axis),) + shape
            elif mode in (NEXT, PREV):
                shape = (reach,) + shape
            elif mode == REDUCE:
                shape = (fs // 2,) + shape[1:]
                own_scratch(k, [pltpu.VMEM(shape, value.dtype)] * 2 + [dma((fs // 2,))])
            elif mode[0] == HALF:
                pieces = len(piece_edges(mode))
                shape = shape[:2] + (mode[2] - mode[1],) + shape[3:]
                own_scratch(k, [dma((pieces, 2 * fs)), dma((pieces, 2 * fs))])
            self.outs.append(jax.ShapeDtypeStruct(shape, value.dtype))
        if self.hops:
            self.ins += [in_hbm(value) for value in ring.chunks + ring.got]
            uses = len(ring.uses)
            shapes = [dma((uses, self.hops)), dma((uses, self.hops)), dma((uses, self.hops, 2))]
            for k, _, _ in ring.uses:
                shape = chunk_shape(ring.chunks[k], cs)
                self.outs += [pltpu.HBM(shape, bf16)] * self.hops
                shapes.append(pltpu.VMEM((self.hops, 2) + shape, bf16))
            own_scratch(RING, shapes)

    def vmem(self):
        total = 4 * MIB
        for held in self.scratch:
            if held.memory_space == pltpu.VMEM:
                size = 2
                for extent in held.shape[:-2]:
                    size *= extent
                total += size * ceil_to(held.shape[-2], 16) * ceil_to(held.shape[-1], 128)
        return total

    def bind(self, ins, outs, scratch):
        self.in_refs, self.out_refs, self.sems = ins, outs, scratch

    def remote(self, source, target, send, take, peer):
        return pltpu.make_async_remote_copy(
            src_ref=source,
            dst_ref=target,
            send_sem=send,
            recv_sem=take,
            device_id=peer,
            device_id_type=pl.DeviceIdType.MESH,
        )

    def greet(self):
        barrier = pltpu.get_barrier_semaphore()
        fs, fi = span_of(FSDP)
        cs, ci = span_of(CTX)

        def signal(peer):
            pl.semaphore_signal(
                barrier, inc=1, device_id=peer, device_id_type=pl.DeviceIdType.MESH
            )

        axes = {axis for _, _, axis in self.items}
        if WEIGHTS in axes:
            axes.add(FSDP)
        total = 0
        for axis in (FSDP, CTX):
            if axis in axes:
                n, me = span_of(axis)
                for d in range(1, n):
                    signal({axis: lax.rem(me + d, n)})
                total += n - 1
        if self.hops and CTX not in axes:
            spot = ring_spot(ci, cs)
            signal({CTX: ring_block(spot + 1, cs)})
            signal({CTX: ring_block(spot - 1, cs)})
            total += 2
        if WEIGHTS in axes and CTX not in axes:
            signal({CTX: ci + 1 - 2 * lax.rem(ci, 2)})
            total += 1
        if BOTH in axes:
            halves = cs // fs
            away = ci // halves != fi

            def meet():
                signal({FSDP: ci // halves, CTX: halves * fi + lax.rem(ci, halves)})

            pl.when(away)(meet)
            if total:
                pl.semaphore_wait(barrier, total + jnp.where(away, 1, 0))
            else:
                pl.when(away)(lambda: pl.semaphore_wait(barrier, 1))
        else:
            pl.semaphore_wait(barrier, total)

    def copies(self):
        starts, relays, waits = [], [], []
        fs, fi = span_of(FSDP)
        cs, ci = span_of(CTX)
        send_sem, take_sem, own_sem = self.sems[:3]
        for k, (_, mode, axis) in enumerate(self.items):
            src, dst = self.in_refs[k], self.out_refs[k]

            def add(copy, sends=None, takes=None):
                starts.append((copy.start, sends))
                waits.append((copy.wait_send, sends))
                waits.append((copy.wait_recv, takes))

            def keep(copy, condition=None):
                starts.append((copy.start, condition))
                waits.append((copy.wait, condition))

            core, chip, chips = lax.rem(fi, 2), fi // 2, fs // 2
            mate = {FSDP: fi + 1 - 2 * core}

            def relay(first, second):
                starts.append((first.start, None))
                relays.append((first.wait_recv, None))
                relays.append((second.start, None))
                waits.append((first.wait_send, None))
                waits.append((second.wait_send, None))
                waits.append((second.wait_recv, None))

            if mode == GATHER:
                for d in range(1, chips):
                    to = 2 * lax.rem(chip + d, chips) + core
                    came = 2 * lax.rem(chip + chips - d, chips) + core
                    relay(
                        self.remote(
                            src, dst.at[fi], send_sem.at[k, d], take_sem.at[k, d], {FSDP: to}
                        ),
                        self.remote(
                            dst.at[came],
                            dst.at[came],
                            send_sem.at[k, chips + d],
                            take_sem.at[k, chips + d],
                            mate,
                        ),
                    )
                add(self.remote(src, dst.at[fi], send_sem.at[k, 0], take_sem.at[k, 0], mate))
                keep(pltpu.make_async_copy(src, dst.at[fi], own_sem.at[k, 0]))
            elif mode == LINE:
                across = {CTX: ci + 1 - 2 * lax.rem(ci, 2)}
                for d in range(1, cs // 2):
                    came = lax.rem(ci + cs - 2 * d, cs)
                    relay(
                        self.remote(
                            src,
                            dst.at[ci],
                            send_sem.at[k, d],
                            take_sem.at[k, d],
                            {CTX: lax.rem(ci + 2 * d, cs)},
                        ),
                        self.remote(
                            dst.at[came],
                            dst.at[came],
                            send_sem.at[k, cs // 2 + d],
                            take_sem.at[k, cs // 2 + d],
                            across,
                        ),
                    )
                add(self.remote(src, dst.at[ci], send_sem.at[k, 0], take_sem.at[k, 0], across))
                keep(pltpu.make_async_copy(src, dst.at[ci], own_sem.at[k, 0]))
            elif mode == REDUCE:
                mine, other, load_sem = self.sems[self.places[k] : self.places[k] + 3]
                for d in list(range(1, chips)) + [0]:
                    to = lax.rem(chip + d, chips)
                    first = self.remote(
                        src.at[2 * to + 1 - core],
                        other.at[to],
                        send_sem.at[k, d],
                        take_sem.at[k, d],
                        mate,
                    )
                    load = pltpu.make_async_copy(
                        src.at[2 * to + core], mine.at[to], load_sem.at[d]
                    )
                    starts.append((first.start, None))
                    starts.append((load.start, None))
                    relays.append((load.wait, None))
                    relays.append((first.wait_recv, None))
                    waits.append((first.wait_send, None))

                    def total(mine=mine, other=other, to=to):
                        mine[to] = mine[to] + other[to]

                    relays.append((total, None))
                    if d:
                        second = self.remote(
                            mine.at[to],
                            dst.at[chip],
                            send_sem.at[k, chips + d],
                            take_sem.at[k, chips + d],
                            {FSDP: 2 * to + core},
                        )
                        waits.append((second.wait_send, None))
                        waits.append((second.wait_recv, None))
                    else:
                        second = pltpu.make_async_copy(mine.at[to], dst.at[to], own_sem.at[k, 0])
                        waits.append((second.wait, None))
                    relays.append((second.start, None))
            elif mode[0] == HALF:
                piece_send, piece_take = self.sems[self.places[k] : self.places[k] + 2]
                side = lax.rem(ci, 2)
                across = {CTX: ci + 1 - 2 * side}
                for q, (low, high) in enumerate(piece_edges(mode)):
                    for d in range(1, chips):
                        for b in range(2):
                            to = 2 * lax.rem(chip + d, chips) + lax.rem(core + b, 2)
                            came = 2 * lax.rem(chip + chips - d, chips) + lax.rem(core + b, 2)
                            e = 2 * d + b
                            relay(
                                self.remote(
                                    src.at[to, side, mode[1] + low : mode[1] + high],
                                    dst.at[fi, side, low:high],
                                    piece_send.at[q, e],
                                    piece_take.at[q, e],
                                    {FSDP: to},
                                ),
                                self.remote(
                                    dst.at[came, side, low:high],
                                    dst.at[came, side, low:high],
                                    piece_send.at[q, fs + e],
                                    piece_take.at[q, fs + e],
                                    across,
                                ),
                            )
                for b in range(2):
                    to = mate[FSDP]
                    add(
                        self.remote(
                            src.at[to, b, mode[1] : mode[2]],
                            dst.at[fi, b],
                            send_sem.at[k, b],
                            take_sem.at[k, b],
                            mate,
                        )
                    )
                    keep(
                        pltpu.make_async_copy(
                            src.at[fi, b, mode[1] : mode[2]], dst.at[fi, b], own_sem.at[k, b]
                        )
                    )
            elif mode in (ALL, EACH):
                n, me = span_of(axis)
                for d in range(1, n):
                    peer = lax.rem(me + d, n)
                    source = src.at[peer] if mode == EACH else src
                    add(
                        self.remote(
                            source, dst.at[me], send_sem.at[k, d], take_sem.at[k, d], {axis: peer}
                        )
                    )
                source = src.at[me] if mode == EACH else src
                keep(pltpu.make_async_copy(source, dst.at[me], own_sem.at[k, 0]))
            elif mode == PAIR:
                for p in range(2):
                    peer = (p * fs + fi) // 2
                    slot = lax.rem(fi, 2)
                    away = peer != fi
                    q = 2 * fi + p
                    comes = lax.rem(q, fs) != fi
                    copy = self.remote(
                        src.at[p],
                        dst.at[slot],
                        send_sem.at[k, p],
                        take_sem.at[k, slot],
                        {FSDP: peer},
                    )
                    starts.append((copy.start, away))
                    waits.append((copy.wait_send, away))
                    taken = self.remote(
                        src.at[p], dst.at[p], send_sem.at[k, p], take_sem.at[k, p], {FSDP: peer}
                    )
                    waits.append((taken.wait_recv, comes))
                    keep(
                        pltpu.make_async_copy(src.at[p], dst.at[slot], own_sem.at[k, p]),
                        peer == fi,
                    )
            elif mode == CROSS:
                halves = cs // fs
                away = ci // halves != fi
                peer = {FSDP: ci // halves, CTX: halves * fi + lax.rem(ci, halves)}
                add(self.remote(src, dst, send_sem.at[k, 0], take_sem.at[k, 0], peer), away, away)
                keep(pltpu.make_async_copy(src, dst, own_sem.at[k, 0]), ci // halves == fi)
            elif mode in (NEXT, PREV):
                reach = self.reach
                m = ci if mode == NEXT else cs - 1 - ci
                odd = lax.rem(m, 2)

                def at(spot):
                    spot = lax.rem(spot + cs, cs)
                    return {CTX: spot if mode == NEXT else cs - 1 - spot}

                def on_line(e, m=m, src=src, dst=dst, k=k, at=at):
                    source = src if e == 2 else dst.at[e - 3]
                    return self.remote(
                        source, dst.at[e - 1], send_sem.at[k, e], take_sem.at[k, e], at(m + 2)
                    )

                def to_mate(g, e, m=m, odd=odd, src=src, dst=dst, k=k, at=at, reach=reach):
                    source = src if e == 0 else dst.at[e - 1]
                    spot = reach + 1 + g
                    return self.remote(
                        source,
                        dst.at[g - 1],
                        send_sem.at[k, spot],
                        take_sem.at[k, spot],
                        at(m + 1 - 2 * odd),
                    )

                starts.append((on_line(2).start, m + 2 < cs))
                waits.append((on_line(2).wait_send, m + 2 < cs))
                starts.append((to_mate(1, 0).start, odd == 0))
                waits.append((to_mate(1, 0).wait_send, odd == 0))
                for e in range(2, reach + 1, 2):
                    here = m - e >= 0
                    relays.append((on_line(e).wait_recv, here))
                    if e + 2 <= reach:
                        goes = here & (m + 2 < cs)
                        relays.append((on_line(e + 2).start, goes))
                        waits.append((on_line(e + 2).wait_send, goes))
                    if e + 1 < reach:
                        relays.append((to_mate(e + 1, e).start, here & (odd == 0)))
                        waits.append((to_mate(e + 1, e).wait_send, here & (odd == 0)))
                    relays.append((to_mate(e - 1, e).start, here & (odd == 1)))
                    waits.append((to_mate(e - 1, e).wait_send, here & (odd == 1)))
                for g in range(1, reach, 2):
                    waits.append((to_mate(g, 0).wait_recv, m - g >= 0))
            else:
                for d in range(1, self.reach + 1):
                    add(
                        self.remote(
                            src.at[d - 1],
                            dst.at[d - 1],
                            send_sem.at[k, d],
                            take_sem.at[k, d],
                            {CTX: lax.rem(ci - d + cs, cs)},
                        ),
                        ci - d >= 0,
                        ci + d < cs,
                    )
        return starts, relays, waits

    def ring_refs(self, u):
        base = self.places[RING]
        outs = self.out_refs[len(self.items) + u * self.hops :]
        return self.sems[base], self.sems[base + 1], self.sems[base + 2], self.sems[base + 3 + u], outs

    def hop_copy(self, u, t):
        cs, ci = span_of(CTX)
        spot = ring_spot(ci, cs)
        k, part, way = self.ring.uses[u]
        send, take, _, buffer, outs = self.ring_refs(u)
        if self.ring.hop + t == 0:
            source = chunk_ref(
                self.in_refs[len(self.items) + k], ring_block(spot - way, cs), part, cs
            )
        else:
            source = buffer.at[t, 1]
        return self.remote(
            source, outs[t], send.at[u, t], take.at[u, t], {CTX: ring_block(spot + way, cs)}
        )

    def load_own(self, u, t):
        cs, ci = span_of(CTX)
        k, part, way = self.ring.uses[u]
        _, _, load, buffer, _ = self.ring_refs(u)
        block = ring_block(ring_spot(ci, cs) - way * (self.ring.hop + t + 1), cs)
        return pltpu.make_async_copy(
            chunk_ref(self.in_refs[len(self.items) + k], block, part, cs),
            buffer.at[t, 1],
            load.at[u, t, 1],
        )

    def load_got(self, u, t):
        _, _, load, buffer, outs = self.ring_refs(u)
        if t == 0:
            source = self.in_refs[len(self.items) + len(self.ring.chunks) + u]
        else:
            source = outs[t - 1]
        return pltpu.make_async_copy(source, buffer.at[t, 0], load.at[u, t, 0])

    def hop_step(self, t):
        uses = range(len(self.ring.uses))
        if self.ring.hop + t > 0:
            for u in uses:
                self.load_own(u, t).start()
                if t > 0:
                    self.hop_copy(u, t - 1).wait_recv()
                self.load_got(u, t).start()
        for u in uses:
            if self.ring.hop + t > 0:
                self.load_own(u, t).wait()
                self.load_got(u, t).wait()
                buffer = self.ring_refs(u)[3]
                buffer[t, 1] = buffer[t, 0] + buffer[t, 1]
            self.hop_copy(u, t).start()

    def begin(self):
        self.greet()
        for start, condition in self.copies()[0]:
            when(condition, start)
        if self.hops:
            self.hop_step(0)

    def end(self, hopped=1):
        _, relays, waits = self.copies()
        for step, condition in relays:
            when(condition, step)
        for t in range(hopped, self.hops):
            self.hop_step(t)
        for wait, condition in waits:
            when(condition, wait)
        for u in range(len(self.ring.uses) if self.hops else 0):
            for t in range(self.hops):
                self.hop_copy(u, t).wait_send()
            self.hop_copy(u, self.hops - 1).wait_recv()

    def take(self, results):
        count = len(self.items)
        if self.hops:
            last = count + self.hops - 1
            self.ring.got = [results[last + u * self.hops] for u in range(len(self.ring.uses))]
            self.ring.hop += self.hops
        return tuple(results[:count])


def exchange(cid, items, ring=None, hops=0, reach=0):
    plan = Traffic(items, ring, hops, reach)
    ins, outs = len(plan.ins), len(plan.outs)

    def body(*refs):
        plan.bind(refs[:ins], refs[ins : ins + outs], refs[ins + outs :])
        plan.begin()
        plan.end()

    results = pl.pallas_call(
        body,
        out_shape=tuple(plan.outs),
        in_specs=[ANY] * ins,
        out_specs=(ANY,) * outs,
        scratch_shapes=plan.scratch,
        compiler_params=pltpu.CompilerParams(
            collective_id=cid, has_side_effects=True, vmem_limit_bytes=plan.vmem() + 4 * MIB
        ),
    )(*plan.ins)
    return plan.take(results)


def scan_tail_body(rows, length, step_ref, u_ref, b_ref, rate_ref, last_ref):
    rate = rate_ref[...]

    def advance(i, states):
        new = []
        for r in range(rows):
            keep = jnp.exp2(step_ref[r, pl.ds(i, 1), :] * rate)
            new.append(keep * states[r] + u_ref[r, pl.ds(i, 1), :] * b_ref[r, i])
        return tuple(new)

    start = tuple(jnp.zeros((DS, 128), f32) for _ in range(rows))
    end = lax.fori_loop(0, length, advance, start, unroll=4)
    for r in range(rows):
        last_ref[r] = end[r]


def scan_full_body(
    rows, length, step_ref, u_ref, b_ref, c_ref, rate_ref, entry_ref, read_ref, hist_ref
):
    rate = rate_ref[...]

    def advance(i, states):
        new = []
        for r in range(rows):
            hist_ref[r, i] = states[r]
            keep = jnp.exp2(step_ref[r, pl.ds(i, 1), :] * rate)
            h = keep * states[r] + u_ref[r, pl.ds(i, 1), :] * b_ref[r, i]
            read_ref[r, pl.ds(i, 1), :] = jnp.sum(h * c_ref[r, i], axis=0, keepdims=True)
            new.append(h)
        return tuple(new)

    lax.fori_loop(0, length, advance, tuple(entry_ref[r] for r in range(rows)), unroll=4)


def adjoint_head_body(rows, length, step_ref, dy_ref, c_ref, rate_ref, first_ref):
    rate = rate_ref[...]

    def advance(k, carried):
        i = length - 1 - k
        new = []
        for r in range(rows):
            keep = jnp.exp2(step_ref[r, pl.ds(i, 1), :] * rate)
            new.append(keep * (carried[r] + dy_ref[r, pl.ds(i, 1), :] * c_ref[r, i]))
        return tuple(new)

    start = tuple(jnp.zeros((DS, 128), f32) for _ in range(rows))
    end = lax.fori_loop(0, length, advance, start, unroll=4)
    for r in range(rows):
        first_ref[r] = end[r]


def adjoint_full_body(
    rows,
    length,
    step_ref,
    u_ref,
    dy_ref,
    b_ref,
    c_ref,
    rate_ref,
    hist_ref,
    later_ref,
    du_ref,
    dexp_ref,
    db_ref,
    dc_ref,
    drate_ref,
):
    rate = rate_ref[...]

    @pl.when(pl.program_id(1) == 0)
    def _():
        db_ref[...] = jnp.zeros_like(db_ref)
        dc_ref[...] = jnp.zeros_like(dc_ref)

    def advance(k, carried):
        i = length - 1 - k
        new = []
        drate = carried[rows]
        for r in range(rows):
            step = step_ref[r, pl.ds(i, 1), :]
            u = u_ref[r, pl.ds(i, 1), :]
            dy = dy_ref[r, pl.ds(i, 1), :]
            keep = jnp.exp2(step * rate)
            b = b_ref[r, i]
            kept = keep * hist_ref[r, i]
            g = carried[r] + dy * c_ref[r, i]
            w = g * kept
            dc_ref[r, i] += (kept + u * b) * dy
            db_ref[r, i] += g * u
            du_ref[r, pl.ds(i, 1), :] = jnp.sum(g * b, axis=0, keepdims=True)
            dexp_ref[r, pl.ds(i, 1), :] = jnp.sum(w * rate, axis=0, keepdims=True)
            drate = drate + w * step
            new.append(keep * g)
        return tuple(new) + (drate,)

    start = tuple(later_ref[r] for r in range(rows)) + (jnp.zeros((DS, 128), f32),)
    end = lax.fori_loop(0, length, advance, start, unroll=2)
    drate_ref[0] = end[rows]


def hosted_call(body, grid, in_specs, out_specs, out_shape, args, cid, plan, own_vmem, later=()):
    steps = 1
    for size in grid:
        steps *= size
    n_in, n_out, x_in, x_out = len(args), len(out_shape), len(plan.ins), len(plan.outs)

    def hosted(*refs):
        mine_in, refs = refs[:n_in], refs[n_in:]
        plan_in, refs = refs[:x_in], refs[x_in:]
        mine_out, refs = refs[:n_out], refs[n_out:]
        plan.bind(plan_in, refs[:x_out], refs[x_out:])
        at = pl.program_id(0)
        for k in range(1, len(grid)):
            at = at * grid[k] + pl.program_id(k)
        pl.when(at == 0)(plan.begin)
        for t in range(1, min(plan.hops, len(later) + 1)):
            pl.when(at == later[t - 1])(functools.partial(plan.hop_step, t))
        body(*mine_in, *mine_out)
        pl.when(at == steps - 1)(functools.partial(plan.end, 1 + len(later)))

    results = pl.pallas_call(
        hosted,
        grid=grid,
        in_specs=in_specs + [ANY] * x_in,
        out_specs=tuple(out_specs) + (ANY,) * x_out,
        out_shape=tuple(out_shape) + tuple(plan.outs),
        scratch_shapes=plan.scratch,
        compiler_params=pltpu.CompilerParams(
            vmem_limit_bytes=plan.vmem() + own_vmem, collective_id=cid, has_side_effects=True
        ),
    )(*args, *plan.ins)
    return tuple(results[:n_out]) + plan.take(results[n_out:])


def scan_call(body, args, kinds, outs, rows_all, length, width, cid, plan, later=()):
    rows = 4 if rows_all % 4 == 0 else rows_all
    single = pl.Buffered(buffer_count=1)
    grid = (rows_all // rows, width // 128)

    def spec(kind):
        extra = {"pipeline_mode": single} if kind == SPREAD else {}
        if kind == SEQ:
            return pl.BlockSpec((rows, length, 128), lambda r, g: (r, 0, g), **extra)
        if kind == SPREAD:
            return pl.BlockSpec((rows, length, DS, 128), lambda r, g: (r, 0, 0, 0), **extra)
        if kind == HIST:
            return pl.BlockSpec((rows, length, DS, 128), lambda r, g: (r, 0, 0, g), **extra)
        if kind == STATE:
            return pl.BlockSpec((rows, DS, 128), lambda r, g: (r, 0, g), **extra)
        if kind == RATE:
            return pl.BlockSpec((DS, 128), lambda r, g: (0, g), **extra)
        return pl.BlockSpec((1, DS, 128), lambda r, g: (r, 0, g), **extra)

    def block_bytes(kind):
        wide = rows * length * 128 * 4
        return {SEQ: 2 * wide, SPREAD: DS * wide, HIST: 2 * DS * wide}.get(kind, MIB // 2)

    shape_of = {
        SEQ: (rows_all, length, width),
        SPREAD: (rows_all, length, DS, 128),
        HIST: (rows_all, length, DS, width),
        STATE: (rows_all, DS, width),
        DRATE: (rows_all // rows, DS, width),
    }
    return hosted_call(
        functools.partial(body, rows, length),
        grid,
        [spec(k) for k in kinds],
        [spec(k) for k in outs],
        [jax.ShapeDtypeStruct(shape_of[k], f32) for k in outs],
        args,
        cid,
        plan,
        8 * MIB + sum(block_bytes(k) for k in tuple(kinds) + tuple(outs)),
        later,
    )


def attend_body(heads, q_ref, k_ref, v_ref, bias_ref, out_ref, total_ref):
    keys = k_ref[...].T
    for h in range(heads):
        rows = slice(h * HD, (h + 1) * HD)
        scores = jnp.dot(keys, q_ref[rows], preferred_element_type=f32)
        scores = scores * HD**-0.5 + bias_ref[...]
        peak = jnp.max(scores, axis=0, keepdims=True)
        grown = jnp.exp(scores - peak)
        total = jnp.sum(grown, axis=0, keepdims=True)
        probs = (grown * (1.0 / total)).astype(bf16)
        out_ref[rows] = jnp.dot(v_ref[...], probs, preferred_element_type=f32).astype(bf16)
        total_ref[0, h : h + 1] = peak + jnp.log(total)


def attend_back_body(
    heads, q_ref, k_ref, v_ref, bias_ref, total_ref, grad_ref, dq_ref, dk_ref, dv_ref
):
    keys = k_ref[...].T
    values = v_ref[...].T
    for h in range(heads):
        rows = slice(h * HD, (h + 1) * HD)
        scores = jnp.dot(keys, q_ref[rows], preferred_element_type=f32)
        probs = jnp.exp(scores * HD**-0.5 + bias_ref[...] - total_ref[0, h : h + 1])
        grad = jnp.dot(values, grad_ref[rows], preferred_element_type=f32)
        mean = jnp.sum(probs * grad, axis=0, keepdims=True)
        low = (probs * (grad - mean)).astype(bf16)
        dq = jnp.dot(k_ref[...], low, preferred_element_type=f32)
        dq_ref[rows] = (dq * HD**-0.5).astype(bf16)
        dk = dense_nt(q_ref[rows], low) * HD**-0.5
        dv = dense_nt(grad_ref[rows], probs.astype(bf16))
        if h == 0:
            dk_ref[...] = dk
            dv_ref[...] = dv
        else:
            dk_ref[...] += dk
            dv_ref[...] += dv


def rows_matmul(values, weight, swapped=False):
    count, tokens, depth = values.shape
    if swapped:
        tokens, depth = depth, tokens
    real, width = weight.shape
    turned = real > tokens * 8
    if turned:
        weight = weight.T

    def body(value_ref, weight_ref, out_ref):
        value = value_ref[0].T if swapped else value_ref[0][:, :real]
        product = dense_nt if turned else dense
        out_ref[0] = product(value, weight_ref[...]).astype(bf16)

    return pl.pallas_call(
        body,
        grid=(count,),
        in_specs=[
            pl.BlockSpec((1,) + values.shape[1:], lambda r: (r, 0, 0)),
            pl.BlockSpec(weight.shape, lambda r: (0, 0), pipeline_mode=pl.Buffered(buffer_count=1)),
        ],
        out_specs=pl.BlockSpec((1, tokens, width), lambda r: (r, 0, 0)),
        out_shape=jax.ShapeDtypeStruct((count, tokens, width), bf16),
        compiler_params=pltpu.CompilerParams(vmem_limit_bytes=24 * MIB),
    )(values, weight)


def rms_norm(values, gain_row):
    return (
        values * lax.rsqrt(jnp.mean(values * values, axis=-1, keepdims=True) + norm_eps) * gain_row
    )


def dense(operand, partner):
    return jnp.dot(operand, partner, preferred_element_type=f32)


def dense_tn(operand, partner):
    return lax.dot_general(
        operand, partner, (((0,), (0,)), ((), ())), preferred_element_type=f32
    )


def dense_nt(operand, partner):
    return lax.dot_general(
        operand, partner, (((1,), (1,)), ((), ())), preferred_element_type=f32
    )


def conv_silu(extended, conv_taps, same_seg):
    length_out = extended.shape[1] - CONV + 1
    summed = jnp.zeros((extended.shape[0], length_out, extended.shape[2]), f32)
    for offset in range(CONV):
        summed = summed + jnp.where(
            same_seg[offset][:, :, None],
            extended[:, offset : offset + length_out] * conv_taps[offset],
            0.0,
        )
    return jax.nn.silu(summed)


def adam_step(gradient, moments_old, weight_now):
    first_moment = beta_one * moments_old[0] + (1.0 - beta_one) * gradient
    second_moment = beta_two * moments_old[1] + (1.0 - beta_two) * gradient * gradient
    corrected = (
        first_moment
        / (1.0 - beta_one**adam_count)
        / (jnp.sqrt(second_moment / (1.0 - beta_two**adam_count)) + adam_eps)
    )
    return (second_moment, -learn_rate * (corrected + decay_rate * weight_now))


def pad_last(values, width):
    return jnp.pad(values, [(0, 0)] * (values.ndim - 1) + [(0, width - values.shape[-1])])


def column_parts(weight, parts, shards_of, width):
    own = weight.shape[1] // parts // shards_of
    return jnp.stack(
        [
            jnp.concatenate(
                [
                    pad_last(weight[:, (p * shards_of + j) * own : (p * shards_of + j + 1) * own], width)
                    for p in range(parts)
                ],
                axis=1,
            )
            for j in range(shards_of)
        ]
    )


def shards(
    tokens,
    cotangent,
    segments,
    w_qkv,
    m_qkv,
    w_attn_out,
    m_attn_out,
    w_mamba_in,
    m_mamba_in,
    w_ssm_proj,
    m_ssm_proj,
    w_mamba_out,
    m_mamba_out,
    w_gate_up,
    m_gate_up,
    w_ffn_down,
    m_ffn_down,
    ssm_vec,
    m_ssm_vec,
    embed_small,
    m_embed_small,
):
    fs, cs = lax.axis_size(FSDP), lax.axis_size(CTX)
    fi, ci = lax.axis_index(FSDP), lax.axis_index(CTX)
    tok = tokens.shape[1]
    dim = tokens.shape[2]
    row_len = segments.shape[1]
    halves = cs // fs
    reach = min(row_len // 2, WINDOW) // tok
    metas = META // cs
    chan = DI // fs
    chan_p = ceil_to(chan, 128)
    ffw = FF // fs
    ffw_p = ceil_to(ffw, 128)
    heads_dim = NH * HD
    kv_dim = KVH * HD
    groups = NH // KVH
    scale_factor = HD ** (-0.5)
    xdim = DTR + 2 * DS
    both = (FSDP, CTX)

    def row_block(weight):
        rows, cols = weight.shape[0] // halves, weight.shape[1] // fs
        return lax.dynamic_slice(
            weight, ((ci % halves) * rows, (ci // halves) * cols), (rows, cols)
        )

    def unpaired(value, width):
        return jnp.concatenate([value[0][:, :width], value[1][:, :width]], axis=1).astype(f32)

    def spread_hops(weights):
        total, done, out = sum(weights), 0, []
        for k in range(len(weights)):
            upto = (cs - 1) * sum(weights[: k + 1]) // total
            out.append(upto - done)
            done = upto
        return out

    def row_chunks(operand, partner):
        grad = dense_tn(operand, partner).astype(bf16)
        return grad.reshape(cs, 1, grad.shape[0] // cs, grad.shape[1])

    def column_chunks(operand, partner, parts=1):
        cols = partner.shape[1] // fs
        wide = jnp.concatenate(
            [
                pad_last(partner[:, j * cols : (j + 1) * cols], ceil_to(cols, 128))
                for j in range(fs)
            ],
            axis=1,
        )
        grad = dense_tn(operand, wide).astype(bf16)
        return grad.reshape(halves, parts, -1, grad.shape[1])

    def by_rows(value):
        return value.astype(bf16).reshape(fs, tok, -1)

    blocks = 25

    def in_blocks(value):
        return value.reshape(fs, 2, blocks, value.shape[1] // (2 * blocks), value.shape[2])

    mi_send = column_parts(w_mamba_in, 2, fs, chan_p)
    qkv_send = column_parts(w_qkv, 1, fs, w_qkv.shape[1] // fs)
    gain_rows = embed_small[META:]
    meta_rows = lax.dynamic_slice_in_dim(embed_small, ci * metas, metas, 0)
    source = tokens[0].astype(f32)
    normed_f, norm_pull = jax.vjp(rms_norm, source, gain_rows[0])
    normed = normed_f.astype(bf16)
    meta_f, meta_pull = jax.vjp(rms_norm, meta_rows, gain_rows[0])
    meta_low = meta_f.astype(bf16)

    normed_all, seg_all, mi_w, qkv_w = exchange(
        0,
        [
            (normed, GATHER, FSDP),
            (segments, ALL, FSDP),
            (in_blocks(mi_send), (HALF, 0, blocks), WEIGHTS),
            (in_blocks(qkv_send), (HALF, 0, blocks), WEIGHTS),
        ],
    )
    gu_send = in_hbm(in_blocks(column_parts(w_gate_up, 2, fs, ffw_p)))
    mi_w = mi_w.reshape(dim, 2 * chan_p)
    qkv_w = qkv_w.reshape(dim, -1)
    seg_all = seg_all.reshape(fs, row_len)
    seg_row = segments[0]
    normed_all = normed_all.reshape(fs * tok, dim)
    xp_w = jnp.pad(w_ssm_proj[:, :xdim], ((0, chan_p - chan), (0, 0)))
    dt_w = jnp.pad(w_ssm_proj[:, xdim:], ((0, chan_p - chan), (0, 0)))
    vec = pad_last(lax.dynamic_slice_in_dim(ssm_vec, fi * chan, chan, 1), chan_p)

    normed_rows = normed_all.reshape(fs, tok, dim)
    qkv_parts = jnp.einsum("ftd,dc->fct", normed_rows, qkv_w, preferred_element_type=f32)
    meta_part = jnp.broadcast_to(
        dense(meta_low, qkv_w).astype(bf16)[None], (fs, metas, qkv_w.shape[1])
    )
    qkv_got, meta_got = exchange(
        1, [(qkv_parts.astype(bf16), EACH, FSDP), (meta_part, EACH, FSDP)]
    )
    qkv_own = qkv_got.reshape(heads_dim + 2 * kv_dim, tok)
    queries = qkv_own[:heads_dim]
    keyval = qkv_own[heads_dim:]
    meta_own = jnp.concatenate([meta_got[j] for j in range(fs)], axis=1)[:, heads_dim:]
    kv_before, meta_kv, gu_0 = exchange(
        2,
        [
            (keyval, NEXT, CTX),
            (meta_own, ALL, CTX),
            (gu_send, (HALF, 0, 5), WEIGHTS),
        ],
        reach=reach,
    )
    kv_before = jnp.where(
        (ci - 1 - jnp.arange(reach) >= 0)[:, None, None], kv_before, jnp.zeros_like(kv_before)
    )
    key_rows = jnp.concatenate(
        [meta_kv.reshape(META, 2 * kv_dim).T]
        + [kv_before[d - 1] for d in range(reach, 0, -1)]
        + [keyval],
        axis=1,
    )

    mamba_in = dense(normed_all, mi_w).reshape(fs, tok, 2 * chan_p)
    inner_pre = mamba_in[:, :, :chan_p]
    gate_z = mamba_in[:, :, chan_p:]
    up_ring = [(c, c + 1) for c in range(cs - 1)]
    down_ring = [(c + 1, c) for c in range(cs - 1)]
    tail_rows = lax.ppermute(inner_pre[:, tok - (CONV - 1) :], CTX, up_ring)
    extended = jnp.concatenate([tail_rows, inner_pre], axis=1)
    seg_ext = lax.dynamic_slice_in_dim(
        jnp.concatenate([jnp.full((fs, CONV - 1), -1, jnp.int32), seg_all], axis=1),
        ci * tok,
        tok + CONV - 1,
        1,
    )
    own_seg = seg_ext[:, CONV - 1 :]
    same_seg = [seg_ext[:, o : o + tok] == own_seg for o in range(CONV)]
    starts = own_seg != seg_ext[:, CONV - 2 : -1]
    inner_x, conv_pull = jax.vjp(
        lambda ext_rows, taps: conv_silu(ext_rows, taps, same_seg), extended, vec[:CONV]
    )
    inner_low = inner_x.astype(bf16).reshape(fs * tok, chan_p)
    xproj_part = lax.dot_general(
        xp_w, inner_low, (((0,), (1,)), ((), ())), preferred_element_type=f32
    )
    xproj_got, attn_old = exchange(
        3,
        [
            (xproj_part, GATHER, FSDP),
            (row_block(w_attn_out), CROSS, BOTH),
        ],
    )
    xproj = jnp.sum(xproj_got, axis=0).T
    delta_low = xproj[:, :DTR].astype(bf16)
    pre_delta = dense_nt(delta_low, dt_w).reshape(fs, tok, chan_p) + vec[CONV]
    step = jax.nn.softplus(pre_delta)
    step_far = jnp.where(starts[:, :, None], FAR, step)
    drive = step * inner_x

    def spread(columns):
        return jnp.broadcast_to(columns.reshape(fs, tok, DS, 1), (fs, tok, DS, 128))

    b_wide = spread(xproj[:, DTR : DTR + DS])
    c_wide = spread(xproj[:, DTR + DS : xdim])
    rate = -jnp.exp(vec[CONV + 2 :])
    rate2 = rate * LOG2E
    sizes = (fs, tok, chan_p)
    last_state, ssm_proj_old = scan_call(
        scan_tail_body,
        (step_far, drive, b_wide, rate2),
        (SEQ, SEQ, SPREAD, RATE),
        (STATE,),
        *sizes,
        cid=19,
        plan=Traffic([(row_block(w_ssm_proj), CROSS, BOTH)]),
    )
    step_sum = jnp.sum(step_far, axis=1)
    state_before, sums, gu_2 = exchange(
        4,
        [
            (last_state.astype(bf16), NEXT, CTX),
            (step_sum, ALL, CTX),
            (gu_send, (HALF, 10, 19), WEIGHTS),
        ],
        reach=reach,
    )

    def decay_of(block):
        total = lax.dynamic_index_in_dim(sums, jnp.clip(block, 0, cs - 1), 0, keepdims=False)
        return jnp.exp2(total[:, None, :] * rate2)

    entry = jnp.zeros((fs, DS, chan_p), f32)
    for d in range(reach, 0, -1):
        there = jnp.where(ci >= d, state_before[d - 1].astype(f32), 0.0)
        entry = decay_of(ci - d) * entry + there
    readout, hist, mamba_out_old = scan_call(
        scan_full_body,
        (step_far, drive, b_wide, c_wide, rate2, entry),
        (SEQ, SEQ, SPREAD, SPREAD, RATE, STATE),
        (SEQ, HIST),
        *sizes,
        cid=20,
        plan=Traffic([(row_block(w_mamba_out), CROSS, BOTH)]),
    )
    skip = vec[CONV + 1]
    pre_mix = readout + skip * inner_x
    gate_s = jax.nn.sigmoid(gate_z)
    gate_silu = gate_z * gate_s
    mixture_low = (pre_mix * gate_silu).astype(bf16).reshape(fs * tok, chan_p)
    ssm_part = rows_matmul(mixture_low.reshape(fs, tok, chan_p), w_mamba_out)

    key_span = (reach + 1) * tok
    padded_seg = jnp.concatenate([jnp.full((reach * tok,), -1, jnp.int32), seg_row])
    key_seg = lax.dynamic_slice_in_dim(padded_seg, ci * tok, key_span, 0)
    query_seg = lax.dynamic_slice_in_dim(seg_row, ci * tok, tok, 0)
    query_pos = jnp.arange(tok, dtype=jnp.int32) + reach * tok
    key_pos = jnp.arange(key_span, dtype=jnp.int32)
    allowed = (
        (key_seg[:, None] == query_seg[None, :])
        & (key_pos[:, None] <= query_pos[None, :])
        & (query_pos[None, :] - key_pos[:, None] < WINDOW)
    )
    allowed = jnp.concatenate([jnp.ones((META, tok), jnp.bool_), allowed], axis=0)
    bias = jnp.where(allowed, 0.0, -1e30)
    seen = META + key_span
    q_spec = pl.BlockSpec((groups * HD, tok), lambda g: (g, 0))
    k_spec = pl.BlockSpec((HD, seen), lambda g: (g, 0))
    v_spec = pl.BlockSpec((HD, seen), lambda g: (g + KVH, 0))
    bias_spec = pl.BlockSpec((seen, tok), lambda g: (0, 0))
    total_spec = pl.BlockSpec((1, groups, tok), lambda g: (g, 0, 0))
    attended, log_totals, gu_1, ffn_down_old = hosted_call(
        functools.partial(attend_body, groups),
        (KVH,),
        [q_spec, k_spec, v_spec, bias_spec],
        [q_spec, total_spec],
        [
            jax.ShapeDtypeStruct((heads_dim, tok), bf16),
            jax.ShapeDtypeStruct((KVH, groups, tok), f32),
        ],
        (queries, key_rows, key_rows, bias),
        16,
        Traffic([(gu_send, (HALF, 5, 10), WEIGHTS), (row_block(w_ffn_down), CROSS, BOTH)]),
        12 * MIB,
    )
    wide = heads_dim // fs
    att_got, gu_3 = exchange(
        5,
        [
            (attended.reshape(fs, wide, tok), EACH, FSDP),
            (gu_send, (HALF, 19, 25), WEIGHTS),
        ],
    )
    gu_w = jnp.concatenate([gu_0, gu_1, gu_2, gu_3], axis=2).reshape(dim, 2 * ffw_p)
    att_tp = jnp.swapaxes(att_got, 1, 2).reshape(fs * tok, wide)
    attn_part = rows_matmul(att_got, w_attn_out, True)
    attn_got, ssm_got = exchange(
        6, [(attn_part, REDUCE, FSDP), (ssm_part, REDUCE, FSDP)]
    )
    attn_proj = jnp.sum(attn_got.astype(f32), axis=0)
    ssm_proj = jnp.sum(ssm_got.astype(f32), axis=0)
    attn_branch, attn_pull = jax.vjp(rms_norm, attn_proj, gain_rows[1])
    ssm_branch, ssm_norm_pull = jax.vjp(rms_norm, ssm_proj, gain_rows[2])
    residual = source + 0.5 * (attn_branch + ssm_branch)
    ffn_in_f, ffn_norm_pull = jax.vjp(rms_norm, residual, gain_rows[3])
    ffn_in, cot_all = exchange(
        7, [(ffn_in_f.astype(bf16), GATHER, FSDP), (cotangent[0], GATHER, FSDP)]
    )
    cot_all = cot_all.reshape(fs * tok, dim)
    ffn_in = ffn_in.reshape(fs * tok, dim)

    gate_up = dense(ffn_in, gu_w)
    hidden_f, glu_pull = jax.vjp(
        lambda values: jax.nn.silu(values[:, :ffw_p]) * values[:, ffw_p:], gate_up
    )
    hidden_wide = hidden_f.astype(bf16)
    hidden = hidden_wide[:, :ffw]
    down_part = rows_matmul(hidden_wide.reshape(fs, tok, ffw_p), w_ffn_down)
    hidden_grad = pad_last(dense_nt(cot_all, w_ffn_down), ffw_p)
    gate_up_grad = glu_pull(hidden_grad)[0].astype(bf16)
    ring_one = Ring(
        [
            row_chunks(ffn_in, gate_up_grad[:, :ffw_p]),
            row_chunks(ffn_in, gate_up_grad[:, ffw_p:]),
            column_chunks(hidden, cot_all, 2),
        ],
        [(0, 0, 1), (1, 0, -1), (2, 0, 1), (2, 1, -1)],
    )
    hops = spread_hops([1, 1, 1, 1, 2, 1])
    ffn_back = by_rows(dense_nt(gate_up_grad, gu_w))
    (back_got,) = exchange(8, [(ffn_back, REDUCE, FSDP)], ring_one, hops[0])
    resid_part, gain_ffn_grad = ffn_norm_pull(jnp.sum(back_got.astype(f32), axis=0))
    residual_grad = cotangent[0].astype(f32) + resid_part
    branch_grad = 0.5 * residual_grad
    attn_proj_grad, gain_attn_grad = attn_pull(branch_grad)
    ssm_proj_grad, gain_ssm_grad = ssm_norm_pull(branch_grad)
    branch_low = (attn_proj_grad.astype(bf16), ssm_proj_grad.astype(bf16))
    attn_proj_low, ssm_proj_low = exchange(
        9,
        [(branch_low[0], GATHER, FSDP), (branch_low[1], GATHER, FSDP)],
        ring_one,
        hops[1],
    )
    attn_proj_low = attn_proj_low.reshape(fs * tok, dim)
    ssm_proj_low = ssm_proj_low.reshape(fs * tok, dim)
    att_grad_tp = jnp.einsum(
        "ftd,cd->fct",
        attn_proj_low.reshape(fs, tok, dim),
        w_attn_out,
        preferred_element_type=f32,
    ).astype(bf16)
    (att_grad_got,) = exchange(10, [(att_grad_tp, EACH, FSDP)], ring_one, hops[2])

    def own_pair(held, part):
        piece = lax.dynamic_slice_in_dim(held, ci * (dim // cs), dim // cs, 0)
        return jnp.stack([piece[:, :part], piece[:, part:]])

    qkv_old = lax.dynamic_slice_in_dim(qkv_w, ci * (dim // cs), dim // cs, 0)
    attended_grad = att_grad_got.reshape(heads_dim, tok)

    query_grad, key_grad, value_grad, mamba_in_old = hosted_call(
        functools.partial(attend_back_body, groups),
        (KVH,),
        [q_spec, k_spec, v_spec, bias_spec, total_spec, q_spec],
        [q_spec, k_spec, k_spec],
        [
            jax.ShapeDtypeStruct((heads_dim, tok), bf16),
            jax.ShapeDtypeStruct((kv_dim, seen), f32),
            jax.ShapeDtypeStruct((kv_dim, seen), f32),
        ],
        (queries, key_rows, key_rows, bias, log_totals, attended_grad),
        24,
        Traffic([(own_pair(mi_w, chan_p), PAIR, FSDP)], ring_one, hops[3]),
        16 * MIB,
    )
    kv_grad_all = jnp.concatenate([key_grad, value_grad], axis=0)
    kv_send = jnp.stack(
        [
            kv_grad_all[:, META + (reach - d) * tok : META + (reach - d + 1) * tok]
            for d in range(1, reach + 1)
        ]
    ).astype(bf16)
    meta_send = kv_grad_all[:, :META].T.astype(bf16).reshape(cs, metas, 2 * kv_dim)
    kv_back, meta_back, down_got = exchange(
        13,
        [
            (kv_send, BACK, CTX),
            (meta_send, EACH, CTX),
            (down_part, REDUCE, FSDP),
        ],
        ring_one,
        hops[4],
        reach,
    )
    output = residual + jnp.sum(down_got.astype(f32), axis=0)
    own_kv_grad = kv_grad_all[:, META + reach * tok :]
    for d in range(1, reach + 1):
        own_kv_grad = own_kv_grad + jnp.where(ci + d < cs, kv_back[d - 1].astype(f32), 0.0)
    meta_kv_grad = jnp.sum(meta_back.astype(f32), axis=0).astype(bf16)
    meta_grad_parts = column_parts(
        jnp.pad(meta_kv_grad, ((0, 0), (heads_dim, 0))), 1, fs, qkv_w.shape[1]
    )
    qkv_grad = jnp.concatenate([query_grad, own_kv_grad.astype(bf16)], axis=0)
    qkv_grad_tp, meta_grad_tp = exchange(
        14,
        [
            (qkv_grad.reshape(fs, -1, tok), EACH, FSDP),
            (meta_grad_parts, EACH, FSDP),
        ],
        ring_one,
        hops[5],
    )

    mixture_grad = pad_last(dense_nt(ssm_proj_low, w_mamba_out), chan_p).reshape(fs, tok, chan_p)
    read_grad = mixture_grad * gate_silu
    gate_grad = mixture_grad * pre_mix * (gate_s * (1.0 + gate_z * (1.0 - gate_s)))
    gate_low = gate_grad.astype(bf16).reshape(fs * tok, chan_p)
    qkv_full = jnp.einsum("ftd,fct->dc", normed_rows, qkv_grad_tp, preferred_element_type=f32)
    qkv_full = qkv_full + jnp.einsum(
        "md,fmc->dc", meta_low, meta_grad_tp, preferred_element_type=f32
    )
    ring_two = Ring(
        [
            row_chunks(normed_all, gate_low),
            qkv_full.astype(bf16).reshape(cs, 1, dim // cs, qkv_w.shape[1]),
            column_chunks(att_tp, attn_proj_low),
            column_chunks(mixture_low[:, :chan], ssm_proj_low),
        ],
        [(0, 0, 1), (1, 0, 1), (2, 0, -1), (3, 0, -1)],
    )
    hops = spread_hops([1, 2, 2, 2])
    gate_sum, up_sum, down_top, down_low = ring_one.finish()
    first_adj, gate_up_old = scan_call(
        adjoint_head_body,
        (step_far, read_grad, c_wide, rate2),
        (SEQ, SEQ, SPREAD, RATE),
        (STATE,),
        *sizes,
        cid=21,
        plan=Traffic([(own_pair(gu_w, ffw_p), PAIR, FSDP)], ring_two, hops[0]),
    )
    adj_after, gate_up_sum = exchange(
        11,
        [
            (first_adj.astype(bf16), PREV, CTX),
            (jnp.stack([gate_sum, up_sum]).astype(bf16), PAIR, FSDP),
        ],
        ring_two,
        hops[1],
        reach,
    )
    gate_up_old = unpaired(gate_up_old, ffw)
    mamba_in_old = unpaired(mamba_in_old, chan)
    later = jnp.zeros((fs, DS, chan_p), f32)
    for d in range(reach, 0, -1):
        there = jnp.where(ci + d < cs, adj_after[d - 1].astype(f32), 0.0)
        later = decay_of(ci + d) * later + there
    drive_grad, exp_grad, b_acc, c_acc, rate_grad = scan_call(
        adjoint_full_body,
        (step_far, drive, read_grad, b_wide, c_wide, rate2, hist, later),
        (SEQ, SEQ, SEQ, SPREAD, SPREAD, RATE, HIST, STATE),
        (SEQ, SEQ, SPREAD, SPREAD, DRATE),
        *sizes,
        cid=22,
        plan=Traffic([], ring_two, hops[2]),
        later=(4,) if hops[2] == 2 else (),
    )
    cross = [
        (f * cs + c, (c // halves) * cs + halves * f + c % halves)
        for f in range(fs)
        for c in range(cs)
    ]
    down_both = jnp.concatenate([down_top, down_low], axis=0).astype(bf16)
    drive_grad, down_both = together(drive_grad, down_both)
    down_sum = lax.ppermute(down_both, (FSDP, CTX), cross)
    step_grad = drive_grad * inner_x + exp_grad * LN2
    pre_delta_grad = step_grad * jax.nn.sigmoid(pre_delta)
    inner_grad = drive_grad * step + skip * read_grad
    small_grad = jnp.concatenate(
        [
            jnp.sum(pre_delta_grad, axis=(0, 1))[None],
            jnp.sum(inner_x * read_grad, axis=(0, 1))[None],
            jnp.sum(rate_grad, axis=0) * rate,
        ],
        axis=0,
    )
    pre_delta_low = pre_delta_grad.astype(bf16).reshape(fs * tok, chan_p)
    xgrad_part = jnp.concatenate(
        [
            lax.dot_general(
                dt_w, pre_delta_low, (((0,), (1,)), ((), ())), preferred_element_type=f32
            ),
            jnp.sum(b_acc, axis=-1).reshape(fs * tok, DS).T,
            jnp.sum(c_acc, axis=-1).reshape(fs * tok, DS).T,
        ],
        axis=0,
    )
    (xgrad_got,) = exchange(12, [(xgrad_part, GATHER, FSDP)], ring_two, hops[3])
    xproj_grad = jnp.sum(xgrad_got, axis=0).T.astype(bf16)
    inner_grad = inner_grad + dense_nt(xproj_grad, xp_w).reshape(fs, tok, chan_p)
    ext_grad, taps_grad = conv_pull(inner_grad)
    returned = lax.ppermute(ext_grad[:, : CONV - 1].astype(bf16), CTX, down_ring).astype(f32)
    inner_pre_grad = ext_grad[:, CONV - 1 :] + jnp.pad(
        returned, ((0, 0), (tok - (CONV - 1), 0), (0, 0))
    )
    inner_pre_low = inner_pre_grad.astype(bf16).reshape(fs * tok, chan_p)
    mamba_in_grad = jnp.concatenate([inner_pre_low, gate_low], axis=1)
    split = ceil_to(chan_p * 9 // 16, 128)
    ring_three = Ring(
        [
            row_chunks(normed_all, inner_pre_low[:, :split]),
            row_chunks(normed_all, inner_pre_low[:, split:]),
            column_chunks(
                jnp.concatenate([inner_low[:, :chan], pre_delta_low[:, :chan]], axis=0),
                jnp.concatenate(
                    [
                        jnp.pad(xproj_grad, ((0, 0), (0, DTR))),
                        jnp.pad(delta_low, ((0, 0), (xdim, 0))),
                    ],
                    axis=0,
                ),
            ),
        ],
        [(0, 0, 1), (1, 0, -1), (2, 0, -1)],
    )
    vec_grad = jnp.concatenate([taps_grad, small_grad], axis=0)
    token_back = jnp.einsum("fct,dc->ftd", qkv_grad_tp, qkv_w, preferred_element_type=f32)
    token_back = token_back + dense_nt(mamba_in_grad, mi_w).reshape(fs, tok, dim)
    meta_back_rows = jnp.einsum("fmc,dc->fmd", meta_grad_tp, qkv_w, preferred_element_type=f32)
    token_back = by_rows(token_back)
    hops = spread_hops([3, 2, 2])
    token_got, meta_rows_got = exchange(
        15,
        [(token_back, REDUCE, FSDP), (meta_back_rows.astype(bf16), REDUCE, FSDP)],
        ring_three,
        hops[0],
    )
    source_part, gain_in_grad = norm_pull(jnp.sum(token_got.astype(f32), axis=0))
    source_grad = residual_grad + source_part
    meta_grad, gain_in_meta = meta_pull(jnp.sum(meta_rows_got.astype(f32), axis=0))
    embed_part = jnp.concatenate(
        [
            meta_grad,
            jnp.stack([gain_in_grad + gain_in_meta, gain_attn_grad, gain_ssm_grad, gain_ffn_grad]),
        ],
        axis=0,
    )
    (embed_rows,) = exchange(17, [(embed_part, GATHER, FSDP)], ring_three, hops[1])
    embed_got, vec_got = exchange(
        18,
        [
            (jnp.sum(embed_rows, axis=0).astype(bf16), LINE, CTX),
            (vec_grad.astype(bf16), LINE, CTX),
        ],
        ring_three,
        hops[2],
    )
    embed_got = embed_got.astype(f32)
    vec_part = jnp.sum(vec_got.astype(f32), axis=0)
    embed_total = jnp.concatenate(
        [embed_got[:, :metas].reshape(META, dim), jnp.sum(embed_got[:, metas:], axis=0)], axis=0
    )
    gate_half, qkv_gradient, attn_sum, mamba_out_sum = ring_two.finish()
    inner_a, inner_b, proj_sum = ring_three.finish()
    mamba_in_sum, attn_sum, mamba_out_sum, proj_sum, vec_all = exchange(
        23,
        [
            (
                jnp.stack([jnp.concatenate([inner_a, inner_b], axis=1), gate_half]).astype(bf16),
                PAIR,
                FSDP,
            ),
            (attn_sum.astype(bf16), CROSS, BOTH),
            (mamba_out_sum.astype(bf16), CROSS, BOTH),
            (proj_sum.astype(bf16), CROSS, BOTH),
            (vec_part, GATHER, FSDP),
        ],
    )
    ssm_total = jnp.concatenate([vec_all[j, :, :chan] for j in range(fs)], axis=1)
    gate_up_gradient = unpaired(gate_up_sum, ffw)
    mamba_in_gradient = unpaired(mamba_in_sum, chan)
    down_turned, old_turned = together(down_sum[:, : dim // fs].T, ffn_down_old.T)
    ffn_down_gradient = down_turned.astype(f32)
    attn_gradient = attn_sum[:, : dim // fs].astype(f32)
    mamba_out_gradient = mamba_out_sum[:, : dim // fs].astype(f32)
    ssm_proj_gradient = proj_sum[:, : w_ssm_proj.shape[1] // fs].astype(f32)

    def adam_block(gradient, moments_old, weight):
        return adam_step(gradient, moments_old, weight.astype(f32))

    qkv_moments, qkv_update = adam_block(qkv_gradient, m_qkv, qkv_old)
    attn_moments, attn_update = adam_block(attn_gradient, m_attn_out, attn_old)
    mamba_in_moments, mamba_in_update = adam_block(mamba_in_gradient, m_mamba_in, mamba_in_old)
    ssm_proj_moments, ssm_proj_update = adam_block(ssm_proj_gradient, m_ssm_proj, ssm_proj_old)
    mamba_out_moments, mamba_out_update = adam_block(
        mamba_out_gradient, m_mamba_out, mamba_out_old
    )
    gate_up_moments, gate_up_update = adam_block(gate_up_gradient, m_gate_up, gate_up_old)
    ffn_down_moments, ffn_down_update = adam_block(
        ffn_down_gradient, jnp.swapaxes(m_ffn_down, 1, 2), old_turned
    )
    ffn_down_gradient, ffn_down_moments, ffn_down_update = (
        ffn_down_gradient.T,
        ffn_down_moments.T,
        ffn_down_update.T,
    )
    ssm_vec_moments, ssm_vec_update = adam_step(ssm_total, m_ssm_vec, ssm_vec)
    embed_moments, embed_update = adam_step(embed_total, m_embed_small, embed_small)
    return (
        output.astype(jnp.bfloat16)[None],
        source_grad[None],
        qkv_gradient,
        qkv_moments,
        qkv_update,
        attn_gradient,
        attn_moments,
        attn_update,
        mamba_in_gradient,
        mamba_in_moments,
        mamba_in_update,
        ssm_proj_gradient,
        ssm_proj_moments,
        ssm_proj_update,
        mamba_out_gradient,
        mamba_out_moments,
        mamba_out_update,
        gate_up_gradient,
        gate_up_moments,
        gate_up_update,
        ffn_down_gradient,
        ffn_down_moments,
        ffn_down_update,
        ssm_total,
        ssm_vec_moments,
        ssm_vec_update,
        embed_total,
        embed_moments,
        embed_update,
    )


def solution(mesh):
    in_specs = (
        P(FSDP, CTX, None),
        P(FSDP, CTX, None),
        P(FSDP, None),
        P(FSDP, None),
        P(None, CTX, FSDP),
        P(FSDP, None),
        P(None, CTX, FSDP),
        P(FSDP, None),
        P(None, CTX, FSDP),
        P(FSDP, None),
        P(None, CTX, FSDP),
        P(FSDP, None),
        P(None, CTX, FSDP),
        P(FSDP, None),
        P(None, CTX, FSDP),
        P(FSDP, None),
        P(None, CTX, FSDP),
        P(),
        P(),
        P(),
        P(),
    )
    out_specs = (
        P(FSDP, CTX, None),
        P(FSDP, CTX, None),
        P(CTX, FSDP),
        P(CTX, FSDP),
        P(CTX, FSDP),
        P(CTX, FSDP),
        P(CTX, FSDP),
        P(CTX, FSDP),
        P(CTX, FSDP),
        P(CTX, FSDP),
        P(CTX, FSDP),
        P(CTX, FSDP),
        P(CTX, FSDP),
        P(CTX, FSDP),
        P(CTX, FSDP),
        P(CTX, FSDP),
        P(CTX, FSDP),
        P(CTX, FSDP),
        P(CTX, FSDP),
        P(CTX, FSDP),
        P(CTX, FSDP),
        P(CTX, FSDP),
        P(CTX, FSDP),
        P(),
        P(),
        P(),
        P(),
        P(),
        P(),
    )
    return jax.shard_map(shards, mesh=mesh, in_specs=in_specs, out_specs=out_specs, check_vma=False)
```

```python
import functools

import jax
import jax.numpy as jnp
from jax import lax
from jax.experimental import pallas as pl
from jax.experimental.pallas import tpu as pltpu
from jax.sharding import PartitionSpec as P

NH = 25
KVH = 5
HD = 64
DI = 3200
DS = 16
DTR = 100
FF = 5504
META = 128
CONV = 4
WINDOW = 1024

norm_eps = 1e-05
beta_one = 0.9
beta_two = 0.95
learn_rate = 0.01
decay_rate = 0.1
adam_eps = 1e-08
adam_count = 10.0

FSDP = "fsdp"
CTX = "ctx"
EACH = "each"
ALL = "all"
GATHER = "gather"
REDUCE = "reduce"
HALF = "half"
WEIGHTS = "weights"
BOTH = "both"
CROSS = "cross"
PAIR = "pair"
NEXT = "next"
PREV = "prev"
BACK = "back"
LINE = "line"
SEQ = "seq"
SPREAD = "spread"
HIST = "hist"
STATE = "state"
RATE = "rate"
DRATE = "drate"
RING = "ring"
LOG2E = 1.4426950408889634
LN2 = 0.6931471805599453
FAR = 1e30
bf16 = jnp.bfloat16
f32 = jnp.float32
ANY = pl.BlockSpec(memory_space=pltpu.HBM)
MIB = 1024 * 1024


def together(*values):
    return lax.optimization_barrier(values)


def ceil_to(value, unit):
    return (value + unit - 1) // unit * unit


def span_of(axis):
    return lax.axis_size(axis), lax.axis_index(axis)


def ring_spot(ci, cs):
    odd = lax.rem(ci, 2)
    return (ci // 2) * (1 - odd) + (cs - 1 - ci // 2) * odd


def ring_block(spot, cs):
    spot = lax.rem(spot + 2 * cs, cs)
    far = spot // (cs // 2)
    return 2 * spot * (1 - far) + (2 * (cs - 1 - spot) + 1) * far


def when(condition, action):
    if condition is None:
        action()
    else:
        pl.when(condition)(action)


def in_hbm(value):
    return pltpu.with_memory_space_constraint(value, pltpu.HBM)


def piece_edges(mode):
    count = mode[2] - mode[1]
    groups = 5 if count > 10 else 3
    edges = [count * k // groups for k in range(groups + 1)]
    return list(zip(edges[:-1], edges[1:]))


def chunk_shape(value, cs):
    lead, _, rows, cols = value.shape
    return (rows, cols if lead == cs else cols * lead // cs)


def chunk_ref(ref, block, part, cs):
    lead = ref.shape[0]
    if lead == cs:
        return ref.at[block, part]
    cols = ref.shape[3] * lead // cs
    columns = pl.ds(pl.multiple_of(block // lead * cols, 128), cols)
    return ref.at[lax.rem(block, lead), part, :, columns]


class Ring:
    def __init__(self, chunks, uses):
        self.chunks, self.uses = chunks, uses
        self.got, self.hop = [], 0

    def finish(self):
        cs, block = span_of(CTX)
        sums = []
        for (k, part, _), got in zip(self.uses, self.got):
            value = self.chunks[k]
            if value.shape[0] == cs:
                own = lax.dynamic_index_in_dim(value, block, 0, keepdims=False)[part]
            else:
                rows, cols = chunk_shape(value, cs)
                at = (block % value.shape[0], part, 0, block // value.shape[0] * cols)
                own = lax.dynamic_slice(value, at, (1, 1, rows, cols))[0, 0]
            sums.append(got.astype(f32) + own.astype(f32))
        return sums


class Traffic:
    def __init__(self, items, ring=None, hops=0, reach=0):
        self.items, self.ring, self.reach = items, ring, reach
        fs, cs = lax.axis_size(FSDP), lax.axis_size(CTX)
        self.hops = min(hops, cs - 1 - ring.hop) if ring is not None else 0
        self.ins = [value for value, _, _ in items]
        self.outs = []
        dma = pltpu.SemaphoreType.DMA
        most = 2 * max(fs, cs)
        count = max(len(items), 1)
        self.scratch = [dma((count, most)), dma((count, most)), dma((count, 2))]
        self.places = {}

        def own_scratch(k, shapes):
            self.places[k] = len(self.scratch)
            self.scratch += shapes

        for k, (value, mode, axis) in enumerate(items):
            shape = value.shape
            if mode in (ALL, GATHER, LINE):
                shape = (lax.axis_size(axis),) + shape
            elif mode in (NEXT, PREV):
                shape = (reach,) + shape
            elif mode == REDUCE:
                shape = (fs // 2,) + shape[1:]
                own_scratch(k, [pltpu.VMEM(shape, value.dtype)] * 2 + [dma((fs // 2,))])
            elif mode[0] == HALF:
                pieces = len(piece_edges(mode))
                shape = shape[:2] + (mode[2] - mode[1],) + shape[3:]
                own_scratch(k, [dma((pieces, 2 * fs)), dma((pieces, 2 * fs))])
            self.outs.append(jax.ShapeDtypeStruct(shape, value.dtype))
        if self.hops:
            self.ins += [in_hbm(value) for value in ring.chunks + ring.got]
            uses = len(ring.uses)
            shapes = [dma((uses, self.hops)), dma((uses, self.hops)), dma((uses, self.hops, 2))]
            for k, _, _ in ring.uses:
                shape = chunk_shape(ring.chunks[k], cs)
                self.outs += [pltpu.HBM(shape, bf16)] * self.hops
                shapes.append(pltpu.VMEM((self.hops, 2) + shape, bf16))
            own_scratch(RING, shapes)

    def vmem(self):
        total = 4 * MIB
        for held in self.scratch:
            if held.memory_space == pltpu.VMEM:
                size = 2
                for extent in held.shape[:-2]:
                    size *= extent
                total += size * ceil_to(held.shape[-2], 16) * ceil_to(held.shape[-1], 128)
        return total

    def bind(self, ins, outs, scratch):
        self.in_refs, self.out_refs, self.sems = ins, outs, scratch

    def remote(self, source, target, send, take, peer):
        return pltpu.make_async_remote_copy(
            src_ref=source,
            dst_ref=target,
            send_sem=send,
            recv_sem=take,
            device_id=peer,
            device_id_type=pl.DeviceIdType.MESH,
        )

    def greet(self):
        barrier = pltpu.get_barrier_semaphore()
        fs, fi = span_of(FSDP)
        cs, ci = span_of(CTX)

        def signal(peer):
            pl.semaphore_signal(
                barrier, inc=1, device_id=peer, device_id_type=pl.DeviceIdType.MESH
            )

        axes = {axis for _, _, axis in self.items}
        if WEIGHTS in axes:
            axes.add(FSDP)
        total = 0
        for axis in (FSDP, CTX):
            if axis in axes:
                n, me = span_of(axis)
                for d in range(1, n):
                    signal({axis: lax.rem(me + d, n)})
                total += n - 1
        if self.hops and CTX not in axes:
            spot = ring_spot(ci, cs)
            signal({CTX: ring_block(spot + 1, cs)})
            signal({CTX: ring_block(spot - 1, cs)})
            total += 2
        if WEIGHTS in axes and CTX not in axes:
            signal({CTX: ci + 1 - 2 * lax.rem(ci, 2)})
            total += 1
        if BOTH in axes:
            halves = cs // fs
            away = ci // halves != fi

            def meet():
                signal({FSDP: ci // halves, CTX: halves * fi + lax.rem(ci, halves)})

            pl.when(away)(meet)
            if total:
                pl.semaphore_wait(barrier, total + jnp.where(away, 1, 0))
            else:
                pl.when(away)(lambda: pl.semaphore_wait(barrier, 1))
        else:
            pl.semaphore_wait(barrier, total)

    def copies(self):
        starts, relays, waits = [], [], []
        fs, fi = span_of(FSDP)
        cs, ci = span_of(CTX)
        send_sem, take_sem, own_sem = self.sems[:3]
        for k, (_, mode, axis) in enumerate(self.items):
            src, dst = self.in_refs[k], self.out_refs[k]

            def add(copy, sends=None, takes=None):
                starts.append((copy.start, sends))
                waits.append((copy.wait_send, sends))
                waits.append((copy.wait_recv, takes))

            def keep(copy, condition=None):
                starts.append((copy.start, condition))
                waits.append((copy.wait, condition))

            core, chip, chips = lax.rem(fi, 2), fi // 2, fs // 2
            mate = {FSDP: fi + 1 - 2 * core}

            def relay(first, second):
                starts.append((first.start, None))
                relays.append((first.wait_recv, None))
                relays.append((second.start, None))
                waits.append((first.wait_send, None))
                waits.append((second.wait_send, None))
                waits.append((second.wait_recv, None))

            if mode == GATHER:
                for d in range(1, chips):
                    to = 2 * lax.rem(chip + d, chips) + core
                    came = 2 * lax.rem(chip + chips - d, chips) + core
                    relay(
                        self.remote(
                            src, dst.at[fi], send_sem.at[k, d], take_sem.at[k, d], {FSDP: to}
                        ),
                        self.remote(
                            dst.at[came],
                            dst.at[came],
                            send_sem.at[k, chips + d],
                            take_sem.at[k, chips + d],
                            mate,
                        ),
                    )
                add(self.remote(src, dst.at[fi], send_sem.at[k, 0], take_sem.at[k, 0], mate))
                keep(pltpu.make_async_copy(src, dst.at[fi], own_sem.at[k, 0]))
            elif mode == LINE:
                across = {CTX: ci + 1 - 2 * lax.rem(ci, 2)}
                for d in range(1, cs // 2):
                    came = lax.rem(ci + cs - 2 * d, cs)
                    relay(
                        self.remote(
                            src,
                            dst.at[ci],
                            send_sem.at[k, d],
                            take_sem.at[k, d],
                            {CTX: lax.rem(ci + 2 * d, cs)},
                        ),
                        self.remote(
                            dst.at[came],
                            dst.at[came],
                            send_sem.at[k, cs // 2 + d],
                            take_sem.at[k, cs // 2 + d],
                            across,
                        ),
                    )
                add(self.remote(src, dst.at[ci], send_sem.at[k, 0], take_sem.at[k, 0], across))
                keep(pltpu.make_async_copy(src, dst.at[ci], own_sem.at[k, 0]))
            elif mode == REDUCE:
                mine, other, load_sem = self.sems[self.places[k] : self.places[k] + 3]
                for d in list(range(1, chips)) + [0]:
                    to = lax.rem(chip + d, chips)
                    first = self.remote(
                        src.at[2 * to + 1 - core],
                        other.at[to],
                        send_sem.at[k, d],
                        take_sem.at[k, d],
                        mate,
                    )
                    load = pltpu.make_async_copy(
                        src.at[2 * to + core], mine.at[to], load_sem.at[d]
                    )
                    starts.append((first.start, None))
                    starts.append((load.start, None))
                    relays.append((load.wait, None))
                    relays.append((first.wait_recv, None))
                    waits.append((first.wait_send, None))

                    def total(mine=mine, other=other, to=to):
                        mine[to] = mine[to] + other[to]

                    relays.append((total, None))
                    if d:
                        second = self.remote(
                            mine.at[to],
                            dst.at[chip],
                            send_sem.at[k, chips + d],
                            take_sem.at[k, chips + d],
                            {FSDP: 2 * to + core},
                        )
                        waits.append((second.wait_send, None))
                        waits.append((second.wait_recv, None))
                    else:
                        second = pltpu.make_async_copy(mine.at[to], dst.at[to], own_sem.at[k, 0])
                        waits.append((second.wait, None))
                    relays.append((second.start, None))
            elif mode[0] == HALF:
                piece_send, piece_take = self.sems[self.places[k] : self.places[k] + 2]
                side = lax.rem(ci, 2)
                across = {CTX: ci + 1 - 2 * side}
                for q, (low, high) in enumerate(piece_edges(mode)):
                    for d in range(1, chips):
                        for b in range(2):
                            to = 2 * lax.rem(chip + d, chips) + lax.rem(core + b, 2)
                            came = 2 * lax.rem(chip + chips - d, chips) + lax.rem(core + b, 2)
                            e = 2 * d + b
                            relay(
                                self.remote(
                                    src.at[to, side, mode[1] + low : mode[1] + high],
                                    dst.at[fi, side, low:high],
                                    piece_send.at[q, e],
                                    piece_take.at[q, e],
                                    {FSDP: to},
                                ),
                                self.remote(
                                    dst.at[came, side, low:high],
                                    dst.at[came, side, low:high],
                                    piece_send.at[q, fs + e],
                                    piece_take.at[q, fs + e],
                                    across,
                                ),
                            )
                for b in range(2):
                    to = mate[FSDP]
                    add(
                        self.remote(
                            src.at[to, b, mode[1] : mode[2]],
                            dst.at[fi, b],
                            send_sem.at[k, b],
                            take_sem.at[k, b],
                            mate,
                        )
                    )
                    keep(
                        pltpu.make_async_copy(
                            src.at[fi, b, mode[1] : mode[2]], dst.at[fi, b], own_sem.at[k, b]
                        )
                    )
            elif mode in (ALL, EACH):
                n, me = span_of(axis)
                for d in range(1, n):
                    peer = lax.rem(me + d, n)
                    source = src.at[peer] if mode == EACH else src
                    add(
                        self.remote(
                            source, dst.at[me], send_sem.at[k, d], take_sem.at[k, d], {axis: peer}
                        )
                    )
                source = src.at[me] if mode == EACH else src
                keep(pltpu.make_async_copy(source, dst.at[me], own_sem.at[k, 0]))
            elif mode == PAIR:
                for p in range(2):
                    peer = (p * fs + fi) // 2
                    slot = lax.rem(fi, 2)
                    away = peer != fi
                    q = 2 * fi + p
                    comes = lax.rem(q, fs) != fi
                    copy = self.remote(
                        src.at[p],
                        dst.at[slot],
                        send_sem.at[k, p],
                        take_sem.at[k, slot],
                        {FSDP: peer},
                    )
                    starts.append((copy.start, away))
                    waits.append((copy.wait_send, away))
                    taken = self.remote(
                        src.at[p], dst.at[p], send_sem.at[k, p], take_sem.at[k, p], {FSDP: peer}
                    )
                    waits.append((taken.wait_recv, comes))
                    keep(
                        pltpu.make_async_copy(src.at[p], dst.at[slot], own_sem.at[k, p]),
                        peer == fi,
                    )
            elif mode == CROSS:
                halves = cs // fs
                away = ci // halves != fi
                peer = {FSDP: ci // halves, CTX: halves * fi + lax.rem(ci, halves)}
                add(self.remote(src, dst, send_sem.at[k, 0], take_sem.at[k, 0], peer), away, away)
                keep(pltpu.make_async_copy(src, dst, own_sem.at[k, 0]), ci // halves == fi)
            elif mode in (NEXT, PREV):
                reach = self.reach
                m = ci if mode == NEXT else cs - 1 - ci
                odd = lax.rem(m, 2)

                def at(spot):
                    spot = lax.rem(spot + cs, cs)
                    return {CTX: spot if mode == NEXT else cs - 1 - spot}

                def on_line(e, m=m, src=src, dst=dst, k=k, at=at):
                    source = src if e == 2 else dst.at[e - 3]
                    return self.remote(
                        source, dst.at[e - 1], send_sem.at[k, e], take_sem.at[k, e], at(m + 2)
                    )

                def to_mate(g, e, m=m, odd=odd, src=src, dst=dst, k=k, at=at, reach=reach):
                    source = src if e == 0 else dst.at[e - 1]
                    spot = reach + 1 + g
                    return self.remote(
                        source,
                        dst.at[g - 1],
                        send_sem.at[k, spot],
                        take_sem.at[k, spot],
                        at(m + 1 - 2 * odd),
                    )

                starts.append((on_line(2).start, m + 2 < cs))
                waits.append((on_line(2).wait_send, m + 2 < cs))
                starts.append((to_mate(1, 0).start, odd == 0))
                waits.append((to_mate(1, 0).wait_send, odd == 0))
                for e in range(2, reach + 1, 2):
                    here = m - e >= 0
                    relays.append((on_line(e).wait_recv, here))
                    if e + 2 <= reach:
                        goes = here & (m + 2 < cs)
                        relays.append((on_line(e + 2).start, goes))
                        waits.append((on_line(e + 2).wait_send, goes))
                    if e + 1 < reach:
                        relays.append((to_mate(e + 1, e).start, here & (odd == 0)))
                        waits.append((to_mate(e + 1, e).wait_send, here & (odd == 0)))
                    relays.append((to_mate(e - 1, e).start, here & (odd == 1)))
                    waits.append((to_mate(e - 1, e).wait_send, here & (odd == 1)))
                for g in range(1, reach, 2):
                    waits.append((to_mate(g, 0).wait_recv, m - g >= 0))
            else:
                for d in range(1, self.reach + 1):
                    add(
                        self.remote(
                            src.at[d - 1],
                            dst.at[d - 1],
                            send_sem.at[k, d],
                            take_sem.at[k, d],
                            {CTX: lax.rem(ci - d + cs, cs)},
                        ),
                        ci - d >= 0,
                        ci + d < cs,
                    )
        return starts, relays, waits

    def ring_refs(self, u):
        base = self.places[RING]
        outs = self.out_refs[len(self.items) + u * self.hops :]
        return self.sems[base], self.sems[base + 1], self.sems[base + 2], self.sems[base + 3 + u], outs

    def hop_copy(self, u, t):
        cs, ci = span_of(CTX)
        spot = ring_spot(ci, cs)
        k, part, way = self.ring.uses[u]
        send, take, _, buffer, outs = self.ring_refs(u)
        if self.ring.hop + t == 0:
            source = chunk_ref(
                self.in_refs[len(self.items) + k], ring_block(spot - way, cs), part, cs
            )
        else:
            source = buffer.at[t, 1]
        return self.remote(
            source, outs[t], send.at[u, t], take.at[u, t], {CTX: ring_block(spot + way, cs)}
        )

    def load_own(self, u, t):
        cs, ci = span_of(CTX)
        k, part, way = self.ring.uses[u]
        _, _, load, buffer, _ = self.ring_refs(u)
        block = ring_block(ring_spot(ci, cs) - way * (self.ring.hop + t + 1), cs)
        return pltpu.make_async_copy(
            chunk_ref(self.in_refs[len(self.items) + k], block, part, cs),
            buffer.at[t, 1],
            load.at[u, t, 1],
        )

    def load_got(self, u, t):
        _, _, load, buffer, outs = self.ring_refs(u)
        if t == 0:
            source = self.in_refs[len(self.items) + len(self.ring.chunks) + u]
        else:
            source = outs[t - 1]
        return pltpu.make_async_copy(source, buffer.at[t, 0], load.at[u, t, 0])

    def hop_step(self, t):
        uses = range(len(self.ring.uses))
        if self.ring.hop + t > 0:
            for u in uses:
                self.load_own(u, t).start()
                if t > 0:
                    self.hop_copy(u, t - 1).wait_recv()
                self.load_got(u, t).start()
        for u in uses:
            if self.ring.hop + t > 0:
                self.load_own(u, t).wait()
                self.load_got(u, t).wait()
                buffer = self.ring_refs(u)[3]
                buffer[t, 1] = buffer[t, 0] + buffer[t, 1]
            self.hop_copy(u, t).start()

    def begin(self):
        self.greet()
        for start, condition in self.copies()[0]:
            when(condition, start)
        if self.hops:
            self.hop_step(0)

    def end(self, hopped=1):
        _, relays, waits = self.copies()
        for step, condition in relays:
            when(condition, step)
        for t in range(hopped, self.hops):
            self.hop_step(t)
        for wait, condition in waits:
            when(condition, wait)
        for u in range(len(self.ring.uses) if self.hops else 0):
            for t in range(self.hops):
                self.hop_copy(u, t).wait_send()
            self.hop_copy(u, self.hops - 1).wait_recv()

    def take(self, results):
        count = len(self.items)
        if self.hops:
            last = count + self.hops - 1
            self.ring.got = [results[last + u * self.hops] for u in range(len(self.ring.uses))]
            self.ring.hop += self.hops
        return tuple(results[:count])


def exchange(cid, items, ring=None, hops=0, reach=0):
    plan = Traffic(items, ring, hops, reach)
    ins, outs = len(plan.ins), len(plan.outs)

    def body(*refs):
        plan.bind(refs[:ins], refs[ins : ins + outs], refs[ins + outs :])
        plan.begin()
        plan.end()

    results = pl.pallas_call(
        body,
        out_shape=tuple(plan.outs),
        in_specs=[ANY] * ins,
        out_specs=(ANY,) * outs,
        scratch_shapes=plan.scratch,
        compiler_params=pltpu.CompilerParams(
            collective_id=cid, has_side_effects=True, vmem_limit_bytes=plan.vmem() + 4 * MIB
        ),
    )(*plan.ins)
    return plan.take(results)


def scan_tail_body(rows, length, step_ref, u_ref, b_ref, rate_ref, last_ref):
    rate = rate_ref[...]

    def advance(i, states):
        new = []
        for r in range(rows):
            keep = jnp.exp2(step_ref[r, pl.ds(i, 1), :] * rate)
            new.append(keep * states[r] + u_ref[r, pl.ds(i, 1), :] * b_ref[r, i])
        return tuple(new)

    start = tuple(jnp.zeros((DS, 128), f32) for _ in range(rows))
    end = lax.fori_loop(0, length, advance, start, unroll=4)
    for r in range(rows):
        last_ref[r] = end[r]


def scan_full_body(
    rows, length, step_ref, u_ref, b_ref, c_ref, rate_ref, entry_ref, read_ref, hist_ref
):
    rate = rate_ref[...]

    def advance(i, states):
        new = []
        for r in range(rows):
            hist_ref[r, i] = states[r]
            keep = jnp.exp2(step_ref[r, pl.ds(i, 1), :] * rate)
            h = keep * states[r] + u_ref[r, pl.ds(i, 1), :] * b_ref[r, i]
            read_ref[r, pl.ds(i, 1), :] = jnp.sum(h * c_ref[r, i], axis=0, keepdims=True)
            new.append(h)
        return tuple(new)

    lax.fori_loop(0, length, advance, tuple(entry_ref[r] for r in range(rows)), unroll=4)


def adjoint_head_body(rows, length, step_ref, dy_ref, c_ref, rate_ref, first_ref):
    rate = rate_ref[...]

    def advance(k, carried):
        i = length - 1 - k
        new = []
        for r in range(rows):
            keep = jnp.exp2(step_ref[r, pl.ds(i, 1), :] * rate)
            new.append(keep * (carried[r] + dy_ref[r, pl.ds(i, 1), :] * c_ref[r, i]))
        return tuple(new)

    start = tuple(jnp.zeros((DS, 128), f32) for _ in range(rows))
    end = lax.fori_loop(0, length, advance, start, unroll=4)
    for r in range(rows):
        first_ref[r] = end[r]


def adjoint_full_body(
    rows,
    length,
    step_ref,
    u_ref,
    dy_ref,
    b_ref,
    c_ref,
    rate_ref,
    hist_ref,
    later_ref,
    du_ref,
    dexp_ref,
    db_ref,
    dc_ref,
    drate_ref,
):
    rate = rate_ref[...]

    @pl.when(pl.program_id(1) == 0)
    def _():
        db_ref[...] = jnp.zeros_like(db_ref)
        dc_ref[...] = jnp.zeros_like(dc_ref)

    def advance(k, carried):
        i = length - 1 - k
        new = []
        drate = carried[rows]
        for r in range(rows):
            step = step_ref[r, pl.ds(i, 1), :]
            u = u_ref[r, pl.ds(i, 1), :]
            dy = dy_ref[r, pl.ds(i, 1), :]
            keep = jnp.exp2(step * rate)
            b = b_ref[r, i]
            kept = keep * hist_ref[r, i]
            g = carried[r] + dy * c_ref[r, i]
            w = g * kept
            dc_ref[r, i] += (kept + u * b) * dy
            db_ref[r, i] += g * u
            du_ref[r, pl.ds(i, 1), :] = jnp.sum(g * b, axis=0, keepdims=True)
            dexp_ref[r, pl.ds(i, 1), :] = jnp.sum(w * rate, axis=0, keepdims=True)
            drate = drate + w * step
            new.append(keep * g)
        return tuple(new) + (drate,)

    start = tuple(later_ref[r] for r in range(rows)) + (jnp.zeros((DS, 128), f32),)
    end = lax.fori_loop(0, length, advance, start, unroll=2)
    drate_ref[0] = end[rows]


def hosted_call(body, grid, in_specs, out_specs, out_shape, args, cid, plan, own_vmem, later=()):
    steps = 1
    for size in grid:
        steps *= size
    n_in, n_out, x_in, x_out = len(args), len(out_shape), len(plan.ins), len(plan.outs)

    def hosted(*refs):
        mine_in, refs = refs[:n_in], refs[n_in:]
        plan_in, refs = refs[:x_in], refs[x_in:]
        mine_out, refs = refs[:n_out], refs[n_out:]
        plan.bind(plan_in, refs[:x_out], refs[x_out:])
        at = pl.program_id(0)
        for k in range(1, len(grid)):
            at = at * grid[k] + pl.program_id(k)
        pl.when(at == 0)(plan.begin)
        for t in range(1, min(plan.hops, len(later) + 1)):
            pl.when(at == later[t - 1])(functools.partial(plan.hop_step, t))
        body(*mine_in, *mine_out)
        pl.when(at == steps - 1)(functools.partial(plan.end, 1 + len(later)))

    results = pl.pallas_call(
        hosted,
        grid=grid,
        in_specs=in_specs + [ANY] * x_in,
        out_specs=tuple(out_specs) + (ANY,) * x_out,
        out_shape=tuple(out_shape) + tuple(plan.outs),
        scratch_shapes=plan.scratch,
        compiler_params=pltpu.CompilerParams(
            vmem_limit_bytes=plan.vmem() + own_vmem, collective_id=cid, has_side_effects=True
        ),
    )(*args, *plan.ins)
    return tuple(results[:n_out]) + plan.take(results[n_out:])


def scan_call(body, args, kinds, outs, rows_all, length, width, cid, plan, later=()):
    rows = 4 if rows_all % 4 == 0 else rows_all
    single = pl.Buffered(buffer_count=1)
    grid = (rows_all // rows, width // 128)

    def spec(kind):
        extra = {"pipeline_mode": single} if kind == SPREAD else {}
        if kind == SEQ:
            return pl.BlockSpec((rows, length, 128), lambda r, g: (r, 0, g), **extra)
        if kind == SPREAD:
            return pl.BlockSpec((rows, length, DS, 128), lambda r, g: (r, 0, 0, 0), **extra)
        if kind == HIST:
            return pl.BlockSpec((rows, length, DS, 128), lambda r, g: (r, 0, 0, g), **extra)
        if kind == STATE:
            return pl.BlockSpec((rows, DS, 128), lambda r, g: (r, 0, g), **extra)
        if kind == RATE:
            return pl.BlockSpec((DS, 128), lambda r, g: (0, g), **extra)
        return pl.BlockSpec((1, DS, 128), lambda r, g: (r, 0, g), **extra)

    def block_bytes(kind):
        wide = rows * length * 128 * 4
        return {SEQ: 2 * wide, SPREAD: DS * wide, HIST: 2 * DS * wide}.get(kind, MIB // 2)

    shape_of = {
        SEQ: (rows_all, length, width),
        SPREAD: (rows_all, length, DS, 128),
        HIST: (rows_all, length, DS, width),
        STATE: (rows_all, DS, width),
        DRATE: (rows_all // rows, DS, width),
    }
    return hosted_call(
        functools.partial(body, rows, length),
        grid,
        [spec(k) for k in kinds],
        [spec(k) for k in outs],
        [jax.ShapeDtypeStruct(shape_of[k], f32) for k in outs],
        args,
        cid,
        plan,
        8 * MIB + sum(block_bytes(k) for k in tuple(kinds) + tuple(outs)),
        later,
    )


def attend_body(heads, q_ref, k_ref, v_ref, bias_ref, out_ref, total_ref):
    keys = k_ref[...].T
    for h in range(heads):
        rows = slice(h * HD, (h + 1) * HD)
        scores = jnp.dot(keys, q_ref[rows], preferred_element_type=f32)
        scores = scores * HD**-0.5 + bias_ref[...]
        peak = jnp.max(scores, axis=0, keepdims=True)
        grown = jnp.exp(scores - peak)
        total = jnp.sum(grown, axis=0, keepdims=True)
        probs = (grown * (1.0 / total)).astype(bf16)
        out_ref[rows] = jnp.dot(v_ref[...], probs, preferred_element_type=f32).astype(bf16)
        total_ref[0, h : h + 1] = peak + jnp.log(total)


def attend_back_body(
    heads, q_ref, k_ref, v_ref, bias_ref, total_ref, grad_ref, dq_ref, dk_ref, dv_ref
):
    keys = k_ref[...].T
    values = v_ref[...].T
    for h in range(heads):
        rows = slice(h * HD, (h + 1) * HD)
        scores = jnp.dot(keys, q_ref[rows], preferred_element_type=f32)
        probs = jnp.exp(scores * HD**-0.5 + bias_ref[...] - total_ref[0, h : h + 1])
        grad = jnp.dot(values, grad_ref[rows], preferred_element_type=f32)
        mean = jnp.sum(probs * grad, axis=0, keepdims=True)
        low = (probs * (grad - mean)).astype(bf16)
        dq = jnp.dot(k_ref[...], low, preferred_element_type=f32)
        dq_ref[rows] = (dq * HD**-0.5).astype(bf16)
        dk = dense_nt(q_ref[rows], low) * HD**-0.5
        dv = dense_nt(grad_ref[rows], probs.astype(bf16))
        if h == 0:
            dk_ref[...] = dk
            dv_ref[...] = dv
        else:
            dk_ref[...] += dk
            dv_ref[...] += dv


def rows_matmul(values, weight, swapped=False):
    count, tokens, depth = values.shape
    if swapped:
        tokens, depth = depth, tokens
    real, width = weight.shape
    turned = real > tokens * 8
    if turned:
        weight = weight.T

    def body(value_ref, weight_ref, out_ref):
        value = value_ref[0].T if swapped else value_ref[0][:, :real]
        product = dense_nt if turned else dense
        out_ref[0] = product(value, weight_ref[...]).astype(bf16)

    return pl.pallas_call(
        body,
        grid=(count,),
        in_specs=[
            pl.BlockSpec((1,) + values.shape[1:], lambda r: (r, 0, 0)),
            pl.BlockSpec(weight.shape, lambda r: (0, 0), pipeline_mode=pl.Buffered(buffer_count=1)),
        ],
        out_specs=pl.BlockSpec((1, tokens, width), lambda r: (r, 0, 0)),
        out_shape=jax.ShapeDtypeStruct((count, tokens, width), bf16),
        compiler_params=pltpu.CompilerParams(vmem_limit_bytes=24 * MIB),
    )(values, weight)


def rms_norm(values, gain_row):
    return (
        values * lax.rsqrt(jnp.mean(values * values, axis=-1, keepdims=True) + norm_eps) * gain_row
    )


def dense(operand, partner):
    return jnp.dot(operand, partner, preferred_element_type=f32)


def dense_tn(operand, partner):
    return lax.dot_general(
        operand, partner, (((0,), (0,)), ((), ())), preferred_element_type=f32
    )


def dense_nt(operand, partner):
    return lax.dot_general(
        operand, partner, (((1,), (1,)), ((), ())), preferred_element_type=f32
    )


def conv_silu(extended, conv_taps, same_seg):
    length_out = extended.shape[1] - CONV + 1
    summed = jnp.zeros((extended.shape[0], length_out, extended.shape[2]), f32)
    for offset in range(CONV):
        summed = summed + jnp.where(
            same_seg[offset][:, :, None],
            extended[:, offset : offset + length_out] * conv_taps[offset],
            0.0,
        )
    return jax.nn.silu(summed)


def adam_step(gradient, moments_old, weight_now):
    first_moment = beta_one * moments_old[0] + (1.0 - beta_one) * gradient
    second_moment = beta_two * moments_old[1] + (1.0 - beta_two) * gradient * gradient
    corrected = (
        first_moment
        / (1.0 - beta_one**adam_count)
        / (jnp.sqrt(second_moment / (1.0 - beta_two**adam_count)) + adam_eps)
    )
    return (second_moment, -learn_rate * (corrected + decay_rate * weight_now))


def pad_last(values, width):
    return jnp.pad(values, [(0, 0)] * (values.ndim - 1) + [(0, width - values.shape[-1])])


def column_parts(weight, parts, shards_of, width):
    own = weight.shape[1] // parts // shards_of
    return jnp.stack(
        [
            jnp.concatenate(
                [
                    pad_last(weight[:, (p * shards_of + j) * own : (p * shards_of + j + 1) * own], width)
                    for p in range(parts)
                ],
                axis=1,
            )
            for j in range(shards_of)
        ]
    )


def shards(
    tokens,
    cotangent,
    segments,
    w_qkv,
    m_qkv,
    w_attn_out,
    m_attn_out,
    w_mamba_in,
    m_mamba_in,
    w_ssm_proj,
    m_ssm_proj,
    w_mamba_out,
    m_mamba_out,
    w_gate_up,
    m_gate_up,
    w_ffn_down,
    m_ffn_down,
    ssm_vec,
    m_ssm_vec,
    embed_small,
    m_embed_small,
):
    fs, cs = lax.axis_size(FSDP), lax.axis_size(CTX)
    fi, ci = lax.axis_index(FSDP), lax.axis_index(CTX)
    tok = tokens.shape[1]
    dim = tokens.shape[2]
    row_len = segments.shape[1]
    halves = cs // fs
    reach = min(row_len // 2, WINDOW) // tok
    metas = META // cs
    chan = DI // fs
    chan_p = ceil_to(chan, 128)
    ffw = FF // fs
    ffw_p = ceil_to(ffw, 128)
    heads_dim = NH * HD
    kv_dim = KVH * HD
    groups = NH // KVH
    scale_factor = HD ** (-0.5)
    xdim = DTR + 2 * DS
    both = (FSDP, CTX)

    def row_block(weight):
        rows, cols = weight.shape[0] // halves, weight.shape[1] // fs
        return lax.dynamic_slice(
            weight, ((ci % halves) * rows, (ci // halves) * cols), (rows, cols)
        )

    def unpaired(value, width):
        return jnp.concatenate([value[0][:, :width], value[1][:, :width]], axis=1).astype(f32)

    def spread_hops(weights):
        total, done, out = sum(weights), 0, []
        for k in range(len(weights)):
            upto = (cs - 1) * sum(weights[: k + 1]) // total
            out.append(upto - done)
            done = upto
        return out

    def row_chunks(operand, partner):
        grad = dense_tn(operand, partner).astype(bf16)
        return grad.reshape(cs, 1, grad.shape[0] // cs, grad.shape[1])

    def column_chunks(operand, partner, parts=1):
        cols = partner.shape[1] // fs
        wide = jnp.concatenate(
            [
                pad_last(partner[:, j * cols : (j + 1) * cols], ceil_to(cols, 128))
                for j in range(fs)
            ],
            axis=1,
        )
        grad = dense_tn(operand, wide).astype(bf16)
        return grad.reshape(halves, parts, -1, grad.shape[1])

    def by_rows(value):
        return value.astype(bf16).reshape(fs, tok, -1)

    blocks = 25

    def in_blocks(value):
        return value.reshape(fs, 2, blocks, value.shape[1] // (2 * blocks), value.shape[2])

    mi_send = column_parts(w_mamba_in, 2, fs, chan_p)
    qkv_send = column_parts(w_qkv, 1, fs, w_qkv.shape[1] // fs)
    gain_rows = embed_small[META:]
    meta_rows = lax.dynamic_slice_in_dim(embed_small, ci * metas, metas, 0)
    source = tokens[0].astype(f32)
    normed_f, norm_pull = jax.vjp(rms_norm, source, gain_rows[0])
    normed = normed_f.astype(bf16)
    meta_f, meta_pull = jax.vjp(rms_norm, meta_rows, gain_rows[0])
    meta_low = meta_f.astype(bf16)

    normed_all, seg_all, mi_w, qkv_w = exchange(
        0,
        [
            (normed, GATHER, FSDP),
            (segments, ALL, FSDP),
            (in_blocks(mi_send), (HALF, 0, blocks), WEIGHTS),
            (in_blocks(qkv_send), (HALF, 0, blocks), WEIGHTS),
        ],
    )
    gu_send = in_hbm(in_blocks(column_parts(w_gate_up, 2, fs, ffw_p)))
    mi_w = mi_w.reshape(dim, 2 * chan_p)
    qkv_w = qkv_w.reshape(dim, -1)
    seg_all = seg_all.reshape(fs, row_len)
    seg_row = segments[0]
    normed_all = normed_all.reshape(fs * tok, dim)
    xp_w = jnp.pad(w_ssm_proj[:, :xdim], ((0, chan_p - chan), (0, 0)))
    dt_w = jnp.pad(w_ssm_proj[:, xdim:], ((0, chan_p - chan), (0, 0)))
    vec = pad_last(lax.dynamic_slice_in_dim(ssm_vec, fi * chan, chan, 1), chan_p)

    normed_rows = normed_all.reshape(fs, tok, dim)
    qkv_parts = jnp.einsum("ftd,dc->fct", normed_rows, qkv_w, preferred_element_type=f32)
    meta_part = jnp.broadcast_to(
        dense(meta_low, qkv_w).astype(bf16)[None], (fs, metas, qkv_w.shape[1])
    )
    qkv_got, meta_got = exchange(
        1, [(qkv_parts.astype(bf16), EACH, FSDP), (meta_part, EACH, FSDP)]
    )
    qkv_own = qkv_got.reshape(heads_dim + 2 * kv_dim, tok)
    queries = qkv_own[:heads_dim]
    keyval = qkv_own[heads_dim:]
    meta_own = jnp.concatenate([meta_got[j] for j in range(fs)], axis=1)[:, heads_dim:]
    kv_before, meta_kv, gu_0 = exchange(
        2,
        [
            (keyval, NEXT, CTX),
            (meta_own, ALL, CTX),
            (gu_send, (HALF, 0, 5), WEIGHTS),
        ],
        reach=reach,
    )
    kv_before = jnp.where(
        (ci - 1 - jnp.arange(reach) >= 0)[:, None, None], kv_before, jnp.zeros_like(kv_before)
    )
    key_rows = jnp.concatenate(
        [meta_kv.reshape(META, 2 * kv_dim).T]
        + [kv_before[d - 1] for d in range(reach, 0, -1)]
        + [keyval],
        axis=1,
    )

    mamba_in = dense(normed_all, mi_w).reshape(fs, tok, 2 * chan_p)
    inner_pre = mamba_in[:, :, :chan_p]
    gate_z = mamba_in[:, :, chan_p:]
    up_ring = [(c, c + 1) for c in range(cs - 1)]
    down_ring = [(c + 1, c) for c in range(cs - 1)]
    tail_rows = lax.ppermute(inner_pre[:, tok - (CONV - 1) :], CTX, up_ring)
    extended = jnp.concatenate([tail_rows, inner_pre], axis=1)
    seg_ext = lax.dynamic_slice_in_dim(
        jnp.concatenate([jnp.full((fs, CONV - 1), -1, jnp.int32), seg_all], axis=1),
        ci * tok,
        tok + CONV - 1,
        1,
    )
    own_seg = seg_ext[:, CONV - 1 :]
    same_seg = [seg_ext[:, o : o + tok] == own_seg for o in range(CONV)]
    starts = own_seg != seg_ext[:, CONV - 2 : -1]
    inner_x, conv_pull = jax.vjp(
        lambda ext_rows, taps: conv_silu(ext_rows, taps, same_seg), extended, vec[:CONV]
    )
    inner_low = inner_x.astype(bf16).reshape(fs * tok, chan_p)
    xproj_part = lax.dot_general(
        xp_w, inner_low, (((0,), (1,)), ((), ())), preferred_element_type=f32
    )
    xproj_got, attn_old = exchange(
        3,
        [
            (xproj_part, GATHER, FSDP),
            (row_block(w_attn_out), CROSS, BOTH),
        ],
    )
    xproj = jnp.sum(xproj_got, axis=0).T
    delta_low = xproj[:, :DTR].astype(bf16)
    pre_delta = dense_nt(delta_low, dt_w).reshape(fs, tok, chan_p) + vec[CONV]
    step = jax.nn.softplus(pre_delta)
    step_far = jnp.where(starts[:, :, None], FAR, step)
    drive = step * inner_x

    def spread(columns):
        return jnp.broadcast_to(columns.reshape(fs, tok, DS, 1), (fs, tok, DS, 128))

    b_wide = spread(xproj[:, DTR : DTR + DS])
    c_wide = spread(xproj[:, DTR + DS : xdim])
    rate = -jnp.exp(vec[CONV + 2 :])
    rate2 = rate * LOG2E
    sizes = (fs, tok, chan_p)
    last_state, ssm_proj_old = scan_call(
        scan_tail_body,
        (step_far, drive, b_wide, rate2),
        (SEQ, SEQ, SPREAD, RATE),
        (STATE,),
        *sizes,
        cid=19,
        plan=Traffic([(row_block(w_ssm_proj), CROSS, BOTH)]),
    )
    step_sum = jnp.sum(step_far, axis=1)
    state_before, sums, gu_2 = exchange(
        4,
        [
            (last_state.astype(bf16), NEXT, CTX),
            (step_sum, ALL, CTX),
            (gu_send, (HALF, 10, 19), WEIGHTS),
        ],
        reach=reach,
    )

    def decay_of(block):
        total = lax.dynamic_index_in_dim(sums, jnp.clip(block, 0, cs - 1), 0, keepdims=False)
        return jnp.exp2(total[:, None, :] * rate2)

    entry = jnp.zeros((fs, DS, chan_p), f32)
    for d in range(reach, 0, -1):
        there = jnp.where(ci >= d, state_before[d - 1].astype(f32), 0.0)
        entry = decay_of(ci - d) * entry + there
    readout, hist, mamba_out_old, cot_all = scan_call(
        scan_full_body,
        (step_far, drive, b_wide, c_wide, rate2, entry),
        (SEQ, SEQ, SPREAD, SPREAD, RATE, STATE),
        (SEQ, HIST),
        *sizes,
        cid=20,
        plan=Traffic([(row_block(w_mamba_out), CROSS, BOTH), (cotangent[0], GATHER, FSDP)]),
    )
    skip = vec[CONV + 1]
    pre_mix = readout + skip * inner_x
    gate_s = jax.nn.sigmoid(gate_z)
    gate_silu = gate_z * gate_s
    mixture_low = (pre_mix * gate_silu).astype(bf16).reshape(fs * tok, chan_p)
    ssm_part = rows_matmul(mixture_low.reshape(fs, tok, chan_p), w_mamba_out)

    key_span = (reach + 1) * tok
    padded_seg = jnp.concatenate([jnp.full((reach * tok,), -1, jnp.int32), seg_row])
    key_seg = lax.dynamic_slice_in_dim(padded_seg, ci * tok, key_span, 0)
    query_seg = lax.dynamic_slice_in_dim(seg_row, ci * tok, tok, 0)
    query_pos = jnp.arange(tok, dtype=jnp.int32) + reach * tok
    key_pos = jnp.arange(key_span, dtype=jnp.int32)
    allowed = (
        (key_seg[:, None] == query_seg[None, :])
        & (key_pos[:, None] <= query_pos[None, :])
        & (query_pos[None, :] - key_pos[:, None] < WINDOW)
    )
    allowed = jnp.concatenate([jnp.ones((META, tok), jnp.bool_), allowed], axis=0)
    bias = jnp.where(allowed, 0.0, -1e30)
    seen = META + key_span
    q_spec = pl.BlockSpec((groups * HD, tok), lambda g: (g, 0))
    k_spec = pl.BlockSpec((HD, seen), lambda g: (g, 0))
    v_spec = pl.BlockSpec((HD, seen), lambda g: (g + KVH, 0))
    bias_spec = pl.BlockSpec((seen, tok), lambda g: (0, 0))
    total_spec = pl.BlockSpec((1, groups, tok), lambda g: (g, 0, 0))
    attended, log_totals, gu_1, ffn_down_old = hosted_call(
        functools.partial(attend_body, groups),
        (KVH,),
        [q_spec, k_spec, v_spec, bias_spec],
        [q_spec, total_spec],
        [
            jax.ShapeDtypeStruct((heads_dim, tok), bf16),
            jax.ShapeDtypeStruct((KVH, groups, tok), f32),
        ],
        (queries, key_rows, key_rows, bias),
        16,
        Traffic([(gu_send, (HALF, 5, 10), WEIGHTS), (row_block(w_ffn_down), CROSS, BOTH)]),
        12 * MIB,
    )
    wide = heads_dim // fs
    att_got, gu_3 = exchange(
        5,
        [
            (attended.reshape(fs, wide, tok), EACH, FSDP),
            (gu_send, (HALF, 19, 25), WEIGHTS),
        ],
    )
    gu_w = jnp.concatenate([gu_0, gu_1, gu_2, gu_3], axis=2).reshape(dim, 2 * ffw_p)
    att_tp = jnp.swapaxes(att_got, 1, 2).reshape(fs * tok, wide)
    attn_part = rows_matmul(att_got, w_attn_out, True)
    attn_got, ssm_got = exchange(
        6, [(attn_part, REDUCE, FSDP), (ssm_part, REDUCE, FSDP)]
    )
    attn_proj = jnp.sum(attn_got.astype(f32), axis=0)
    ssm_proj = jnp.sum(ssm_got.astype(f32), axis=0)
    attn_branch, attn_pull = jax.vjp(rms_norm, attn_proj, gain_rows[1])
    ssm_branch, ssm_norm_pull = jax.vjp(rms_norm, ssm_proj, gain_rows[2])
    residual = source + 0.5 * (attn_branch + ssm_branch)
    ffn_in_f, ffn_norm_pull = jax.vjp(rms_norm, residual, gain_rows[3])
    (ffn_in,) = exchange(7, [(ffn_in_f.astype(bf16), GATHER, FSDP)])
    cot_all = cot_all.reshape(fs * tok, dim)
    ffn_in = ffn_in.reshape(fs * tok, dim)

    gate_up = dense(ffn_in, gu_w)
    hidden_f, glu_pull = jax.vjp(
        lambda values: jax.nn.silu(values[:, :ffw_p]) * values[:, ffw_p:], gate_up
    )
    hidden_wide = hidden_f.astype(bf16)
    hidden = hidden_wide[:, :ffw]
    down_part = rows_matmul(hidden_wide.reshape(fs, tok, ffw_p), w_ffn_down)
    hidden_grad = pad_last(dense_nt(cot_all, w_ffn_down), ffw_p)
    gate_up_grad = glu_pull(hidden_grad)[0].astype(bf16)
    ring_one = Ring(
        [
            row_chunks(ffn_in, gate_up_grad[:, :ffw_p]),
            row_chunks(ffn_in, gate_up_grad[:, ffw_p:]),
            column_chunks(hidden, cot_all, 2),
        ],
        [(0, 0, 1), (1, 0, -1), (2, 0, 1), (2, 1, -1)],
    )
    hops = spread_hops([1, 1, 1, 1, 2, 1])
    ffn_back = by_rows(dense_nt(gate_up_grad, gu_w))
    (back_got,) = exchange(8, [(ffn_back, REDUCE, FSDP)], ring_one, hops[0])
    resid_part, gain_ffn_grad = ffn_norm_pull(jnp.sum(back_got.astype(f32), axis=0))
    residual_grad = cotangent[0].astype(f32) + resid_part
    branch_grad = 0.5 * residual_grad
    attn_proj_grad, gain_attn_grad = attn_pull(branch_grad)
    ssm_proj_grad, gain_ssm_grad = ssm_norm_pull(branch_grad)
    branch_low = (attn_proj_grad.astype(bf16), ssm_proj_grad.astype(bf16))
    attn_proj_low, ssm_proj_low = exchange(
        9,
        [(branch_low[0], GATHER, FSDP), (branch_low[1], GATHER, FSDP)],
        ring_one,
        hops[1],
    )
    attn_proj_low = attn_proj_low.reshape(fs * tok, dim)
    ssm_proj_low = ssm_proj_low.reshape(fs * tok, dim)
    att_grad_tp = jnp.einsum(
        "ftd,cd->fct",
        attn_proj_low.reshape(fs, tok, dim),
        w_attn_out,
        preferred_element_type=f32,
    ).astype(bf16)
    (att_grad_got,) = exchange(10, [(att_grad_tp, EACH, FSDP)], ring_one, hops[2])

    def own_pair(held, part):
        piece = lax.dynamic_slice_in_dim(held, ci * (dim // cs), dim // cs, 0)
        return jnp.stack([piece[:, :part], piece[:, part:]])

    qkv_old = lax.dynamic_slice_in_dim(qkv_w, ci * (dim // cs), dim // cs, 0)
    attended_grad = att_grad_got.reshape(heads_dim, tok)

    query_grad, key_grad, value_grad, mamba_in_old = hosted_call(
        functools.partial(attend_back_body, groups),
        (KVH,),
        [q_spec, k_spec, v_spec, bias_spec, total_spec, q_spec],
        [q_spec, k_spec, k_spec],
        [
            jax.ShapeDtypeStruct((heads_dim, tok), bf16),
            jax.ShapeDtypeStruct((kv_dim, seen), f32),
            jax.ShapeDtypeStruct((kv_dim, seen), f32),
        ],
        (queries, key_rows, key_rows, bias, log_totals, attended_grad),
        24,
        Traffic([(own_pair(mi_w, chan_p), PAIR, FSDP)], ring_one, hops[3]),
        16 * MIB,
    )
    kv_grad_all = jnp.concatenate([key_grad, value_grad], axis=0)
    kv_send = jnp.stack(
        [
            kv_grad_all[:, META + (reach - d) * tok : META + (reach - d + 1) * tok]
            for d in range(1, reach + 1)
        ]
    ).astype(bf16)
    meta_send = kv_grad_all[:, :META].T.astype(bf16).reshape(cs, metas, 2 * kv_dim)
    kv_back, meta_back, down_got = exchange(
        13,
        [
            (kv_send, BACK, CTX),
            (meta_send, EACH, CTX),
            (down_part, REDUCE, FSDP),
        ],
        ring_one,
        hops[4],
        reach,
    )
    output = residual + jnp.sum(down_got.astype(f32), axis=0)
    own_kv_grad = kv_grad_all[:, META + reach * tok :]
    for d in range(1, reach + 1):
        own_kv_grad = own_kv_grad + jnp.where(ci + d < cs, kv_back[d - 1].astype(f32), 0.0)
    meta_kv_grad = jnp.sum(meta_back.astype(f32), axis=0).astype(bf16)
    meta_grad_parts = column_parts(
        jnp.pad(meta_kv_grad, ((0, 0), (heads_dim, 0))), 1, fs, qkv_w.shape[1]
    )
    qkv_grad = jnp.concatenate([query_grad, own_kv_grad.astype(bf16)], axis=0)
    qkv_grad_tp, meta_grad_tp = exchange(
        14,
        [
            (qkv_grad.reshape(fs, -1, tok), EACH, FSDP),
            (meta_grad_parts, EACH, FSDP),
        ],
        ring_one,
        hops[5],
    )

    mixture_grad = pad_last(dense_nt(ssm_proj_low, w_mamba_out), chan_p).reshape(fs, tok, chan_p)
    read_grad = mixture_grad * gate_silu
    gate_grad = mixture_grad * pre_mix * (gate_s * (1.0 + gate_z * (1.0 - gate_s)))
    gate_low = gate_grad.astype(bf16).reshape(fs * tok, chan_p)
    qkv_full = jnp.einsum("ftd,fct->dc", normed_rows, qkv_grad_tp, preferred_element_type=f32)
    qkv_full = qkv_full + jnp.einsum(
        "md,fmc->dc", meta_low, meta_grad_tp, preferred_element_type=f32
    )
    ring_two = Ring(
        [
            row_chunks(normed_all, gate_low),
            qkv_full.astype(bf16).reshape(cs, 1, dim // cs, qkv_w.shape[1]),
            column_chunks(att_tp, attn_proj_low),
            column_chunks(mixture_low[:, :chan], ssm_proj_low),
        ],
        [(0, 0, 1), (1, 0, 1), (2, 0, -1), (3, 0, -1)],
    )
    hops = spread_hops([1, 2, 2, 2])
    gate_sum, up_sum, down_top, down_low = ring_one.finish()
    first_adj, gate_up_old = scan_call(
        adjoint_head_body,
        (step_far, read_grad, c_wide, rate2),
        (SEQ, SEQ, SPREAD, RATE),
        (STATE,),
        *sizes,
        cid=21,
        plan=Traffic([(own_pair(gu_w, ffw_p), PAIR, FSDP)], ring_two, hops[0]),
    )
    adj_after, gate_up_sum = exchange(
        11,
        [
            (first_adj.astype(bf16), PREV, CTX),
            (jnp.stack([gate_sum, up_sum]).astype(bf16), PAIR, FSDP),
        ],
        ring_two,
        hops[1],
        reach,
    )
    gate_up_old = unpaired(gate_up_old, ffw)
    mamba_in_old = unpaired(mamba_in_old, chan)
    later = jnp.zeros((fs, DS, chan_p), f32)
    for d in range(reach, 0, -1):
        there = jnp.where(ci + d < cs, adj_after[d - 1].astype(f32), 0.0)
        later = decay_of(ci + d) * later + there
    drive_grad, exp_grad, b_acc, c_acc, rate_grad = scan_call(
        adjoint_full_body,
        (step_far, drive, read_grad, b_wide, c_wide, rate2, hist, later),
        (SEQ, SEQ, SEQ, SPREAD, SPREAD, RATE, HIST, STATE),
        (SEQ, SEQ, SPREAD, SPREAD, DRATE),
        *sizes,
        cid=22,
        plan=Traffic([], ring_two, hops[2]),
        later=(4,) if hops[2] == 2 else (),
    )
    cross = [
        (f * cs + c, (c // halves) * cs + halves * f + c % halves)
        for f in range(fs)
        for c in range(cs)
    ]
    down_both = jnp.concatenate([down_top, down_low], axis=0).astype(bf16)
    drive_grad, down_both = together(drive_grad, down_both)
    down_sum = lax.ppermute(down_both, (FSDP, CTX), cross)
    step_grad = drive_grad * inner_x + exp_grad * LN2
    pre_delta_grad = step_grad * jax.nn.sigmoid(pre_delta)
    inner_grad = drive_grad * step + skip * read_grad
    small_grad = jnp.concatenate(
        [
            jnp.sum(pre_delta_grad, axis=(0, 1))[None],
            jnp.sum(inner_x * read_grad, axis=(0, 1))[None],
            jnp.sum(rate_grad, axis=0) * rate,
        ],
        axis=0,
    )
    pre_delta_low = pre_delta_grad.astype(bf16).reshape(fs * tok, chan_p)
    xgrad_part = jnp.concatenate(
        [
            lax.dot_general(
                dt_w, pre_delta_low, (((0,), (1,)), ((), ())), preferred_element_type=f32
            ),
            jnp.sum(b_acc, axis=-1).reshape(fs * tok, DS).T,
            jnp.sum(c_acc, axis=-1).reshape(fs * tok, DS).T,
        ],
        axis=0,
    )
    (xgrad_got,) = exchange(12, [(xgrad_part, GATHER, FSDP)], ring_two, hops[3])
    xproj_grad = jnp.sum(xgrad_got, axis=0).T.astype(bf16)
    inner_grad = inner_grad + dense_nt(xproj_grad, xp_w).reshape(fs, tok, chan_p)
    ext_grad, taps_grad = conv_pull(inner_grad)
    returned = lax.ppermute(ext_grad[:, : CONV - 1].astype(bf16), CTX, down_ring).astype(f32)
    inner_pre_grad = ext_grad[:, CONV - 1 :] + jnp.pad(
        returned, ((0, 0), (tok - (CONV - 1), 0), (0, 0))
    )
    inner_pre_low = inner_pre_grad.astype(bf16).reshape(fs * tok, chan_p)
    mamba_in_grad = jnp.concatenate([inner_pre_low, gate_low], axis=1)
    split = ceil_to(chan_p * 9 // 16, 128)
    ring_three = Ring(
        [
            row_chunks(normed_all, inner_pre_low[:, :split]),
            row_chunks(normed_all, inner_pre_low[:, split:]),
            column_chunks(
                jnp.concatenate([inner_low[:, :chan], pre_delta_low[:, :chan]], axis=0),
                jnp.concatenate(
                    [
                        jnp.pad(xproj_grad, ((0, 0), (0, DTR))),
                        jnp.pad(delta_low, ((0, 0), (xdim, 0))),
                    ],
                    axis=0,
                ),
            ),
        ],
        [(0, 0, 1), (1, 0, -1), (2, 0, -1)],
    )
    vec_grad = jnp.concatenate([taps_grad, small_grad], axis=0)
    token_back = jnp.einsum("fct,dc->ftd", qkv_grad_tp, qkv_w, preferred_element_type=f32)
    token_back = token_back + dense_nt(mamba_in_grad, mi_w).reshape(fs, tok, dim)
    meta_back_rows = jnp.einsum("fmc,dc->fmd", meta_grad_tp, qkv_w, preferred_element_type=f32)
    token_back = by_rows(token_back)
    hops = spread_hops([3, 2, 2])
    token_got, meta_rows_got = exchange(
        15,
        [(token_back, REDUCE, FSDP), (meta_back_rows.astype(bf16), REDUCE, FSDP)],
        ring_three,
        hops[0],
    )
    source_part, gain_in_grad = norm_pull(jnp.sum(token_got.astype(f32), axis=0))
    source_grad = residual_grad + source_part
    meta_grad, gain_in_meta = meta_pull(jnp.sum(meta_rows_got.astype(f32), axis=0))
    embed_part = jnp.concatenate(
        [
            meta_grad,
            jnp.stack([gain_in_grad + gain_in_meta, gain_attn_grad, gain_ssm_grad, gain_ffn_grad]),
        ],
        axis=0,
    )
    (embed_rows,) = exchange(17, [(embed_part, GATHER, FSDP)], ring_three, hops[1])
    embed_got, vec_got = exchange(
        18,
        [
            (jnp.sum(embed_rows, axis=0).astype(bf16), LINE, CTX),
            (vec_grad.astype(bf16), LINE, CTX),
        ],
        ring_three,
        hops[2],
    )
    embed_got = embed_got.astype(f32)
    vec_part = jnp.sum(vec_got.astype(f32), axis=0)
    embed_total = jnp.concatenate(
        [embed_got[:, :metas].reshape(META, dim), jnp.sum(embed_got[:, metas:], axis=0)], axis=0
    )
    gate_half, qkv_gradient, attn_sum, mamba_out_sum = ring_two.finish()
    inner_a, inner_b, proj_sum = ring_three.finish()
    mamba_in_sum, attn_sum, mamba_out_sum, proj_sum, vec_all = exchange(
        23,
        [
            (
                jnp.stack([jnp.concatenate([inner_a, inner_b], axis=1), gate_half]).astype(bf16),
                PAIR,
                FSDP,
            ),
            (attn_sum.astype(bf16), CROSS, BOTH),
            (mamba_out_sum.astype(bf16), CROSS, BOTH),
            (proj_sum.astype(bf16), CROSS, BOTH),
            (vec_part, GATHER, FSDP),
        ],
    )
    ssm_total = jnp.concatenate([vec_all[j, :, :chan] for j in range(fs)], axis=1)
    gate_up_gradient = unpaired(gate_up_sum, ffw)
    mamba_in_gradient = unpaired(mamba_in_sum, chan)
    down_turned, old_turned = together(down_sum[:, : dim // fs].T, ffn_down_old.T)
    ffn_down_gradient = down_turned.astype(f32)
    attn_gradient = attn_sum[:, : dim // fs].astype(f32)
    mamba_out_gradient = mamba_out_sum[:, : dim // fs].astype(f32)
    ssm_proj_gradient = proj_sum[:, : w_ssm_proj.shape[1] // fs].astype(f32)

    def adam_block(gradient, moments_old, weight):
        return adam_step(gradient, moments_old, weight.astype(f32))

    qkv_moments, qkv_update = adam_block(qkv_gradient, m_qkv, qkv_old)
    attn_moments, attn_update = adam_block(attn_gradient, m_attn_out, attn_old)
    mamba_in_moments, mamba_in_update = adam_block(mamba_in_gradient, m_mamba_in, mamba_in_old)
    ssm_proj_moments, ssm_proj_update = adam_block(ssm_proj_gradient, m_ssm_proj, ssm_proj_old)
    mamba_out_moments, mamba_out_update = adam_block(
        mamba_out_gradient, m_mamba_out, mamba_out_old
    )
    gate_up_moments, gate_up_update = adam_block(gate_up_gradient, m_gate_up, gate_up_old)
    ffn_down_moments, ffn_down_update = adam_block(
        ffn_down_gradient, jnp.swapaxes(m_ffn_down, 1, 2), old_turned
    )
    ffn_down_gradient, ffn_down_moments, ffn_down_update = (
        ffn_down_gradient.T,
        ffn_down_moments.T,
        ffn_down_update.T,
    )
    ssm_vec_moments, ssm_vec_update = adam_step(ssm_total, m_ssm_vec, ssm_vec)
    embed_moments, embed_update = adam_step(embed_total, m_embed_small, embed_small)
    return (
        output.astype(jnp.bfloat16)[None],
        source_grad[None],
        qkv_gradient,
        qkv_moments,
        qkv_update,
        attn_gradient,
        attn_moments,
        attn_update,
        mamba_in_gradient,
        mamba_in_moments,
        mamba_in_update,
        ssm_proj_gradient,
        ssm_proj_moments,
        ssm_proj_update,
        mamba_out_gradient,
        mamba_out_moments,
        mamba_out_update,
        gate_up_gradient,
        gate_up_moments,
        gate_up_update,
        ffn_down_gradient,
        ffn_down_moments,
        ffn_down_update,
        ssm_total,
        ssm_vec_moments,
        ssm_vec_update,
        embed_total,
        embed_moments,
        embed_update,
    )


def solution(mesh):
    in_specs = (
        P(FSDP, CTX, None),
        P(FSDP, CTX, None),
        P(FSDP, None),
        P(FSDP, None),
        P(None, CTX, FSDP),
        P(FSDP, None),
        P(None, CTX, FSDP),
        P(FSDP, None),
        P(None, CTX, FSDP),
        P(FSDP, None),
        P(None, CTX, FSDP),
        P(FSDP, None),
        P(None, CTX, FSDP),
        P(FSDP, None),
        P(None, CTX, FSDP),
        P(FSDP, None),
        P(None, CTX, FSDP),
        P(),
        P(),
        P(),
        P(),
    )
    out_specs = (
        P(FSDP, CTX, None),
        P(FSDP, CTX, None),
        P(CTX, FSDP),
        P(CTX, FSDP),
        P(CTX, FSDP),
        P(CTX, FSDP),
        P(CTX, FSDP),
        P(CTX, FSDP),
        P(CTX, FSDP),
        P(CTX, FSDP),
        P(CTX, FSDP),
        P(CTX, FSDP),
        P(CTX, FSDP),
        P(CTX, FSDP),
        P(CTX, FSDP),
        P(CTX, FSDP),
        P(CTX, FSDP),
        P(CTX, FSDP),
        P(CTX, FSDP),
        P(CTX, FSDP),
        P(CTX, FSDP),
        P(CTX, FSDP),
        P(CTX, FSDP),
        P(),
        P(),
        P(),
        P(),
        P(),
        P(),
    )
    return jax.shard_map(shards, mesh=mesh, in_specs=in_specs, out_specs=out_specs, check_vma=False)
```
